128 devices in a mesh: space: 32 (over x, z_lo, y), member: 4 (over z_hi, core).
Axes of the slice: x: 4, y: 4, z: 4 (z_hi: 2, z_lo: 2; z = z_hi * 2 + z_lo), core: 2. Of those that a mesh axis runs over, the one named last changes fastest.
Arguments:
- latent: bfloat16 [8, 768, 4096], P('member', None, 'space'), may hold values from -6 to 6
- send_rows: int32 [2, 512], P(None, 'space'), may hold values from 0 to 127, as said below
- neighbours: int32 [8, 4096], P(None, 'space'), may hold values from 0 to 159, as said below
- degree: int32 [4096], P('space'), may hold values from 4 to 8
- dec_nodes: int32 [3, 32768], P(None, 'space'), may hold values from 0 to 127, as said below
- counts: int32 [32], replicated, may hold values from 512 to 1024, as said below
- targets: float32 [83, 32768], P(None, 'space')
- member_noise: float32 [8, 32], P('member'), may hold values from -5 to 5
- w_qkv: bfloat16 [768, 2304], replicated, may hold values from -0.21875 to 0.21875
- w_out: bfloat16 [768, 768], replicated, may hold values from -0.21875 to 0.21875
- w_noise: float32 [32, 768], replicated, may hold values from -0.5 to 0.5
- decoder_hidden_weight: bfloat16 [768, 768], replicated, may hold values from -0.21875 to 0.21875
- decoder_output_weight: bfloat16 [83, 768], replicated, may hold values from -0.21875 to 0.21875
Outputs:
- mean_fair_crps: float32 [], replicated
- d_latent: float32 [8, 768, 4096], P('member', None, 'space')
- grad_qkv: float32 [768, 2304], replicated
- grad_out: float32 [768, 768], replicated
- grad_noise: float32 [32, 768], replicated
- grad_dec1: float32 [768, 768], replicated
- grad_dec2: float32 [83, 768], replicated
The draws below stay inside these ranges and needn't reach their ends.
Inputs may be any that keep to these rules, and one draw needn't show every extreme that they name: `neighbours`: entries index a shard's extended rows; slot 0 is the node itself, every entry lies within 16 rows of it. The first degree slots of a node are live. `send_rows`: local node indices; within each row of a shard distinct. `dec_nodes`: local node indices of the shard that holds the grid point; for the point at place p of its shard each entry lies from p * 128 // 1024 to 3 more. `counts`: the live points of a shard are its first ones.
All inputs are finite; a program needn't handle non-finite values.
Results may differ from the reference program's by a relative error of at most 0.024.
Values may be sent and summed in bfloat16 or wider, within the bound.
No kernel may reach another device: no remote copies, remote signals or barrier semaphores. Data moves between devices by JAX's collectives and lax.ppermute only.
A program may use at most 128 MiB of HBM per device.

```python
import jax
import jax.numpy as jnp
from jax import lax

H = 768
HEADS = 6
OUTPUT_CHANNELS = 83
NOISE = 32
SLOTS = 8
MEMBERS_PER_SLOT = 2
NODE_DEV = 128
SHARD_GRID_SIZE = 1024
RIM = 16
ENSEMBLE_SIZE = 8
NODES = 4096
GRID = 32768
N_SPACE = 32
N_MEMBER = 4


def draw_neighbours(key, part):
    key = jax.random.fold_in(key, 11)
    position = jnp.arange(NODES, dtype=jnp.int32)
    local_node = position % NODE_DEV
    offsets = jax.random.randint(key, (SLOTS, NODES), -RIM, RIM + 1, dtype=jnp.int32)
    entries = RIM + local_node[None, :] + offsets
    slot_row = jnp.arange(SLOTS, dtype=jnp.int32)[:, None]
    entries = jnp.where(slot_row == 0, RIM + local_node[None, :], entries)
    entries = jnp.where((slot_row == 1) & (local_node[None, :] == 0), 0, entries)
    entries = jnp.where((slot_row == 1) & (local_node[None, :] == NODE_DEV - 1), NODE_DEV + 2 * RIM - 1, entries)
    return entries.astype(jnp.int32)


def draw_send_rows(key, part):
    key = jax.random.fold_in(key, 12)
    choose_bits = jax.random.randint(key, (2, N_SPACE, RIM), 0, 2, dtype=jnp.int32)
    choose_bits = choose_bits.at[:, :, 0].set(0)
    step_index = jnp.arange(RIM, dtype=jnp.int32)[None, :]
    upper_rows = NODE_DEV - 1 - 2 * step_index - choose_bits[0]
    lower_rows = 2 * step_index + choose_bits[1]
    return jnp.stack([upper_rows, lower_rows]).reshape(2, N_SPACE * RIM).astype(jnp.int32)


def draw_dec_nodes(key, part):
    key = jax.random.fold_in(key, 13)
    position = jnp.arange(GRID, dtype=jnp.int32) % SHARD_GRID_SIZE
    base_node = position * NODE_DEV // SHARD_GRID_SIZE
    offsets = jax.random.randint(key, (3, GRID), 0, 4, dtype=jnp.int32)
    offsets = offsets.at[0].set(0)
    return jnp.minimum(base_node[None, :] + offsets, NODE_DEV - 1).astype(jnp.int32)


def draw_counts(key, part):
    key = jax.random.fold_in(key, 14)
    first_key, second_key, third_key = jax.random.split(key, 3)
    drawn = jax.random.randint(first_key, (N_SPACE,), SHARD_GRID_SIZE // 2, SHARD_GRID_SIZE + 1, dtype=jnp.int32)
    fullest = jax.random.randint(second_key, (), 0, N_SPACE, dtype=jnp.int32)
    emptiest = (fullest + 1 + jax.random.randint(third_key, (), 0, N_SPACE - 1, dtype=jnp.int32)) % N_SPACE
    shard_index = jnp.arange(N_SPACE, dtype=jnp.int32)
    drawn = jnp.where(shard_index == fullest, SHARD_GRID_SIZE, drawn)
    drawn = jnp.where(shard_index == emptiest, SHARD_GRID_SIZE // 2, drawn)
    return drawn.astype(jnp.int32)


def draw_targets(key, part):
    key = jax.random.fold_in(key, 15)
    first_key = jax.random.fold_in(key, 0)
    position = jnp.arange(GRID, dtype=jnp.float32)
    ramp = 1.0 + 2.0 * position / (GRID - 1)
    values = jax.random.normal(first_key, (OUTPUT_CHANNELS, GRID), jnp.float32)
    return (values * ramp[None, :]).astype(jnp.float32)


def touch_ends(values, rng, smallest, high):
    spot = [jax.random.randint(jax.random.fold_in(rng, axis), (), 0, length) for axis, length in enumerate(values.shape)]
    main_axis = values.shape.index(max(values.shape))
    neighbour = spot[:main_axis] + [(spot[main_axis] + 1) % values.shape[main_axis]] + spot[main_axis + 1:]
    return values.at[tuple(spot)].set(smallest).at[tuple(neighbour)].set(high)


def levels(key, dims, cuts, smallest, high):
    def one(dim, blocks):
        draws = jax.random.uniform(jax.random.fold_in(jax.random.fold_in(key, 6), dim), (blocks,), jnp.float32, smallest / len(cuts), high / len(cuts))
        return jnp.repeat(jnp.exp(draws), dims[dim] // blocks).reshape((-1,) + (1,) * (len(dims) - dim - 1))

    gain = one(*cuts[0])
    for cut in cuts[1:]:
        gain = gain * one(*cut)
    return gain


def scatter_about(key, extent, scale, most, shards=(), kind=jnp.bfloat16):
    level = levels(key, extent, shards, -0.22, 0.18) if shards else 1.0
    result = jax.random.normal(key, extent, jnp.float32) * scale * level
    return jnp.minimum(jnp.maximum(result, -most), most).astype(kind)


def setup_inputs(seed: int = 0) -> dict:
    seeds = jax.random.split(jax.random.key(seed), 14)
    return {
        "latent": scatter_about(seeds[0], (ENSEMBLE_SIZE, H, NODES), 1.0, 6.0, ((0, 4), (2, 32))),
        "send_rows": draw_send_rows(jax.random.fold_in(seeds[13], 71), 0),
        "neighbours": draw_neighbours(jax.random.fold_in(seeds[13], 71), 0),
        "degree": touch_ends(jax.random.randint(seeds[3], (NODES,), 4, SLOTS + 1), jax.random.fold_in(seeds[3], 1), 4, SLOTS).astype(jnp.int32),
        "dec_nodes": draw_dec_nodes(jax.random.fold_in(seeds[13], 71), 0),
        "counts": draw_counts(jax.random.fold_in(seeds[13], 71), 0),
        "targets": draw_targets(jax.random.fold_in(seeds[13], 71), 0),
        "member_noise": scatter_about(seeds[7], (ENSEMBLE_SIZE, NOISE), 1.0, 5.0, ((0, 4),), jnp.float32),
        "w_qkv": scatter_about(seeds[8], (H, 3 * H), H ** -0.5, 0.21875),
        "w_out": scatter_about(seeds[9], (H, H), H ** -0.5, 0.21875),
        "w_noise": scatter_about(seeds[10], (NOISE, H), (4 * NOISE) ** -0.5, 0.5, (), jnp.float32),
        "decoder_hidden_weight": scatter_about(seeds[11], (H, H), H ** -0.5, 0.21875),
        "decoder_output_weight": scatter_about(seeds[12], (OUTPUT_CHANNELS, H), H ** -0.5, 0.21875),
    }


def smooth_abs(values):
    return jnp.sqrt(values * values + 0.25) - 0.5

def processor(extended, w_qkv, w_out, w_noise, member_noise, neighbours, degree):
    members = extended.shape[0]
    latent_width = extended.shape[1]
    nodes_here = neighbours.shape[1]
    slot_count = neighbours.shape[0]
    rim_width = (extended.shape[2] - nodes_here) // 2
    head_size = latent_width // HEADS
    norm_gain = 1.0 + jnp.dot(member_noise, w_noise, precision=lax.Precision.HIGHEST)
    centre = extended - lax.optimization_barrier(jnp.mean(extended, axis=1, keepdims=True))
    spread = lax.optimization_barrier(jnp.mean(centre * centre, axis=1, keepdims=True))
    normed = (centre * lax.rsqrt(spread + 1e-05) * norm_gain[:, :, None]).astype(jnp.bfloat16)
    projected = jnp.einsum('hc,mhe->mce', w_qkv.astype(jnp.float32), normed.astype(jnp.float32)).astype(jnp.bfloat16)
    queries = projected[:, :latent_width, rim_width:rim_width + nodes_here]
    gathered = jnp.take(projected[:, latent_width:], neighbours, axis=2)
    query_heads = queries.reshape(members, HEADS, head_size, nodes_here).astype(jnp.float32)
    key_heads = gathered[:, :latent_width].reshape(members, HEADS, head_size, slot_count, nodes_here).astype(jnp.float32)
    value_heads = gathered[:, latent_width:].reshape(members, HEADS, head_size, slot_count, nodes_here).astype(jnp.float32)
    scores = jnp.einsum('mhdn,mhdjn->mhjn', query_heads, key_heads) * head_size ** (-0.5)
    allowed = (jnp.arange(slot_count)[:, None] < degree[None, :]).astype(jnp.float32)
    weights = (jax.nn.sigmoid(scores) * allowed / degree.astype(jnp.float32)).astype(jnp.bfloat16)
    attended = jnp.einsum('mhjn,mhdjn->mhdn', weights.astype(jnp.float32), value_heads)
    attended = attended.reshape(members, latent_width, nodes_here).astype(jnp.bfloat16)
    branch = jnp.einsum('hc,mhn->mcn', w_out.astype(jnp.float32), attended.astype(jnp.float32))
    return extended[:, :, rim_width:rim_width + nodes_here] + branch

def decoder(refreshed_latent, decoder_hidden_weight, decoder_output_weight, dec_nodes):
    stored = refreshed_latent.astype(jnp.bfloat16)
    interp = jnp.take(stored, dec_nodes[0], axis=2).astype(jnp.float32)
    interp = interp + jnp.take(stored, dec_nodes[1], axis=2).astype(jnp.float32)
    interp = interp + jnp.take(stored, dec_nodes[2], axis=2).astype(jnp.float32)
    interp = (interp / 3.0).astype(jnp.bfloat16)
    hidden = jax.nn.silu(jnp.einsum('hc,mhg->mcg', decoder_hidden_weight.astype(jnp.float32), interp.astype(jnp.float32))).astype(jnp.bfloat16)
    return jnp.einsum('ch,mhg->mcg', decoder_output_weight.astype(jnp.float32), hidden.astype(jnp.float32))

def pointwise_crps(prediction, observed_field, validity_mask):
    member_stack = prediction.shape[0]
    error_penalty = lax.optimization_barrier(jnp.sum(smooth_abs(prediction - observed_field[None]), axis=0)) / member_stack
    spread_penalty = jnp.zeros_like(error_penalty)
    for member_slice in range(member_stack - 1):
        spread_penalty = spread_penalty + lax.optimization_barrier(jnp.sum(smooth_abs(prediction[member_slice][None] - prediction[member_slice + 1:]), axis=0))
    return lax.optimization_barrier(jnp.sum(error_penalty - spread_penalty / (member_stack * (member_stack - 1)), axis=0)) * validity_mask

def shard_apply(model_parameters, extended, member_noise, neighbours, degree, dec_nodes):
    refreshed_latent = processor(extended, model_parameters[0], model_parameters[1], model_parameters[2], member_noise, neighbours, degree)
    return decoder(refreshed_latent, model_parameters[3], model_parameters[4], dec_nodes)

def reference(latent, send_rows, neighbours, degree, dec_nodes, counts, targets, member_noise, w_qkv, w_out, w_noise, decoder_hidden_weight, decoder_output_weight):
    space_shards = N_SPACE
    member_groups = N_MEMBER
    whole = latent.astype(jnp.float32).reshape(ENSEMBLE_SIZE, H, space_shards, NODE_DEV)
    send_index = send_rows.reshape(2, space_shards, RIM)
    pick = jax.vmap(lambda block, index: jnp.take(block, index, axis=2), in_axes=(2, 0), out_axes=2)
    upper_part = pick(whole, send_index[0])
    lower_part = pick(whole, send_index[1])
    zero_rim = jnp.zeros((ENSEMBLE_SIZE, H, 1, RIM), jnp.float32)
    low_rim = jnp.concatenate([zero_rim, upper_part[:, :, :-1]], axis=2)
    high_rim = jnp.concatenate([lower_part[:, :, 1:], zero_rim], axis=2)
    extended = jnp.concatenate([low_rim, whole, high_rim], axis=3)
    ext_rows = NODE_DEV + 2 * RIM
    ext_dev = extended.reshape(member_groups, MEMBERS_PER_SLOT, H, space_shards, ext_rows).transpose(3, 0, 1, 2, 4)
    ext_dev = ext_dev.reshape(space_shards * member_groups, MEMBERS_PER_SLOT, H, ext_rows)
    noise_dev = jnp.tile(member_noise.reshape(1, member_groups, MEMBERS_PER_SLOT, NOISE), (space_shards, 1, 1, 1))
    noise_dev = noise_dev.reshape(space_shards * member_groups, MEMBERS_PER_SLOT, NOISE)
    nbr_dev = jnp.repeat(neighbours.reshape(SLOTS, space_shards, NODE_DEV).transpose(1, 0, 2), member_groups, axis=0)
    degree_dev = jnp.repeat(degree.reshape(space_shards, NODE_DEV), member_groups, axis=0)
    edge_dev = jnp.repeat(dec_nodes.reshape(3, space_shards, SHARD_GRID_SIZE).transpose(1, 0, 2), member_groups, axis=0)
    model_parameters = (w_qkv, w_out, w_noise, decoder_hidden_weight, decoder_output_weight)
    input_fields = (ext_dev, noise_dev, nbr_dev, degree_dev, edge_dev)
    prediction = lax.map(lambda shard_parts: shard_apply(model_parameters, shard_parts[0], shard_parts[1], shard_parts[2], shard_parts[3], shard_parts[4]), input_fields)
    prediction = prediction.reshape(space_shards, ENSEMBLE_SIZE, OUTPUT_CHANNELS, SHARD_GRID_SIZE)
    validity_mask = (jnp.arange(SHARD_GRID_SIZE)[None, :] < counts[:, None]).astype(jnp.float32)
    shard_observed = targets.reshape(OUTPUT_CHANNELS, space_shards, SHARD_GRID_SIZE).transpose(1, 0, 2)

    def crps_per_shard(shard_parts):
        values, crps_back = jax.vjp(lambda block: pointwise_crps(block, shard_parts[1], shard_parts[2]), shard_parts[0])
        return (jnp.sum(values), crps_back(jnp.ones_like(values))[0])
    loss_per_shard, prediction_cotangent = lax.map(crps_per_shard, (prediction, shard_observed, validity_mask))
    shard_cotangent = prediction_cotangent.reshape(space_shards * member_groups, MEMBERS_PER_SLOT, OUTPUT_CHANNELS, SHARD_GRID_SIZE)

    def backward_step(running, shard_parts):

        def local_forward(ext_in, qkv_in, out_in, noise_in, first_in, second_in):
            return shard_apply((qkv_in, out_in, noise_in, first_in, second_in), ext_in, shard_parts[1], shard_parts[2], shard_parts[3], shard_parts[4])
        outputs, device_back = jax.vjp(local_forward, shard_parts[0], w_qkv, w_out, w_noise, decoder_hidden_weight, decoder_output_weight)
        gradients = device_back(shard_parts[5])
        running = tuple((acc + gradient.astype(jnp.float32) for acc, gradient in zip(running, gradients[1:])))
        return (running, gradients[0])
    start = tuple((jnp.zeros(weight.shape, jnp.float32) for weight in model_parameters))
    totals, d_ext = lax.scan(backward_step, start, input_fields + (shard_cotangent,))
    d_ext = d_ext.reshape(space_shards, member_groups, MEMBERS_PER_SLOT, H, ext_rows).transpose(1, 2, 3, 0, 4).reshape(ENSEMBLE_SIZE, H, space_shards, ext_rows)
    d_local = d_ext[:, :, :, RIM:RIM + NODE_DEV]
    from_next = jnp.concatenate([d_ext[:, :, 1:, :RIM], zero_rim], axis=2)
    from_prev = jnp.concatenate([zero_rim, d_ext[:, :, :-1, RIM + NODE_DEV:]], axis=2)
    scatter = jax.vmap(lambda block, first, first_add, second, second_add: block.at[:, :, first].add(first_add).at[:, :, second].add(second_add), in_axes=(2, 0, 2, 0, 2), out_axes=2)
    d_latent = scatter(d_local, send_index[0], from_next, send_index[1], from_prev).reshape(ENSEMBLE_SIZE, H, NODES)
    mean_fair_crps = jnp.sum(loss_per_shard) / (OUTPUT_CHANNELS * jnp.sum(counts).astype(jnp.float32))
    return (mean_fair_crps, d_latent, totals[0], totals[1], totals[2], totals[3], totals[4])
```

```python
import jax
import jax.numpy as jnp
from jax import lax
from jax.experimental import pallas as pl
from jax.experimental.pallas import tpu as pltpu
from jax.sharding import PartitionSpec as P

HEADS = 6
HEAD = 128
EPS = 1e-5
F32 = jnp.float32
BF16 = jnp.bfloat16
NN = (((1,), (0,)), ((), ()))
NT = (((1,), (1,)), ((), ()))
TN = (((0,), (0,)), ((), ()))
VMEM = pl.BlockSpec(memory_space=pltpu.VMEM)
SMEM = pl.BlockSpec(memory_space=pltpu.SMEM)
PARAMS = pltpu.CompilerParams(vmem_limit_bytes=48 * 1024 * 1024)


def mm(a, b, dims=NN):
    return lax.dot_general(a, b, dims, preferred_element_type=F32)


def call(body, out_shape, *args, smem=(), flops=0, scratch=()):
    out_shape = [jax.ShapeDtypeStruct(s, d) for s, d in out_shape]
    size = sum(a.size * a.dtype.itemsize for a in args)
    size += sum(o.size * o.dtype.itemsize for o in out_shape)
    return pl.pallas_call(
        body,
        out_shape=out_shape,
        in_specs=[SMEM if i in smem else VMEM for i in range(len(args))],
        out_specs=[VMEM] * len(out_shape),
        scratch_shapes=list(scratch),
        compiler_params=PARAMS,
        cost_estimate=pl.CostEstimate(flops=flops, bytes_accessed=size, transcendentals=0),
    )(*args)


def gains(noise, w_noise):
    return 1.0 + lax.dot_general(
        noise, w_noise, NN, precision=lax.Precision.HIGHEST, preferred_element_type=F32
    )


def normalise(rows):
    centre = rows - jnp.mean(rows, axis=1, keepdims=True)
    inverse = lax.rsqrt(jnp.mean(centre * centre, axis=1, keepdims=True) + EPS)
    return centre * inverse, inverse


def norm_back(cotangent, gain, hat, inverse):
    d_hat = cotangent * gain
    mean = jnp.mean(d_hat, axis=1, keepdims=True)
    along = jnp.mean(d_hat * hat, axis=1, keepdims=True)
    return inverse * (d_hat - mean - hat * along)


def send_body(latent, rows, sent):
    nodes = latent.shape[2]
    rim = rows.shape[1]
    both = jnp.concatenate([rows[0:1, :], rows[1:2, :]], axis=1)
    table = lax.broadcasted_iota(jnp.int32, (nodes, 2 * rim), 0) == both
    table = table.astype(F32).T.astype(BF16)
    for m in range(latent.shape[0]):
        picked = mm(table, latent[m], NT).astype(BF16)
        sent[0, m] = picked[:rim]
        sent[1, m] = picked[rim:]


def local_body(latent, noise, w_noise, w_qkv, own, normed, proj):
    gain = gains(noise[...], w_noise[...])
    members, _, nodes = latent.shape
    for m in range(members):
        rows = latent[m].astype(F32).T
        own[m] = rows.astype(BF16)
        hat, _ = normalise(rows)
        normed[m * nodes : (m + 1) * nodes] = (hat * gain[m : m + 1]).astype(BF16)
    proj[...] = mm(normed[...], w_qkv[...]).astype(BF16)


def slot_mask(nbr, degree, rows):
    slots, nodes = nbr.shape
    index = lax.broadcasted_iota(jnp.int32, (rows, nodes), 0)
    total = jnp.zeros((rows, nodes), F32)
    for j in range(slots):
        live = (index == nbr[j : j + 1, :]) & (degree[...] > j)
        total = total + live.astype(F32)
    return total / degree[...].astype(F32)


def point_table(dec_nodes, nodes):
    points = dec_nodes.shape[1]
    index = lax.broadcasted_iota(jnp.int32, (nodes, points), 0)
    total = jnp.zeros((nodes, points), F32)
    for j in range(dec_nodes.shape[0]):
        total = total + (index == dec_nodes[j : j + 1, :]).astype(F32)
    return total.astype(BF16)


def extend(own, low, high):
    return jnp.concatenate([low, own, high], axis=0)


def forward_body(
    own, proj, low, high, noise, w_noise, w_qkv, w_out, w_hid, w_pred, nbr, degree, dec_nodes,
    normed_rim, proj_rim, attended, stored, hidden, slope, forecast, table,
):
    members, nodes, width = own.shape
    rim = low.shape[1]
    gain = gains(noise[...], w_noise[...])
    for m in range(members):
        rows = jnp.concatenate([low[m], high[m]], axis=0).astype(F32)
        hat, _ = normalise(rows)
        normed_rim[2 * rim * m : 2 * rim * (m + 1)] = (hat * gain[m : m + 1]).astype(BF16)
    proj_rim[...] = mm(normed_rim[...], w_qkv[:, width:]).astype(BF16)
    mask = slot_mask(nbr, degree, nodes + 2 * rim)
    for m in range(members):
        here = slice(m * nodes, (m + 1) * nodes)
        lo = slice(2 * rim * m, 2 * rim * m + rim)
        hi = slice(2 * rim * m + rim, 2 * rim * (m + 1))
        for h in range(HEADS):
            at = [slice(k * width + h * HEAD, k * width + (h + 1) * HEAD) for k in range(3)]
            rim_at = [slice(a.start - width, a.stop - width) for a in at]
            key = extend(proj[here, at[1]], proj_rim[lo, rim_at[1]], proj_rim[hi, rim_at[1]])
            value = extend(proj[here, at[2]], proj_rim[lo, rim_at[2]], proj_rim[hi, rim_at[2]])
            score = mm(key, proj[here, at[0]], NT) * HEAD**-0.5
            weight = (jax.nn.sigmoid(score) * mask).astype(BF16)
            attended[here, at[0]] = mm(weight, value, TN).astype(BF16)
    branch = mm(attended[...], w_out[...])
    for m in range(members):
        here = slice(m * nodes, (m + 1) * nodes)
        stored[here] = (own[m].astype(F32) + branch[here]).astype(BF16)
    table[...] = point_table(dec_nodes, nodes)
    mixed = mm(stored[...], w_hid[...]).astype(BF16)
    block = 256
    for m in range(members):
        part = mixed[m * nodes : (m + 1) * nodes]
        for g in range(0, dec_nodes.shape[1], block):
            pre = mm(part, table[:, g : g + block], TN) * (1.0 / 3.0)
            sig = 0.5 * jnp.tanh(0.5 * pre) + 0.5
            hid = pre * sig
            hidden[m, :, g : g + block] = hid.astype(BF16)
            slope[m, :, g : g + block] = (sig + hid * (1.0 - sig)).astype(BF16)
            forecast[m, :, g : g + block] = mm(
                w_pred[...], hidden[m, :, g : g + block]
            ).astype(BF16)


def smooth(v):
    square = v * v + 0.25
    inverse = lax.rsqrt(square)
    return square * inverse - 0.5, v * inverse


def crps_body(
    live_count, mine, *rest
):
    (*others, targets, hidden, slope, table, stored, attended, w_out, w_hid, w_pred,
     d_updated, d_attended, g_out, g_hid, g_pred, loss, d_pre, d_cast) = rest
    members, channels, points = mine.shape
    total = members * (1 + len(others))
    block = 256
    nodes = table.shape[0]
    scale = 0.5 / (total * (total - 1))
    losses = []
    for g in range(0, points, block):
        at = slice(g, g + block)
        live = lax.broadcasted_iota(jnp.int32, (1, block), 1) + g < live_count[0]
        live = live.astype(F32)
        own = [mine[m, :, at].astype(F32) for m in range(members)]
        aim = targets[:, at]
        near = jnp.zeros((channels, block), F32)
        far = jnp.zeros((channels, block), F32)
        slopes = []
        for m in range(members):
            value, grad = smooth(own[m] - aim)
            near = near + value
            slopes.append([grad, jnp.zeros((channels, block), F32)])
        for a in range(members):
            for b in range(a + 1, members):
                value, grad = smooth(own[a] - own[b])
                far = far + 2.0 * value
                slopes[a][1] = slopes[a][1] + grad
                slopes[b][1] = slopes[b][1] - grad
        for other in others:
            for k in range(members):
                theirs = other[k, :, at].astype(F32)
                for m in range(members):
                    value, grad = smooth(own[m] - theirs)
                    far = far + value
                    slopes[m][1] = slopes[m][1] + grad
        for m in range(members):
            grad = slopes[m][0] * (1.0 / total) - slopes[m][1] * (2.0 * scale)
            d_cast[m, :, at] = (grad * live).astype(BF16)
        column = jnp.sum(near * (1.0 / total) - far * scale, axis=0, keepdims=True) * live
        losses.append(column)
    loss[...] = losses[0] + losses[1] + losses[2] + losses[3]
    back = w_pred[...].astype(F32).T.astype(BF16)
    grad = jnp.zeros((channels, hidden.shape[1]), F32)
    for m in range(members):
        grad = grad + mm(d_cast[m], hidden[m], NT)
        for g in range(0, points, block):
            at = slice(g, g + block)
            d_hid = mm(back, d_cast[m, :, at])
            d_pre[m, :, at] = (d_hid * slope[m, :, at].astype(F32)).astype(BF16)
    g_pred[...] = grad.astype(BF16)
    pooled = [
        (mm(table[...], d_pre[m], NT) * (1.0 / 3.0)).astype(BF16) for m in range(members)
    ]
    pooled = jnp.concatenate(pooled, axis=0)
    g_hid[...] = mm(stored[...], pooled, TN).astype(BF16)
    d_updated[...] = mm(pooled, w_hid[...], NT).astype(BF16)
    g_out[...] = mm(attended[...], d_updated[...], TN).astype(BF16)
    d_attended[...] = mm(d_updated[...], w_out[...], NT).astype(BF16)


def back_body(
    own, proj, low, high, noise, w_noise, w_qkv, normed, normed_rim, proj_rim, nbr, degree,
    d_updated, d_attended,
    d_own, d_low, d_high, g_qkv, g_noise, d_proj, d_rim,
):
    members, nodes, width = own.shape
    rim = low.shape[1]
    noises = noise[...]
    gain = gains(noises, w_noise[...])
    mask = slot_mask(nbr, degree, nodes + 2 * rim)
    for m in range(members):
        here = slice(m * nodes, (m + 1) * nodes)
        lo = slice(2 * rim * m, 2 * rim * m + rim)
        hi = slice(2 * rim * m + rim, 2 * rim * (m + 1))
        for h in range(HEADS):
            at = [slice(k * width + h * HEAD, k * width + (h + 1) * HEAD) for k in range(3)]
            rim_at = [slice(a.start - width, a.stop - width) for a in at]
            query = proj[here, at[0]]
            key = extend(proj[here, at[1]], proj_rim[lo, rim_at[1]], proj_rim[hi, rim_at[1]])
            value = extend(proj[here, at[2]], proj_rim[lo, rim_at[2]], proj_rim[hi, rim_at[2]])
            out = d_attended[here, at[0]]
            sig = jax.nn.sigmoid(mm(key, query, NT) * HEAD**-0.5)
            weight = sig * mask
            d_value = mm(weight.astype(BF16), out).astype(BF16)
            d_weight = mm(value, out, NT)
            d_score = (d_weight * weight * (1.0 - sig) * HEAD**-0.5).astype(BF16)
            d_key = mm(d_score, query).astype(BF16)
            d_proj[here, at[0]] = mm(d_score, key, TN).astype(BF16)
            for k, d in ((1, d_key), (2, d_value)):
                d_rim[lo, rim_at[k]] = d[:rim]
                d_proj[here, at[k]] = d[rim : rim + nodes]
                d_rim[hi, rim_at[k]] = d[rim + nodes :]
    g_qkv[:, :width] = mm(normed[...], d_proj[:, :width], TN).astype(BF16)
    g_qkv[:, width:] = (
        mm(normed[...], d_proj[:, width:], TN) + mm(normed_rim[...], d_rim[...], TN)
    ).astype(BF16)
    d_normed = mm(d_proj[...], w_qkv[...], NT)
    d_normed_rim = mm(d_rim[...], w_qkv[:, width:], NT)
    d_noise = jnp.zeros(g_noise.shape, F32)
    noise_columns = jnp.concatenate([noises] * (8 // members), axis=0).T
    for m in range(members):
        here = slice(m * nodes, (m + 1) * nodes)
        rims = slice(2 * rim * m, 2 * rim * (m + 1))
        hat, inverse = normalise(own[m].astype(F32))
        d_gain = jnp.sum(d_normed[here] * hat, axis=0, keepdims=True)
        rows = norm_back(d_normed[here], gain[m : m + 1], hat, inverse)
        d_own[m] = (rows + d_updated[here].astype(F32)).T
        hat, inverse = normalise(jnp.concatenate([low[m], high[m]], axis=0).astype(F32))
        d_gain = d_gain + jnp.sum(d_normed_rim[rims] * hat, axis=0, keepdims=True)
        rows = norm_back(d_normed_rim[rims], gain[m : m + 1], hat, inverse)
        d_low[m] = rows[:rim].astype(BF16)
        d_high[m] = rows[rim:].astype(BF16)
        d_noise = d_noise + noise_columns[:, m : m + 1] * d_gain
    g_noise[...] = d_noise.astype(g_noise.dtype)


def join_body(d_own, rows, from_next, from_prev, d_latent):
    nodes = d_own.shape[2]
    rim = rows.shape[1]
    index = lax.broadcasted_iota(jnp.int32, (nodes, 2 * rim), 0)
    both = jnp.concatenate([rows[0:1, :], rows[1:2, :]], axis=1)
    table = (index == both).astype(F32).T.astype(BF16)
    for m in range(d_own.shape[0]):
        back = jnp.concatenate([from_next[m], from_prev[m]], axis=0)
        d_latent[m] = d_own[m] + mm(back, table, TN)


def on_device(
    latent, send_rows, neighbours, degree, dec_nodes, counts, targets, member_noise,
    w_qkv, w_out, w_noise, w_hid, w_pred,
):
    members, width, nodes = latent.shape
    rim = send_rows.shape[1]
    points = dec_nodes.shape[1]
    channels = targets.shape[0]
    rows = members * nodes
    rims = members * 2 * rim
    degree = degree[None, :]
    size = lax.axis_size("space")
    up = [(i, i + 1) for i in range(size - 1)]
    down = [(i + 1, i) for i in range(size - 1)]

    (sent,) = call(send_body, [((2, members, rim, width), BF16)], latent, send_rows)
    low = lax.ppermute(sent[0], "space", up)
    high = lax.ppermute(sent[1], "space", down)
    own, normed, proj = call(
        local_body,
        [((members, nodes, width), BF16), ((rows, width), BF16), ((rows, 3 * width), BF16)],
        latent, member_noise, w_noise, w_qkv,
        flops=2 * rows * width * 3 * width,
    )
    normed_rim, proj_rim, attended, stored, hidden, slope, forecast, table = call(
        forward_body,
        [
            ((rims, width), BF16), ((rims, 2 * width), BF16), ((rows, width), BF16),
            ((rows, width), BF16), ((members, width, points), BF16),
            ((members, width, points), BF16), ((members, channels, points), BF16),
            ((nodes, points), BF16),
        ],
        own, proj, low, high, member_noise, w_noise, w_qkv, w_out, w_hid, w_pred,
        neighbours, degree, dec_nodes,
        flops=3 * 10**9,
    )
    gathered = gather_members(forecast)
    live_count = lax.dynamic_slice_in_dim(counts, lax.axis_index("space"), 1)
    d_updated, d_attended, g_out, g_hid, g_pred, loss = call(
        crps_body,
        [
            ((rows, width), BF16), ((rows, width), BF16), ((width, width), BF16),
            ((width, width), BF16), ((channels, width), BF16), ((1, 256), F32),
        ],
        live_count, forecast, *gathered, targets, hidden, slope, table, stored, attended,
        w_out, w_hid, w_pred,
        smem=(0,),
        scratch=[
            pltpu.VMEM((members, width, points), BF16),
            pltpu.VMEM((members, channels, points), BF16),
        ],
        flops=6 * 10**9,
    )
    d_own, d_low, d_high, g_qkv, g_noise = call(
        back_body,
        [
            ((members, width, nodes), F32), ((members, rim, width), BF16),
            ((members, rim, width), BF16), ((width, 3 * width), BF16), ((32, width), F32),
        ],
        own, proj, low, high, member_noise, w_noise, w_qkv, normed, normed_rim, proj_rim,
        neighbours, degree, d_updated, d_attended,
        scratch=[pltpu.VMEM((rows, 3 * width), BF16), pltpu.VMEM((rims, 2 * width), BF16)],
        flops=6 * 10**9,
    )
    everywhere = ("space", "member")
    g_out, g_hid, g_pred = lax.psum((g_out, g_hid, g_pred), everywhere)
    g_qkv, g_noise, loss = lax.psum((g_qkv, g_noise, loss), everywhere)
    from_next = lax.ppermute(d_low, "space", down)
    from_prev = lax.ppermute(d_high, "space", up)
    (d_latent,) = call(
        join_body, [((members, width, nodes), F32)], d_own, send_rows, from_next, from_prev
    )
    mean = jnp.sum(loss) / (channels * jnp.sum(counts).astype(F32))
    return (
        mean, d_latent, g_qkv.astype(F32), g_out.astype(F32), g_noise, g_hid.astype(F32),
        g_pred.astype(F32),
    )


def gather_members(forecast):
    size = lax.axis_size("member")
    return [
        lax.ppermute(forecast, "member", [(i, (i + s) % size) for i in range(size)])
        for s in range(1, size)
    ]


def solution(mesh):
    in_specs = (
        P("member", None, "space"), P(None, "space"), P(None, "space"), P("space"),
        P(None, "space"), P(), P(None, "space"), P("member", None), P(), P(), P(), P(), P(),
    )
    out_specs = (P(), P("member", None, "space"), P(), P(), P(), P(), P())
    return jax.shard_map(
        on_device, mesh=mesh, in_specs=in_specs, out_specs=out_specs, check_vma=False
    )
```

```python
import jax
import jax.numpy as jnp
from jax import lax
from jax.experimental import pallas as pl
from jax.experimental.pallas import tpu as pltpu
from jax.sharding import PartitionSpec as P

HEADS = 6
HEAD = 128
TILE = 128
GROUPS = 16
SLOTS_A = 5
SLOTS_B = 7
CHUNKS = 4 * GROUPS
EPS = 1e-5
F32 = jnp.float32
BF16 = jnp.bfloat16
NN = (((1,), (0,)), ((), ()))
NT = (((1,), (1,)), ((), ()))
TN = (((0,), (0,)), ((), ()))
VMEM = pl.BlockSpec(memory_space=pltpu.VMEM)
SMEM = pl.BlockSpec(memory_space=pltpu.SMEM)
PARAMS = pltpu.CompilerParams(vmem_limit_bytes=48 * 1024 * 1024)


def mm(a, b, dims=NN):
    return lax.dot_general(a, b, dims, preferred_element_type=F32)


def call(body, out_shape, *args, smem=(), flops=0, scratch=()):
    out_shape = [jax.ShapeDtypeStruct(s, d) for s, d in out_shape]
    size = sum(a.size * a.dtype.itemsize for a in args)
    size += sum(o.size * o.dtype.itemsize for o in out_shape)
    return pl.pallas_call(
        body,
        out_shape=out_shape,
        in_specs=[SMEM if i in smem else VMEM for i in range(len(args))],
        out_specs=[VMEM] * len(out_shape),
        scratch_shapes=list(scratch),
        compiler_params=PARAMS,
        cost_estimate=pl.CostEstimate(flops=flops, bytes_accessed=size, transcendentals=0),
    )(*args)


def gains(noise, w_noise):
    return 1.0 + lax.dot_general(
        noise, w_noise, NN, precision=lax.Precision.HIGHEST, preferred_element_type=F32
    )


def normalise(rows):
    centre = rows - jnp.mean(rows, axis=1, keepdims=True)
    inverse = lax.rsqrt(jnp.mean(centre * centre, axis=1, keepdims=True) + EPS)
    return centre * inverse, inverse


def norm_back(cotangent, gain, hat, inverse):
    d_hat = cotangent * gain
    mean = jnp.mean(d_hat, axis=1, keepdims=True)
    along = jnp.mean(d_hat * hat, axis=1, keepdims=True)
    return inverse * (d_hat - mean - hat * along)


def send_body(latent, rows, sent):
    nodes = latent.shape[2]
    rim = rows.shape[1]
    both = jnp.concatenate([rows[0:1, :], rows[1:2, :]], axis=1)
    table = lax.broadcasted_iota(jnp.int32, (nodes, 2 * rim), 0) == both
    table = table.astype(F32).T.astype(BF16)
    for m in range(latent.shape[0]):
        picked = mm(table, latent[m], NT).astype(BF16)
        sent[0, m] = picked[:rim]
        sent[1, m] = picked[rim:]


def local_body(latent, noise, w_noise, w_qkv, own, normed, proj):
    gain = gains(noise[...], w_noise[...])
    members, _, nodes = latent.shape
    for m in range(members):
        rows = latent[m].astype(F32).T
        own[m] = rows.astype(BF16)
        hat, _ = normalise(rows)
        normed[m * nodes : (m + 1) * nodes] = (hat * gain[m : m + 1]).astype(BF16)
    proj[...] = mm(normed[...], w_qkv[...]).astype(BF16)


def slot_mask(nbr, degree, rows):
    slots, nodes = nbr.shape
    index = lax.broadcasted_iota(jnp.int32, (rows, nodes), 0)
    total = jnp.zeros((rows, nodes), F32)
    for j in range(slots):
        live = (index == nbr[j : j + 1, :]) & (degree[...] > j)
        total = total + live.astype(F32)
    return total / degree[...].astype(F32)


def point_table(dec_nodes, nodes):
    points = dec_nodes.shape[1]
    index = lax.broadcasted_iota(jnp.int32, (nodes, points), 0)
    total = jnp.zeros((nodes, points), F32)
    for j in range(dec_nodes.shape[0]):
        total = total + (index == dec_nodes[j : j + 1, :]).astype(F32)
    return total.astype(BF16)


def extend(own, low, high):
    return jnp.concatenate([low, own, high], axis=0)


def forward_body(
    own, proj, low, high, noise, w_noise, w_qkv, w_out, w_hid, w_pred, nbr, degree, dec_nodes,
    normed_rim, proj_rim, attended, stored, hidden, slope, forecast, table,
):
    members, nodes, width = own.shape
    rim = low.shape[1]
    gain = gains(noise[...], w_noise[...])
    for m in range(members):
        rows = jnp.concatenate([low[m], high[m]], axis=0).astype(F32)
        hat, _ = normalise(rows)
        normed_rim[2 * rim * m : 2 * rim * (m + 1)] = (hat * gain[m : m + 1]).astype(BF16)
    proj_rim[...] = mm(normed_rim[...], w_qkv[:, width:]).astype(BF16)
    mask = slot_mask(nbr, degree, nodes + 2 * rim)
    for m in range(members):
        here = slice(m * nodes, (m + 1) * nodes)
        lo = slice(2 * rim * m, 2 * rim * m + rim)
        hi = slice(2 * rim * m + rim, 2 * rim * (m + 1))
        for h in range(HEADS):
            at = [slice(k * width + h * HEAD, k * width + (h + 1) * HEAD) for k in range(3)]
            rim_at = [slice(a.start - width, a.stop - width) for a in at]
            key = extend(proj[here, at[1]], proj_rim[lo, rim_at[1]], proj_rim[hi, rim_at[1]])
            value = extend(proj[here, at[2]], proj_rim[lo, rim_at[2]], proj_rim[hi, rim_at[2]])
            score = mm(key, proj[here, at[0]], NT) * HEAD**-0.5
            weight = (jax.nn.sigmoid(score) * mask).astype(BF16)
            attended[here, at[0]] = mm(weight, value, TN).astype(BF16)
    branch = mm(attended[...], w_out[...])
    for m in range(members):
        here = slice(m * nodes, (m + 1) * nodes)
        stored[here] = (own[m].astype(F32) + branch[here]).astype(BF16)
    table[...] = point_table(dec_nodes, nodes)
    mixed = mm(stored[...], w_hid[...]).astype(BF16)
    block = 256
    for m in range(members):
        part = mixed[m * nodes : (m + 1) * nodes]
        for g in range(0, dec_nodes.shape[1], block):
            pre = mm(part, table[:, g : g + block], TN) * (1.0 / 3.0)
            sig = 0.5 * jnp.tanh(0.5 * pre) + 0.5
            hid = pre * sig
            hidden[m, :, g : g + block] = hid.astype(BF16)
            slope[m, :, g : g + block] = (sig + hid * (1.0 - sig)).astype(BF16)
            forecast[m, :, g : g + block] = mm(
                w_pred[...], hidden[m, :, g : g + block]
            ).astype(BF16)


def smooth(v):
    square = v * v + 0.25
    inverse = lax.rsqrt(square)
    return square * inverse - 0.5, v * inverse


def crps_body(
    core, live_count, mine, *rest
):
    (*others, targets, hidden, slope, table, stored, attended, w_out, w_hid, w_pred,
     d_updated, d_attended, keep, send, loss, d_pre, d_cast, halves) = rest
    members, channels, points = mine.shape
    total = members * (1 + len(others))
    block = 256
    nodes = table.shape[0]
    scale = 0.5 / (total * (total - 1))
    losses = []
    for g in range(0, points, block):
        at = slice(g, g + block)
        live = lax.broadcasted_iota(jnp.int32, (1, block), 1) + g < live_count[0]
        live = live.astype(F32)
        own = [mine[m, :, at].astype(F32) for m in range(members)]
        aim = targets[:, at]
        near = jnp.zeros((channels, block), F32)
        far = jnp.zeros((channels, block), F32)
        slopes = []
        for m in range(members):
            value, grad = smooth(own[m] - aim)
            near = near + value
            slopes.append([grad, jnp.zeros((channels, block), F32)])
        for a in range(members):
            for b in range(a + 1, members):
                value, grad = smooth(own[a] - own[b])
                far = far + 2.0 * value
                slopes[a][1] = slopes[a][1] + grad
                slopes[b][1] = slopes[b][1] - grad
        for other in others:
            for k in range(members):
                theirs = other[k, :, at].astype(F32)
                for m in range(members):
                    value, grad = smooth(own[m] - theirs)
                    far = far + value
                    slopes[m][1] = slopes[m][1] + grad
        for m in range(members):
            grad = slopes[m][0] * (1.0 / total) - slopes[m][1] * (2.0 * scale)
            d_cast[m, :, at] = (grad * live).astype(BF16)
        column = jnp.sum(near * (1.0 / total) - far * scale, axis=0, keepdims=True) * live
        losses.append(column)
    for i in range(16):
        at = i % 2
        piece = losses[i // 2 % 4][:, TILE * at : TILE * (at + 1)]
        loss[i : i + 1] = piece.astype(BF16) if i < 8 else jnp.zeros((1, TILE), BF16)
    back = w_pred[...].astype(F32).T.astype(BF16)
    grad = jnp.zeros((channels, hidden.shape[1]), F32)
    for m in range(members):
        grad = grad + mm(d_cast[m], hidden[m], NT)
        for g in range(0, points, block):
            at = slice(g, g + block)
            d_hid = mm(back, d_cast[m, :, at])
            d_pre[m, :, at] = (d_hid * slope[m, :, at].astype(F32)).astype(BF16)
    g_pred = jnp.zeros((96 - channels, grad.shape[1]), F32)
    g_pred = jnp.concatenate([grad, g_pred], axis=0).astype(BF16)
    pooled = [
        (mm(table[...], d_pre[m], NT) * (1.0 / 3.0)).astype(BF16) for m in range(members)
    ]
    pooled = jnp.concatenate(pooled, axis=0)
    g_hid = mm(stored[...], pooled, TN).astype(BF16)
    d_updated[...] = mm(pooled, w_hid[...], NT).astype(BF16)
    g_out = mm(attended[...], d_updated[...], TN).astype(BF16)
    d_attended[...] = mm(d_updated[...], w_out[...], NT).astype(BF16)
    half = g_hid.shape[1] // 2
    for c in range(2):
        for k in range(GROUPS):
            for slot in range(SLOTS_A * 4):
                chunk, lane = 4 * k + slot // SLOTS_A, TILE * (slot % SLOTS_A)
                grad, row, column = tile_of_first(k, slot, (g_hid, g_out, g_pred))
                if grad is None:
                    piece = jnp.zeros((16, TILE), BF16)
                else:
                    column = c * half + TILE * column
                    piece = grad[16 * row : 16 * row + 16, column : column + TILE]
                halves[c, chunk, :, lane : lane + TILE] = piece
    keep[...] = halves[core[0]]
    send[...] = halves[1 - core[0]]


def tile_of_first(k, slot, grads):
    if slot < 18:
        part = slot % 9
        return grads[slot // 9], 3 * k + part // 3, part % 3
    tile = k + GROUPS * (slot - 18)
    if tile < 18:
        return grads[2], tile // 3, tile % 3
    return None, 0, 0


def attend_back_body(
    core, proj, proj_rim, nbr, degree, d_attended,
    d_proj, d_rim, send, mask,
):
    nodes = nbr.shape[1]
    members = proj.shape[0] // nodes
    width = HEADS * HEAD
    rim = proj_rim.shape[0] // (2 * members)
    per_half = HEADS // 2
    part = width // 2
    mask[...] = slot_mask(nbr, degree, nodes + 2 * rim)
    for m in range(members):
        here = slice(m * nodes, (m + 1) * nodes)
        lo = slice(2 * rim * m, 2 * rim * m + rim)
        hi = slice(2 * rim * m + rim, 2 * rim * (m + 1))
        for h in range(HEADS):
            at = [slice(k * width + h * HEAD, k * width + (h + 1) * HEAD) for k in range(3)]
            rim_at = [slice(a.start - width, a.stop - width) for a in at]
            query = proj[here, at[0]]
            key = extend(proj[here, at[1]], proj_rim[lo, rim_at[1]], proj_rim[hi, rim_at[1]])
            value = extend(proj[here, at[2]], proj_rim[lo, rim_at[2]], proj_rim[hi, rim_at[2]])
            out = d_attended[here, at[0]]
            sig = jax.nn.sigmoid(mm(key, query, NT) * HEAD**-0.5)
            weight = sig * mask[...]
            d_value = mm(weight.astype(BF16), out).astype(BF16)
            d_weight = mm(value, out, NT)
            d_score = (d_weight * weight * (1.0 - sig) * HEAD**-0.5).astype(BF16)
            d_key = mm(d_score, query).astype(BF16)
            c, j = h // per_half, h % per_half
            spot = [slice(k * part + j * HEAD, k * part + (j + 1) * HEAD) for k in range(3)]
            d_proj[c, here, spot[0]] = mm(d_score, key, TN).astype(BF16)
            for k, d in ((1, d_key), (2, d_value)):
                d_rim[c, lo, spot[k - 1]] = d[:rim]
                d_proj[c, here, spot[k]] = d[rim : rim + nodes]
                d_rim[c, hi, spot[k - 1]] = d[rim + nodes :]
    rows = members * nodes
    send[:rows] = d_proj[1 - core[0]]
    send[rows:, : 2 * part] = d_rim[1 - core[0]]
    send[rows:, 2 * part :] = jnp.zeros((2 * rim * members, part), BF16)


def norm_back_body(
    own, low, high, noise, w_noise, w_qkv, d_proj, d_rim, d_updated,
    d_own, d_low, d_high, g_noise,
):
    members, nodes, width = own.shape
    rim = low.shape[1]
    part = width // 2
    noises = noise[...]
    gain = gains(noises, w_noise[...])
    d_normed = jnp.zeros((members * nodes, width), F32)
    d_normed_rim = jnp.zeros((members * 2 * rim, width), F32)
    for c in range(2):
        for k in range(3):
            column = k * width + c * part
            weight = w_qkv[:, column : column + part]
            d_normed = d_normed + mm(d_proj[c, :, k * part : (k + 1) * part], weight, NT)
            if k:
                d_normed_rim = d_normed_rim + mm(
                    d_rim[c, :, (k - 1) * part : k * part], weight, NT
                )
    d_noise = jnp.zeros(g_noise.shape, F32)
    noise_columns = jnp.concatenate([noises] * (8 // members), axis=0).T
    for m in range(members):
        here = slice(m * nodes, (m + 1) * nodes)
        rims = slice(2 * rim * m, 2 * rim * (m + 1))
        hat, inverse = normalise(own[m].astype(F32))
        d_gain = jnp.sum(d_normed[here] * hat, axis=0, keepdims=True)
        rows = norm_back(d_normed[here], gain[m : m + 1], hat, inverse)
        d_own[m] = (rows + d_updated[here].astype(F32)).T
        hat, inverse = normalise(jnp.concatenate([low[m], high[m]], axis=0).astype(F32))
        d_gain = d_gain + jnp.sum(d_normed_rim[rims] * hat, axis=0, keepdims=True)
        rows = norm_back(d_normed_rim[rims], gain[m : m + 1], hat, inverse)
        d_low[m] = rows[:rim].astype(BF16)
        d_high[m] = rows[rim:].astype(BF16)
        d_noise = d_noise + noise_columns[:, m : m + 1] * d_gain
    g_noise[...] = d_noise.astype(BF16)


def pack_body(
    core, normed, normed_rim, normed_theirs, d_proj, d_rim, d_theirs, keep, came, g_noise, loss,
    packed, g_half,
):
    rows = normed.shape[0]
    wide = 2 * d_proj.shape[2] // 3
    width = normed.shape[1]
    mine = d_proj[core[0]]
    rim = d_rim[core[0]]
    for r in range(0, width, 256):
        at = slice(r, r + 256)
        total = mm(normed[:, at], mine, TN) + mm(normed_theirs[:rows, at], d_theirs[:rows], TN)
        g_half[at, : wide // 2] = total[:, : wide // 2].astype(BF16)
        edge = mm(normed_rim[:, at], rim, TN)
        edge = edge + mm(normed_theirs[rows:, at], d_theirs[rows:, :wide], TN)
        g_half[at, wide // 2 :] = (total[:, wide // 2 :] + edge).astype(BF16)
    first = TILE * SLOTS_A
    packed[:, :, :first] = (keep[...].astype(F32) + came[...].astype(F32)).astype(BF16)
    for k in range(GROUPS):
        for slot in range(SLOTS_B * 4):
            chunk, lane = 4 * k + slot // SLOTS_B, first + TILE * (slot % SLOTS_B)
            if slot < 27:
                row, column = 48 * k + 16 * (slot // 9), TILE * (slot % 9)
                piece = g_half[row : row + 16, column : column + TILE]
            elif k < 12:
                row, column = 16 * (k // 6), TILE * (k % 6)
                piece = g_noise[row : row + 16, column : column + TILE]
            elif k == 12:
                piece = loss[...]
            else:
                piece = jnp.zeros((16, TILE), BF16)
            packed[chunk, :, lane : lane + TILE] = piece


def sum_body(came, spread):
    chips, chunks = came.shape[0], came.shape[1]
    for j in range(chunks):
        total = came[0, j].astype(F32)
        for i in range(1, chips):
            total = total + came[i, j].astype(F32)
        total = total.astype(BF16)
        for i in range(chips):
            spread[i, j] = total


def unpack_body(
    core, counts, own, other, g_qkv, g_out, g_noise, g_hid, g_pred, mean, pred_rows
):
    k = pl.program_id(0)
    first_core = core[0] == 0
    width = g_hid.shape[1]
    half = width // 2
    for c in range(2):
        def tile(chunk, lane):
            at = (chunk, slice(None), slice(lane, lane + TILE))
            mine, theirs = own[at].astype(F32), other[at].astype(F32)
            return jnp.where(first_core == (c == 0), mine, theirs)

        for slot in range(18):
            target = (g_hid, g_out)[slot // 9]
            row, column = 16 * (slot % 9 // 3), c * half + TILE * (slot % 3)
            target[row : row + 16, column : column + TILE] = tile(
                slot // SLOTS_A, TILE * (slot % SLOTS_A)
            )
        for slot in range(27):
            row, column = 16 * (slot // 9), slot % 9
            column = width * (column // 3) + c * half + TILE * (column % 3)
            g_qkv[row : row + 16, column : column + TILE] = tile(
                slot // SLOTS_B, TILE * (SLOTS_A + slot % SLOTS_B)
            )
        for slot in (18, 19):
            index = k + GROUPS * (slot - 18)

            @pl.when(index < 18)
            def _(slot=slot, index=index, c=c, tile=tile):
                row = pl.multiple_of(16 * (index // 3), 16)
                column = pl.multiple_of(c * half + TILE * (index % 3), TILE)
                pred_rows[pl.ds(row, 16), pl.ds(column, TILE)] = tile(
                    slot // SLOTS_A, TILE * (slot % SLOTS_A)
                )

    spare = (3, slice(None), slice(TILE * (SLOTS_A + 6), TILE * (SLOTS_A + 7)))

    @pl.when(k < 12)
    def _():
        row = pl.multiple_of(16 * (k // 6), 16)
        column = pl.multiple_of(TILE * (k % 6), TILE)
        g_noise[pl.ds(row, 16), pl.ds(column, TILE)] = own[spare].astype(F32) + other[
            spare
        ].astype(F32)

    @pl.when(k == 12)
    def _():
        channels = g_pred.shape[0]
        total = jnp.sum(own[spare].astype(F32) + other[spare].astype(F32), keepdims=True)
        live = jnp.sum(counts[...].astype(F32), keepdims=True)
        mean[...] = total / (channels * live)

    @pl.when(k == GROUPS - 1)
    def _():
        g_pred[...] = pred_rows[: g_pred.shape[0]]


def join_body(d_own, rows, from_next, from_prev, d_latent):
    nodes = d_own.shape[2]
    rim = rows.shape[1]
    index = lax.broadcasted_iota(jnp.int32, (nodes, 2 * rim), 0)
    both = jnp.concatenate([rows[0:1, :], rows[1:2, :]], axis=1)
    table = (index == both).astype(F32).T.astype(BF16)
    for m in range(d_own.shape[0]):
        back = jnp.concatenate([from_next[m], from_prev[m]], axis=0)
        d_latent[m] = d_own[m] + mm(back, table, TN)


def on_device(
    latent, send_rows, neighbours, degree, dec_nodes, counts, targets, member_noise,
    w_qkv, w_out, w_noise, w_hid, w_pred,
):
    members, width, nodes = latent.shape
    rim = send_rows.shape[1]
    points = dec_nodes.shape[1]
    channels = targets.shape[0]
    rows = members * nodes
    rims = members * 2 * rim
    degree = degree[None, :]
    size = lax.axis_size("space")
    up = [(i, i + 1) for i in range(size - 1)]
    down = [(i + 1, i) for i in range(size - 1)]

    (sent,) = call(send_body, [((2, members, rim, width), BF16)], latent, send_rows)
    low = lax.ppermute(sent[0], "space", up)
    high = lax.ppermute(sent[1], "space", down)
    own, normed, proj = call(
        local_body,
        [((members, nodes, width), BF16), ((rows, width), BF16), ((rows, 3 * width), BF16)],
        latent, member_noise, w_noise, w_qkv,
        flops=2 * rows * width * 3 * width,
    )
    normed_rim, proj_rim, attended, stored, hidden, slope, forecast, table = call(
        forward_body,
        [
            ((rims, width), BF16), ((rims, 2 * width), BF16), ((rows, width), BF16),
            ((rows, width), BF16), ((members, width, points), BF16),
            ((members, width, points), BF16), ((members, channels, points), BF16),
            ((nodes, points), BF16),
        ],
        own, proj, low, high, member_noise, w_noise, w_qkv, w_out, w_hid, w_pred,
        neighbours, degree, dec_nodes,
        flops=3 * 10**9,
    )
    gathered = gather_members(forecast)
    packed_shape = (CHUNKS, 16, TILE * (SLOTS_A + SLOTS_B))
    first_shape = (CHUNKS, 16, TILE * SLOTS_A)
    core = lax.axis_index("core").astype(jnp.int32)[None]
    swap = [(0, 1), (1, 0)]
    normed_theirs = lax.ppermute(jnp.concatenate([normed, normed_rim], axis=0), "core", swap)
    live_count = lax.dynamic_slice_in_dim(counts, lax.axis_index("space"), 1)
    d_updated, d_attended, keep, send, loss = call(
        crps_body,
        [
            ((rows, width), BF16), ((rows, width), BF16), (first_shape, BF16),
            (first_shape, BF16), ((16, TILE), BF16),
        ],
        core, live_count, forecast, *gathered, targets, hidden, slope, table, stored, attended,
        w_out, w_hid, w_pred,
        smem=(0, 1),
        scratch=[
            pltpu.VMEM((members, width, points), BF16),
            pltpu.VMEM((members, channels, points), BF16),
            pltpu.VMEM((2,) + first_shape, BF16),
        ],
        flops=6 * 10**9,
    )
    came = lax.ppermute(send, "core", swap)
    d_proj, d_rim, d_send = call(
        attend_back_body,
        [
            ((2, rows, 3 * width // 2), BF16), ((2, rims, width), BF16),
            ((rows + rims, 3 * width // 2), BF16),
        ],
        core, proj, proj_rim, neighbours, degree, d_attended,
        smem=(0,),
        scratch=[pltpu.VMEM((nodes + 2 * rim, nodes), F32)],
        flops=2 * 10**9,
    )
    d_theirs = lax.ppermute(d_send, "core", swap)
    d_own, d_low, d_high, g_noise = call(
        norm_back_body,
        [
            ((members, width, nodes), F32), ((members, rim, width), BF16),
            ((members, rim, width), BF16), ((32, width), BF16),
        ],
        own, low, high, member_noise, w_noise, w_qkv, d_proj, d_rim, d_updated,
        flops=2 * 10**9,
    )
    (packed,) = call(
        pack_body,
        [(packed_shape, BF16)],
        core, normed, normed_rim, normed_theirs, d_proj, d_rim, d_theirs, keep, came, g_noise,
        loss,
        smem=(0,),
        scratch=[pltpu.VMEM((width, 3 * width // 2), BF16)],
        flops=2 * 10**9,
    )
    chips = ("space", "zhi")
    count = lax.axis_size(chips)
    parts = lax.all_to_all(packed, chips, 0, 0, tiled=True)
    (spread,) = call(
        sum_body,
        [((count, CHUNKS // count) + packed_shape[1:], BF16)],
        parts.reshape((count, CHUNKS // count) + packed_shape[1:]),
    )
    half = lax.all_to_all(spread.reshape(packed_shape), chips, 0, 0, tiled=True)
    other = lax.ppermute(half, "core", swap)
    from_next = lax.ppermute(d_low, "space", down)
    from_prev = lax.ppermute(d_high, "space", up)
    (d_latent,) = call(
        join_body, [((members, width, nodes), F32)], d_own, send_rows, from_next, from_prev
    )
    block = pl.BlockSpec((4,) + packed_shape[1:], lambda k: (k, 0, 0))
    whole = lambda shape: pl.BlockSpec(shape, lambda k: (0, 0))
    g_qkv, g_out, g_noise, g_hid, g_pred, mean = pl.pallas_call(
        unpack_body,
        grid=(GROUPS,),
        out_shape=[
            jax.ShapeDtypeStruct(shape, F32)
            for shape in (
                (width, 3 * width), (width, width), (32, width), (width, width),
                (channels, width), (1, 1),
            )
        ],
        in_specs=[SMEM, whole((1, counts.shape[0])), block, block],
        out_specs=[
            pl.BlockSpec((48, 3 * width), lambda k: (k, 0)),
            pl.BlockSpec((48, width), lambda k: (k, 0)),
            whole((32, width)),
            pl.BlockSpec((48, width), lambda k: (k, 0)),
            whole((channels, width)),
            whole((1, 1)),
        ],
        scratch_shapes=[pltpu.VMEM((96, width), F32)],
        compiler_params=PARAMS,
    )(core, counts[None, :], half, other)
    return mean[0, 0], d_latent, g_qkv, g_out, g_noise, g_hid, g_pred


def gather_members(forecast):
    axes = ("zhi", "core")
    return [
        lax.ppermute(forecast, axes, [(i, i ^ step) for i in range(4)]) for step in (1, 2, 3)
    ]


def solution(mesh):
    space = mesh.shape["space"]
    mesh = jax.sharding.Mesh(mesh.devices.reshape(space, 2, 2), ("space", "zhi", "core"))
    member = ("zhi", "core")
    in_specs = (
        P(member, None, "space"), P(None, "space"), P(None, "space"), P("space"),
        P(None, "space"), P(), P(None, "space"), P(member, None), P(), P(), P(), P(), P(),
    )
    out_specs = (P(), P(member, None, "space"), P(), P(), P(), P(), P())
    return jax.shard_map(
        on_device, mesh=mesh, in_specs=in_specs, out_specs=out_specs, check_vma=False
    )
```

```python
import jax
import jax.numpy as jnp
from jax import lax
from jax.experimental import pallas as pl
from jax.experimental.pallas import tpu as pltpu
from jax.sharding import PartitionSpec as P

HEADS = 6
HEAD = 128
TILE = 128
GROUPS = 16
BLOCKS = 4
SLOTS_A = 5
SLOTS_B = 7
CHUNKS = 4 * GROUPS
EPS = 1e-5
F32 = jnp.float32
BF16 = jnp.bfloat16
NN = (((1,), (0,)), ((), ()))
NT = (((1,), (1,)), ((), ()))
TN = (((0,), (0,)), ((), ()))
VMEM = pl.BlockSpec(memory_space=pltpu.VMEM)
SMEM = pl.BlockSpec(memory_space=pltpu.SMEM)
MIB = 1024 * 1024


def mm(a, b, dims=NN):
    return lax.dot_general(a, b, dims, preferred_element_type=F32)


def call(body, out_shape, *args, smem=(), flops=0, scratch=(), vmem=16):
    out_shape = [jax.ShapeDtypeStruct(s, d) for s, d in out_shape]
    size = sum(a.size * a.dtype.itemsize for a in args)
    size += sum(o.size * o.dtype.itemsize for o in out_shape)
    return pl.pallas_call(
        body,
        out_shape=out_shape,
        in_specs=[SMEM if i in smem else VMEM for i in range(len(args))],
        out_specs=[VMEM] * len(out_shape),
        scratch_shapes=list(scratch),
        compiler_params=pltpu.CompilerParams(vmem_limit_bytes=vmem * MIB),
        cost_estimate=pl.CostEstimate(flops=flops, bytes_accessed=size, transcendentals=0),
    )(*args)


def gains(noise, w_noise):
    return 1.0 + lax.dot_general(
        noise, w_noise, NN, precision=lax.Precision.HIGHEST, preferred_element_type=F32
    )


def normalise(rows):
    centre = rows - jnp.mean(rows, axis=1, keepdims=True)
    inverse = lax.rsqrt(jnp.mean(centre * centre, axis=1, keepdims=True) + EPS)
    return centre * inverse, inverse


def norm_back(cotangent, gain, hat, inverse):
    d_hat = cotangent * gain
    mean = jnp.mean(d_hat, axis=1, keepdims=True)
    along = jnp.mean(d_hat * hat, axis=1, keepdims=True)
    return inverse * (d_hat - mean - hat * along)


def send_body(latent, rows, sent):
    nodes = latent.shape[2]
    rim = rows.shape[1]
    both = jnp.concatenate([rows[0:1, :], rows[1:2, :]], axis=1)
    table = lax.broadcasted_iota(jnp.int32, (nodes, 2 * rim), 0) == both
    table = table.astype(F32).T.astype(BF16)
    for m in range(latent.shape[0]):
        picked = mm(table, latent[m], NT).astype(BF16)
        sent[0, m] = picked[:rim]
        sent[1, m] = picked[rim:]


def local_body(latent, noise, w_noise, w_qkv, own, normed, proj):
    gain = gains(noise[...], w_noise[...])
    members, _, nodes = latent.shape
    for m in range(members):
        rows = latent[m].astype(F32).T
        own[m] = rows.astype(BF16)
        hat, _ = normalise(rows)
        normed[m * nodes : (m + 1) * nodes] = (hat * gain[m : m + 1]).astype(BF16)
    proj[...] = mm(normed[...], w_qkv[...]).astype(BF16)


def slot_mask(nbr, degree, rows):
    slots, nodes = nbr.shape
    index = lax.broadcasted_iota(jnp.int32, (rows, nodes), 0)
    total = jnp.zeros((rows, nodes), F32)
    for j in range(slots):
        live = (index == nbr[j : j + 1, :]) & (degree[...] > j)
        total = total + live.astype(F32)
    return total / degree[...].astype(F32)


def point_table(dec_nodes, nodes):
    points = dec_nodes.shape[1]
    index = lax.broadcasted_iota(jnp.int32, (nodes, points), 0)
    total = jnp.zeros((nodes, points), F32)
    for j in range(dec_nodes.shape[0]):
        total = total + (index == dec_nodes[j : j + 1, :]).astype(F32)
    return total.astype(BF16)


def extend(own, low, high):
    return jnp.concatenate([low, own, high], axis=0)


def forward_body(
    own, proj, low, high, noise, w_noise, w_qkv, w_out, w_hid, w_pred, nbr, degree, dec_nodes,
    normed_rim, proj_rim, attended, stored, hidden, slope, forecast, table,
):
    members, nodes, width = own.shape
    rim = low.shape[1]
    gain = gains(noise[...], w_noise[...])
    for m in range(members):
        rows = jnp.concatenate([low[m], high[m]], axis=0).astype(F32)
        hat, _ = normalise(rows)
        normed_rim[2 * rim * m : 2 * rim * (m + 1)] = (hat * gain[m : m + 1]).astype(BF16)
    proj_rim[...] = mm(normed_rim[...], w_qkv[:, width:]).astype(BF16)
    mask = slot_mask(nbr, degree, nodes + 2 * rim)
    for m in range(members):
        here = slice(m * nodes, (m + 1) * nodes)
        lo = slice(2 * rim * m, 2 * rim * m + rim)
        hi = slice(2 * rim * m + rim, 2 * rim * (m + 1))
        for h in range(HEADS):
            at = [slice(k * width + h * HEAD, k * width + (h + 1) * HEAD) for k in range(3)]
            rim_at = [slice(a.start - width, a.stop - width) for a in at]
            key = extend(proj[here, at[1]], proj_rim[lo, rim_at[1]], proj_rim[hi, rim_at[1]])
            value = extend(proj[here, at[2]], proj_rim[lo, rim_at[2]], proj_rim[hi, rim_at[2]])
            score = mm(key, proj[here, at[0]], NT) * HEAD**-0.5
            weight = (jax.nn.sigmoid(score) * mask).astype(BF16)
            attended[here, at[0]] = mm(weight, value, TN).astype(BF16)
    branch = mm(attended[...], w_out[...])
    for m in range(members):
        here = slice(m * nodes, (m + 1) * nodes)
        stored[here] = (own[m].astype(F32) + branch[here]).astype(BF16)
    table[...] = point_table(dec_nodes, nodes)
    mixed = mm(stored[...], w_hid[...]).astype(BF16)
    block = 256
    for m in range(members):
        part = mixed[m * nodes : (m + 1) * nodes]
        for g in range(0, dec_nodes.shape[1], block):
            pre = mm(part, table[:, g : g + block], TN) * (1.0 / 3.0)
            sig = 0.5 * jnp.tanh(0.5 * pre) + 0.5
            hid = pre * sig
            hidden[m, :, g : g + block] = hid.astype(BF16)
            slope[m, :, g : g + block] = (sig + hid * (1.0 - sig)).astype(BF16)
            forecast[m, :, g : g + block] = mm(
                w_pred[...], hidden[m, :, g : g + block]
            ).astype(BF16)


def smooth(v):
    square = v * v + 0.25
    inverse = lax.rsqrt(square)
    return square * inverse - 0.5, v * inverse


def crps_body(
    core, live_count, mine, *rest
):
    (*others, targets, hidden, slope, table, stored, attended, w_out, w_hid, w_pred,
     d_updated, d_attended, keep, send, loss, d_pre, d_cast, halves) = rest
    members, channels, points = mine.shape
    total = members * (1 + len(others))
    block = 256
    nodes = table.shape[0]
    scale = 0.5 / (total * (total - 1))
    losses = []
    for g in range(0, points, block):
        at = slice(g, g + block)
        live = lax.broadcasted_iota(jnp.int32, (1, block), 1) + g < live_count[0]
        live = live.astype(F32)
        own = [mine[m, :, at].astype(F32) for m in range(members)]
        aim = targets[:, at]
        near = jnp.zeros((channels, block), F32)
        far = jnp.zeros((channels, block), F32)
        slopes = []
        for m in range(members):
            value, grad = smooth(own[m] - aim)
            near = near + value
            slopes.append([grad, jnp.zeros((channels, block), F32)])
        for a in range(members):
            for b in range(a + 1, members):
                value, grad = smooth(own[a] - own[b])
                far = far + 2.0 * value
                slopes[a][1] = slopes[a][1] + grad
                slopes[b][1] = slopes[b][1] - grad
        for other in others:
            for k in range(members):
                theirs = other[k, :, at].astype(F32)
                for m in range(members):
                    value, grad = smooth(own[m] - theirs)
                    far = far + value
                    slopes[m][1] = slopes[m][1] + grad
        for m in range(members):
            grad = slopes[m][0] * (1.0 / total) - slopes[m][1] * (2.0 * scale)
            d_cast[m, :, at] = (grad * live).astype(BF16)
        column = jnp.sum(near * (1.0 / total) - far * scale, axis=0, keepdims=True) * live
        losses.append(column)
    for i in range(16):
        at = i % 2
        piece = losses[i // 2 % 4][:, TILE * at : TILE * (at + 1)]
        loss[i : i + 1] = piece.astype(BF16) if i < 8 else jnp.zeros((1, TILE), BF16)
    back = w_pred[...].astype(F32).T.astype(BF16)
    grad = jnp.zeros((channels, hidden.shape[1]), F32)
    for m in range(members):
        grad = grad + mm(d_cast[m], hidden[m], NT)
        for g in range(0, points, block):
            at = slice(g, g + block)
            d_hid = mm(back, d_cast[m, :, at])
            d_pre[m, :, at] = (d_hid * slope[m, :, at].astype(F32)).astype(BF16)
    g_pred = jnp.zeros((96 - channels, grad.shape[1]), F32)
    g_pred = jnp.concatenate([grad, g_pred], axis=0).astype(BF16)
    pooled = [
        (mm(table[...], d_pre[m], NT) * (1.0 / 3.0)).astype(BF16) for m in range(members)
    ]
    pooled = jnp.concatenate(pooled, axis=0)
    g_hid = mm(stored[...], pooled, TN).astype(BF16)
    d_updated[...] = mm(pooled, w_hid[...], NT).astype(BF16)
    g_out = mm(attended[...], d_updated[...], TN).astype(BF16)
    d_attended[...] = mm(d_updated[...], w_out[...], NT).astype(BF16)
    half = g_hid.shape[1] // 2
    for c in range(2):
        for k in range(GROUPS):
            for slot in range(SLOTS_A * 4):
                chunk, lane = 4 * k + slot // SLOTS_A, TILE * (slot % SLOTS_A)
                grad, row, column = tile_of_first(k, slot, (g_hid, g_out, g_pred))
                if grad is None:
                    piece = jnp.zeros((16, TILE), BF16)
                else:
                    column = c * half + TILE * column
                    piece = grad[16 * row : 16 * row + 16, column : column + TILE]
                halves[c, chunk, :, lane : lane + TILE] = piece
    keep[...] = halves[core[0]]
    send[...] = halves[1 - core[0]]


def tile_of_first(k, slot, grads):
    if slot < 18:
        part = slot % 9
        return grads[slot // 9], 3 * k + part // 3, part % 3
    tile = k + GROUPS * (slot - 18)
    if tile < 18:
        return grads[2], tile // 3, tile % 3
    return None, 0, 0


def attend_back_body(
    core, proj, proj_rim, nbr, degree, d_attended,
    d_proj, d_rim, send, mask,
):
    nodes = nbr.shape[1]
    members = proj.shape[0] // nodes
    width = HEADS * HEAD
    rim = proj_rim.shape[0] // (2 * members)
    per_half = HEADS // 2
    part = width // 2
    mask[...] = slot_mask(nbr, degree, nodes + 2 * rim)
    for m in range(members):
        here = slice(m * nodes, (m + 1) * nodes)
        lo = slice(2 * rim * m, 2 * rim * m + rim)
        hi = slice(2 * rim * m + rim, 2 * rim * (m + 1))
        for h in range(HEADS):
            at = [slice(k * width + h * HEAD, k * width + (h + 1) * HEAD) for k in range(3)]
            rim_at = [slice(a.start - width, a.stop - width) for a in at]
            query = proj[here, at[0]]
            key = extend(proj[here, at[1]], proj_rim[lo, rim_at[1]], proj_rim[hi, rim_at[1]])
            value = extend(proj[here, at[2]], proj_rim[lo, rim_at[2]], proj_rim[hi, rim_at[2]])
            out = d_attended[here, at[0]]
            sig = jax.nn.sigmoid(mm(key, query, NT) * HEAD**-0.5)
            weight = sig * mask[...]
            d_value = mm(weight.astype(BF16), out).astype(BF16)
            d_weight = mm(value, out, NT)
            d_score = (d_weight * weight * (1.0 - sig) * HEAD**-0.5).astype(BF16)
            d_key = mm(d_score, query).astype(BF16)
            c, j = h // per_half, h % per_half
            spot = [slice(k * part + j * HEAD, k * part + (j + 1) * HEAD) for k in range(3)]
            d_proj[c, here, spot[0]] = mm(d_score, key, TN).astype(BF16)
            for k, d in ((1, d_key), (2, d_value)):
                d_rim[c, lo, spot[k - 1]] = d[:rim]
                d_proj[c, here, spot[k]] = d[rim : rim + nodes]
                d_rim[c, hi, spot[k - 1]] = d[rim + nodes :]
    rows = members * nodes
    send[:rows] = d_proj[1 - core[0]]
    send[rows:, : 2 * part] = d_rim[1 - core[0]]
    send[rows:, 2 * part :] = jnp.zeros((2 * rim * members, part), BF16)


def norm_back_body(
    own, low, high, noise, w_noise, w_qkv, d_proj, d_rim, d_updated,
    d_own, d_low, d_high, g_noise,
):
    members, nodes, width = own.shape
    rim = low.shape[1]
    part = width // 2
    noises = noise[...]
    gain = gains(noises, w_noise[...])
    d_normed = jnp.zeros((members * nodes, width), F32)
    d_normed_rim = jnp.zeros((members * 2 * rim, width), F32)
    for c in range(2):
        for k in range(3):
            column = k * width + c * part
            weight = w_qkv[:, column : column + part]
            d_normed = d_normed + mm(d_proj[c, :, k * part : (k + 1) * part], weight, NT)
            if k:
                d_normed_rim = d_normed_rim + mm(
                    d_rim[c, :, (k - 1) * part : k * part], weight, NT
                )
    d_noise = jnp.zeros(g_noise.shape, F32)
    noise_columns = jnp.concatenate([noises] * (8 // members), axis=0).T
    for m in range(members):
        here = slice(m * nodes, (m + 1) * nodes)
        rims = slice(2 * rim * m, 2 * rim * (m + 1))
        hat, inverse = normalise(own[m].astype(F32))
        d_gain = jnp.sum(d_normed[here] * hat, axis=0, keepdims=True)
        rows = norm_back(d_normed[here], gain[m : m + 1], hat, inverse)
        d_own[m] = (rows + d_updated[here].astype(F32)).T
        hat, inverse = normalise(jnp.concatenate([low[m], high[m]], axis=0).astype(F32))
        d_gain = d_gain + jnp.sum(d_normed_rim[rims] * hat, axis=0, keepdims=True)
        rows = norm_back(d_normed_rim[rims], gain[m : m + 1], hat, inverse)
        d_low[m] = rows[:rim].astype(BF16)
        d_high[m] = rows[rim:].astype(BF16)
        d_noise = d_noise + noise_columns[:, m : m + 1] * d_gain
    g_noise[...] = d_noise.astype(BF16)


def pack_body(
    core, normed, normed_rim, normed_theirs, d_proj, d_rim, d_theirs, keep, came, g_noise, loss,
    packed, g_half,
):
    rows = normed.shape[0]
    wide = 2 * d_proj.shape[2] // 3
    width = normed.shape[1]
    mine = d_proj[core[0]]
    rim = d_rim[core[0]]
    for r in range(0, width, 256):
        at = slice(r, r + 256)
        total = mm(normed[:, at], mine, TN) + mm(normed_theirs[:rows, at], d_theirs[:rows], TN)
        g_half[at, : wide // 2] = total[:, : wide // 2].astype(BF16)
        edge = mm(normed_rim[:, at], rim, TN)
        edge = edge + mm(normed_theirs[rows:, at], d_theirs[rows:, :wide], TN)
        g_half[at, wide // 2 :] = (total[:, wide // 2 :] + edge).astype(BF16)
    first = TILE * SLOTS_A
    packed[:, :, :first] = (keep[...].astype(F32) + came[...].astype(F32)).astype(BF16)
    for k in range(GROUPS):
        for slot in range(SLOTS_B * 4):
            chunk, lane = 4 * k + slot // SLOTS_B, first + TILE * (slot % SLOTS_B)
            if slot < 27:
                row, column = 48 * k + 16 * (slot // 9), TILE * (slot % 9)
                piece = g_half[row : row + 16, column : column + TILE]
            elif k < 12:
                row, column = 16 * (k // 6), TILE * (k % 6)
                piece = g_noise[row : row + 16, column : column + TILE]
            elif k == 12:
                piece = loss[...]
            else:
                piece = jnp.zeros((16, TILE), BF16)
            packed[chunk, :, lane : lane + TILE] = piece


def sum_body(came, spread):
    chips, chunks = came.shape[0], came.shape[1]
    for j in range(chunks):
        total = came[0, j].astype(F32)
        for i in range(1, chips):
            total = total + came[i, j].astype(F32)
        total = total.astype(BF16)
        for i in range(chips):
            spread[i, j] = total


def unpack_body(
    core, half, *rest
):
    (g_qkv, g_out, g_hid, g_pred, g_noise, loss, pred_rows) = rest[-7:]
    before = rest[:-7]
    r, section = pl.program_id(0), pl.program_id(1)
    per_block = GROUPS // BLOCKS

    def tile(group, slot, first=0, size=SLOTS_A):
        lane = first + TILE * (slot % size)
        return half[4 * group + slot // size, :, lane : lane + TILE].astype(F32)

    for group in range(per_block):
        for row in range(3):
            at = slice(48 * group + 16 * row, 48 * group + 16 * row + 16)
            for s in range(3):

                @pl.when(section == s)
                def _(group=group, row=row, at=at, s=s):
                    for j in range(3):
                        g_qkv[at, TILE * j : TILE * (j + 1)] = tile(
                            group, 9 * row + 3 * s + j, TILE * SLOTS_A, SLOTS_B
                        )

    @pl.when(section == 0)
    def _():
        for group in range(per_block):
            for slot in range(18):
                target = (g_hid, g_out)[slot // 9]
                row, column = 48 * group + 16 * (slot % 9 // 3), TILE * (slot % 3)
                target[row : row + 16, column : column + TILE] = tile(group, slot)
            k = per_block * r + group
            for slot in (18, 19):
                index = k + GROUPS * (slot - 18)

                @pl.when(index < 18)
                def _(slot=slot, index=index, group=group):
                    row = pl.multiple_of(16 * (index // 3), 16)
                    column = pl.multiple_of(TILE * (index % 3), TILE)
                    pred_rows[pl.ds(row, 16), pl.ds(column, TILE)] = tile(group, slot)

            spare = tile(group, 27, TILE * SLOTS_A, SLOTS_B)

            @pl.when(k < 12)
            def _(k=k, spare=spare):
                row = pl.multiple_of(16 * (k // 6), 16)
                column = pl.multiple_of(TILE * (k % 6), TILE)
                here = (pl.ds(row, 16), pl.ds(column, TILE))
                g_noise[here] = spare + before[-2][here] if before else spare

            @pl.when(k == 12)
            def _(spare=spare):
                total = jnp.sum(spare, keepdims=True)
                loss[...] = total + before[-1][...] if before else total

        @pl.when(r == BLOCKS - 1)
        def _():
            g_pred[...] = pred_rows[: g_pred.shape[0]]


def unpack(which, half, width, channels, before=()):
    wide = width // 2
    rows = width // BLOCKS
    const = lambda r, s, c: (0, 0)
    spec = lambda shape, at: pl.BlockSpec(shape, at)
    in_specs = [spec((CHUNKS // BLOCKS,) + half.shape[1:], lambda r, s, c: (r, 0, 0))]
    if before:
        in_specs += [pl.BlockSpec(memory_space=pl.ANY)] * 4
        in_specs += [spec((32, width), const), spec((1, 1), const)]
    shapes = (
        (width, 3 * width), (width, width), (width, width), (channels, width), (32, width), (1, 1),
    )
    return pl.pallas_call(
        unpack_body,
        grid_spec=pltpu.PrefetchScalarGridSpec(
            num_scalar_prefetch=1,
            grid=(BLOCKS, 3),
            in_specs=in_specs,
            out_specs=[
                spec((rows, wide), lambda r, s, c: (r, 2 * s + c[0])),
                spec((rows, wide), lambda r, s, c: (r, c[0])),
                spec((rows, wide), lambda r, s, c: (r, c[0])),
                spec((channels, wide), lambda r, s, c: (0, c[0])),
                spec((32, width), const),
                spec((1, 1), const),
            ],
            scratch_shapes=[pltpu.VMEM((96, wide), F32)],
        ),
        out_shape=[jax.ShapeDtypeStruct(shape, F32) for shape in shapes],
        input_output_aliases={2 + i: i for i in range(4)} if before else {},
        compiler_params=pltpu.CompilerParams(vmem_limit_bytes=16 * MIB),
        cost_estimate=pl.CostEstimate(flops=0, bytes_accessed=9 * 10**6, transcendentals=0),
    )(which, half, *before)


def join_body(d_own, rows, from_next, from_prev, d_latent):
    nodes = d_own.shape[2]
    rim = rows.shape[1]
    index = lax.broadcasted_iota(jnp.int32, (nodes, 2 * rim), 0)
    both = jnp.concatenate([rows[0:1, :], rows[1:2, :]], axis=1)
    table = (index == both).astype(F32).T.astype(BF16)
    for m in range(d_own.shape[0]):
        back = jnp.concatenate([from_next[m], from_prev[m]], axis=0)
        d_latent[m] = d_own[m] + mm(back, table, TN)


def on_device(
    latent, send_rows, neighbours, degree, dec_nodes, counts, targets, member_noise,
    w_qkv, w_out, w_noise, w_hid, w_pred,
):
    members, width, nodes = latent.shape
    rim = send_rows.shape[1]
    points = dec_nodes.shape[1]
    channels = targets.shape[0]
    rows = members * nodes
    rims = members * 2 * rim
    degree = degree[None, :]
    size = lax.axis_size("space")
    up = [(i, i + 1) for i in range(size - 1)]
    down = [(i + 1, i) for i in range(size - 1)]

    (sent,) = call(send_body, [((2, members, rim, width), BF16)], latent, send_rows)
    low = lax.ppermute(sent[0], "space", up)
    high = lax.ppermute(sent[1], "space", down)
    own, normed, proj = call(
        local_body,
        [((members, nodes, width), BF16), ((rows, width), BF16), ((rows, 3 * width), BF16)],
        latent, member_noise, w_noise, w_qkv,
        flops=2 * rows * width * 3 * width,
    )
    normed_rim, proj_rim, attended, stored, hidden, slope, forecast, table = call(
        forward_body,
        [
            ((rims, width), BF16), ((rims, 2 * width), BF16), ((rows, width), BF16),
            ((rows, width), BF16), ((members, width, points), BF16),
            ((members, width, points), BF16), ((members, channels, points), BF16),
            ((nodes, points), BF16),
        ],
        own, proj, low, high, member_noise, w_noise, w_qkv, w_out, w_hid, w_pred,
        neighbours, degree, dec_nodes,
        flops=3 * 10**9,
    )
    gathered = gather_members(forecast)
    packed_shape = (CHUNKS, 16, TILE * (SLOTS_A + SLOTS_B))
    first_shape = (CHUNKS, 16, TILE * SLOTS_A)
    core = lax.axis_index("core").astype(jnp.int32)[None]
    swap = [(0, 1), (1, 0)]
    normed_theirs = lax.ppermute(jnp.concatenate([normed, normed_rim], axis=0), "core", swap)
    live_count = lax.dynamic_slice_in_dim(counts, lax.axis_index("space"), 1)
    d_updated, d_attended, keep, send, loss = call(
        crps_body,
        [
            ((rows, width), BF16), ((rows, width), BF16), (first_shape, BF16),
            (first_shape, BF16), ((16, TILE), BF16),
        ],
        core, live_count, forecast, *gathered, targets, hidden, slope, table, stored, attended,
        w_out, w_hid, w_pred,
        smem=(0, 1),
        scratch=[
            pltpu.VMEM((members, width, points), BF16),
            pltpu.VMEM((members, channels, points), BF16),
            pltpu.VMEM((2,) + first_shape, BF16),
        ],
        flops=6 * 10**9,
    )
    came = lax.ppermute(send, "core", swap)
    d_proj, d_rim, d_send = call(
        attend_back_body,
        [
            ((2, rows, 3 * width // 2), BF16), ((2, rims, width), BF16),
            ((rows + rims, 3 * width // 2), BF16),
        ],
        core, proj, proj_rim, neighbours, degree, d_attended,
        smem=(0,),
        scratch=[pltpu.VMEM((nodes + 2 * rim, nodes), F32)],
        flops=2 * 10**9,
    )
    d_theirs = lax.ppermute(d_send, "core", swap)
    d_own, d_low, d_high, g_noise = call(
        norm_back_body,
        [
            ((members, width, nodes), F32), ((members, rim, width), BF16),
            ((members, rim, width), BF16), ((32, width), BF16),
        ],
        own, low, high, member_noise, w_noise, w_qkv, d_proj, d_rim, d_updated,
        flops=2 * 10**9,
    )
    (packed,) = call(
        pack_body,
        [(packed_shape, BF16)],
        core, normed, normed_rim, normed_theirs, d_proj, d_rim, d_theirs, keep, came, g_noise,
        loss,
        smem=(0,),
        scratch=[pltpu.VMEM((width, 3 * width // 2), BF16)],
        flops=2 * 10**9,
    )
    chips = ("space", "zhi")
    count = lax.axis_size(chips)
    from_next = lax.ppermute(d_low, "space", down)
    from_prev = lax.ppermute(d_high, "space", up)
    packed, from_next, from_prev = lax.optimization_barrier((packed, from_next, from_prev))
    parts = lax.all_to_all(packed, chips, 0, 0, tiled=True)
    (spread,) = call(
        sum_body,
        [((count, CHUNKS // count) + packed_shape[1:], BF16)],
        parts.reshape((count, CHUNKS // count) + packed_shape[1:]),
    )
    half = lax.all_to_all(spread.reshape(packed_shape), chips, 0, 0, tiled=True)
    other = lax.ppermute(half, "core", swap)
    (d_latent,) = call(
        join_body, [((members, width, nodes), F32)], d_own, send_rows, from_next, from_prev
    )
    mine = unpack(core, half, width, channels)
    g_qkv, g_out, g_hid, g_pred, g_noise, loss = unpack(1 - core, other, width, channels, mine)
    mean = loss[0, 0] / (channels * jnp.sum(counts).astype(F32))
    return mean, d_latent, g_qkv, g_out, g_noise, g_hid, g_pred


def gather_members(forecast):
    swap = [(0, 1), (1, 0)]
    far = lax.ppermute(forecast, "zhi", swap)
    near = lax.ppermute(forecast, "core", swap)
    return near, far, lax.ppermute(far, "core", swap)


def solution(mesh):
    space = mesh.shape["space"]
    mesh = jax.sharding.Mesh(mesh.devices.reshape(space, 2, 2), ("space", "zhi", "core"))
    member = ("zhi", "core")
    in_specs = (
        P(member, None, "space"), P(None, "space"), P(None, "space"), P("space"),
        P(None, "space"), P(), P(None, "space"), P(member, None), P(), P(), P(), P(), P(),
    )
    out_specs = (P(), P(member, None, "space"), P(), P(), P(), P(), P())
    return jax.shard_map(
        on_device, mesh=mesh, in_specs=in_specs, out_specs=out_specs, check_vma=False
    )
```

```python
import jax
import jax.numpy as jnp
from jax import lax
from jax.experimental import pallas as pl
from jax.experimental.pallas import tpu as pltpu
from jax.sharding import PartitionSpec as P

HEADS = 6
HEAD = 128
TILE = 128
GROUPS = 16
SPACE = ("x", "zlo", "y")
HALF = 768
SLOTS_A = 5
SLOTS_B = 7
CHUNKS = 4 * GROUPS
EPS = 1e-5
F32 = jnp.float32
BF16 = jnp.bfloat16
NN = (((1,), (0,)), ((), ()))
NT = (((1,), (1,)), ((), ()))
TN = (((0,), (0,)), ((), ()))
VMEM = pl.BlockSpec(memory_space=pltpu.VMEM)
SMEM = pl.BlockSpec(memory_space=pltpu.SMEM)
MIB = 1024 * 1024


def mm(a, b, dims=NN):
    return lax.dot_general(a, b, dims, preferred_element_type=F32)


def call(body, out_shape, *args, smem=(), flops=0, scratch=(), vmem=16):
    out_shape = [jax.ShapeDtypeStruct(s, d) for s, d in out_shape]
    size = sum(a.size * a.dtype.itemsize for a in args)
    size += sum(o.size * o.dtype.itemsize for o in out_shape)
    return pl.pallas_call(
        body,
        out_shape=out_shape,
        in_specs=[SMEM if i in smem else VMEM for i in range(len(args))],
        out_specs=[VMEM] * len(out_shape),
        scratch_shapes=list(scratch),
        compiler_params=pltpu.CompilerParams(vmem_limit_bytes=vmem * MIB),
        cost_estimate=pl.CostEstimate(flops=flops, bytes_accessed=size, transcendentals=0),
    )(*args)


def gains(noise, w_noise):
    return 1.0 + lax.dot_general(
        noise, w_noise, NN, precision=lax.Precision.HIGHEST, preferred_element_type=F32
    )


def normalise(rows):
    centre = rows - jnp.mean(rows, axis=1, keepdims=True)
    inverse = lax.rsqrt(jnp.mean(centre * centre, axis=1, keepdims=True) + EPS)
    return centre * inverse, inverse


def norm_back(cotangent, gain, hat, inverse):
    d_hat = cotangent * gain
    mean = jnp.mean(d_hat, axis=1, keepdims=True)
    along = jnp.mean(d_hat * hat, axis=1, keepdims=True)
    return inverse * (d_hat - mean - hat * along)


def depth_here():
    return 2 * lax.axis_index("zhi") + lax.axis_index("zlo")


def send_body(latent, rows, sent_up, sent_down):
    nodes = latent.shape[2]
    rim = rows.shape[1]
    both = jnp.concatenate([rows[0:1, :], rows[1:2, :]], axis=1)
    table = lax.broadcasted_iota(jnp.int32, (nodes, 2 * rim), 0) == both
    table = table.astype(F32).T.astype(BF16)
    for m in range(latent.shape[0]):
        picked = mm(table, latent[m], NT).astype(BF16)
        sent_up[m] = picked[:rim]
        sent_down[m] = picked[rim:]


def local_body(latent, noise, w_noise, w_qkv, own, normed, proj):
    gain = gains(noise[...], w_noise[...])
    members, _, nodes = latent.shape
    for m in range(members):
        rows = latent[m].astype(F32).T
        own[m] = rows.astype(BF16)
        hat, _ = normalise(rows)
        normed[m * nodes : (m + 1) * nodes] = (hat * gain[m : m + 1]).astype(BF16)
    proj[...] = mm(normed[...], w_qkv[...]).astype(BF16)


def slot_mask(nbr, degree, rows):
    slots, nodes = nbr.shape
    index = lax.broadcasted_iota(jnp.int32, (rows, nodes), 0)
    total = jnp.zeros((rows, nodes), F32)
    for j in range(slots):
        live = (index == nbr[j : j + 1, :]) & (degree[...] > j)
        total = total + live.astype(F32)
    return total / degree[...].astype(F32)


def point_table(dec_nodes, nodes):
    points = dec_nodes.shape[1]
    index = lax.broadcasted_iota(jnp.int32, (nodes, points), 0)
    total = jnp.zeros((nodes, points), F32)
    for j in range(dec_nodes.shape[0]):
        total = total + (index == dec_nodes[j : j + 1, :]).astype(F32)
    return total.astype(BF16)


def extend(own, low, high):
    return jnp.concatenate([low, own, high], axis=0)


def forward_body(
    own, normed, proj, low, high, noise, w_noise, w_qkv, w_out, w_hid, w_pred, nbr, degree,
    dec_nodes,
    normed_all, proj_rim, attended, stored, hidden, slope, forecast, table,
):
    members, nodes, width = own.shape
    rim = low.shape[1]
    gain = gains(noise[...], w_noise[...])
    for m in range(members):
        rows = jnp.concatenate([low[m], high[m]], axis=0).astype(F32)
        hat, _ = normalise(rows)
        at = members * nodes + 2 * rim * m
        normed_all[at : at + 2 * rim] = (hat * gain[m : m + 1]).astype(BF16)
    normed_all[: members * nodes] = normed[...]
    proj_rim[...] = mm(normed_all[members * nodes :], w_qkv[:, width:]).astype(BF16)
    mask = slot_mask(nbr, degree, nodes + 2 * rim)
    for m in range(members):
        here = slice(m * nodes, (m + 1) * nodes)
        lo = slice(2 * rim * m, 2 * rim * m + rim)
        hi = slice(2 * rim * m + rim, 2 * rim * (m + 1))
        for h in range(HEADS):
            at = [slice(k * width + h * HEAD, k * width + (h + 1) * HEAD) for k in range(3)]
            rim_at = [slice(a.start - width, a.stop - width) for a in at]
            key = extend(proj[here, at[1]], proj_rim[lo, rim_at[1]], proj_rim[hi, rim_at[1]])
            value = extend(proj[here, at[2]], proj_rim[lo, rim_at[2]], proj_rim[hi, rim_at[2]])
            score = mm(key, proj[here, at[0]], NT) * HEAD**-0.5
            weight = (jax.nn.sigmoid(score) * mask).astype(BF16)
            attended[here, at[0]] = mm(weight, value, TN).astype(BF16)
    branch = mm(attended[...], w_out[...])
    for m in range(members):
        here = slice(m * nodes, (m + 1) * nodes)
        stored[here] = (own[m].astype(F32) + branch[here]).astype(BF16)
    table[...] = point_table(dec_nodes, nodes)
    mixed = mm(stored[...], w_hid[...]).astype(BF16)
    block = 256
    for m in range(members):
        part = mixed[m * nodes : (m + 1) * nodes]
        for g in range(0, dec_nodes.shape[1], block):
            pre = mm(part, table[:, g : g + block], TN) * (1.0 / 3.0)
            sig = 0.5 * jnp.tanh(0.5 * pre) + 0.5
            hid = pre * sig
            hidden[m, :, g : g + block] = hid.astype(BF16)
            slope[m, :, g : g + block] = (sig + hid * (1.0 - sig)).astype(BF16)
            forecast[m, :, g : g + block] = mm(
                w_pred[...], hidden[m, :, g : g + block]
            ).astype(BF16)


def smooth(v):
    square = v * v + 0.25
    inverse = lax.rsqrt(square)
    return square * inverse - 0.5, v * inverse


def crps_body(
    counts, mine, *rest
):
    (*others, targets, hidden, slope, table, stored, attended, w_out, w_hid, w_pred,
     d_updated, d_attended, keep, send, loss, d_pre, d_cast, halves) = rest
    live_count = counts[lax.axis_index(SPACE)]
    core = lax.axis_index("core")
    members, channels, points = mine.shape
    total = members * (1 + len(others))
    block = 256
    nodes = table.shape[0]
    scale = 0.5 / (total * (total - 1))
    losses = []
    for g in range(0, points, block):
        at = slice(g, g + block)
        live = lax.broadcasted_iota(jnp.int32, (1, block), 1) + g < live_count
        live = live.astype(F32)
        own = [mine[m, :, at].astype(F32) for m in range(members)]
        aim = targets[:, at]
        near = jnp.zeros((channels, block), F32)
        far = jnp.zeros((channels, block), F32)
        slopes = []
        for m in range(members):
            value, grad = smooth(own[m] - aim)
            near = near + value
            slopes.append([grad, jnp.zeros((channels, block), F32)])
        for a in range(members):
            for b in range(a + 1, members):
                value, grad = smooth(own[a] - own[b])
                far = far + 2.0 * value
                slopes[a][1] = slopes[a][1] + grad
                slopes[b][1] = slopes[b][1] - grad
        for other in others:
            for k in range(members):
                theirs = other[k, :, at].astype(F32)
                for m in range(members):
                    value, grad = smooth(own[m] - theirs)
                    far = far + value
                    slopes[m][1] = slopes[m][1] + grad
        for m in range(members):
            grad = slopes[m][0] * (1.0 / total) - slopes[m][1] * (2.0 * scale)
            d_cast[m, :, at] = (grad * live).astype(BF16)
        column = jnp.sum(near * (1.0 / total) - far * scale, axis=0, keepdims=True) * live
        losses.append(column)
    for i in range(16):
        at = i % 2
        piece = losses[i // 2 % 4][:, TILE * at : TILE * (at + 1)]
        loss[i : i + 1] = piece.astype(BF16) if i < 8 else jnp.zeros((1, TILE), BF16)
    back = w_pred[...].astype(F32).T.astype(BF16)
    grad = jnp.zeros((channels, hidden.shape[1]), F32)
    for m in range(members):
        grad = grad + mm(d_cast[m], hidden[m], NT)
        for g in range(0, points, block):
            at = slice(g, g + block)
            d_hid = mm(back, d_cast[m, :, at])
            d_pre[m, :, at] = (d_hid * slope[m, :, at].astype(F32)).astype(BF16)
    g_pred = jnp.zeros((96 - channels, grad.shape[1]), F32)
    g_pred = jnp.concatenate([grad, g_pred], axis=0).astype(BF16)
    pooled = [
        (mm(table[...], d_pre[m], NT) * (1.0 / 3.0)).astype(BF16) for m in range(members)
    ]
    pooled = jnp.concatenate(pooled, axis=0)
    g_hid = mm(stored[...], pooled, TN).astype(BF16)
    d_updated[...] = mm(pooled, w_hid[...], NT).astype(BF16)
    g_out = mm(attended[...], d_updated[...], TN).astype(BF16)
    d_attended[...] = mm(d_updated[...], w_out[...], NT).astype(BF16)
    half = g_hid.shape[1] // 2
    for c in range(2):
        for k in range(GROUPS):
            for slot in range(SLOTS_A * 4):
                chunk, lane = 4 * k + slot // SLOTS_A, TILE * (slot % SLOTS_A)
                grad, row, column = tile_of_first(k, slot, (g_hid, g_out, g_pred))
                if grad is None:
                    piece = jnp.zeros((16, TILE), BF16)
                else:
                    column = c * half + TILE * column
                    piece = grad[16 * row : 16 * row + 16, column : column + TILE]
                halves[c, chunk, :, lane : lane + TILE] = piece
    keep[...] = halves[core]
    send[...] = halves[1 - core]


def tile_of_first(k, slot, grads):
    if slot < 18:
        part = slot % 9
        return grads[slot // 9], 3 * k + part // 3, part % 3
    tile = k + GROUPS * (slot - 18)
    if tile < 18:
        return grads[2], tile // 3, tile % 3
    return None, 0, 0


def attend_back_body(
    proj, proj_rim, nbr, degree, d_attended,
    d_proj, d_rim, send, mask,
):
    nodes = nbr.shape[1]
    members = proj.shape[0] // nodes
    width = HEADS * HEAD
    rim = proj_rim.shape[0] // (2 * members)
    per_half = HEADS // 2
    part = width // 2
    mask[...] = slot_mask(nbr, degree, nodes + 2 * rim)
    for m in range(members):
        here = slice(m * nodes, (m + 1) * nodes)
        lo = slice(2 * rim * m, 2 * rim * m + rim)
        hi = slice(2 * rim * m + rim, 2 * rim * (m + 1))
        for h in range(HEADS):
            at = [slice(k * width + h * HEAD, k * width + (h + 1) * HEAD) for k in range(3)]
            rim_at = [slice(a.start - width, a.stop - width) for a in at]
            query = proj[here, at[0]]
            key = extend(proj[here, at[1]], proj_rim[lo, rim_at[1]], proj_rim[hi, rim_at[1]])
            value = extend(proj[here, at[2]], proj_rim[lo, rim_at[2]], proj_rim[hi, rim_at[2]])
            out = d_attended[here, at[0]]
            sig = jax.nn.sigmoid(mm(key, query, NT) * HEAD**-0.5)
            weight = sig * mask[...]
            d_value = mm(weight.astype(BF16), out).astype(BF16)
            d_weight = mm(value, out, NT)
            d_score = (d_weight * weight * (1.0 - sig) * HEAD**-0.5).astype(BF16)
            d_key = mm(d_score, query).astype(BF16)
            c, j = h // per_half, h % per_half
            spot = [slice(k * part + j * HEAD, k * part + (j + 1) * HEAD) for k in range(3)]
            d_proj[c, here, spot[0]] = mm(d_score, key, TN).astype(BF16)
            for k, d in ((1, d_key), (2, d_value)):
                d_rim[c, lo, spot[k - 1]] = d[:rim]
                d_proj[c, here, spot[k]] = d[rim : rim + nodes]
                d_rim[c, hi, spot[k - 1]] = d[rim + nodes :]
    rows = members * nodes
    theirs = 1 - lax.axis_index("core")
    send[:rows] = d_proj[theirs]
    send[rows:, : 2 * part] = d_rim[theirs]
    send[rows:, 2 * part :] = jnp.zeros((2 * rim * members, part), BF16)


def norm_back_body(
    own, low, high, noise, w_noise, w_qkv, d_proj, d_rim, d_updated,
    d_own, d_low, d_high, g_noise,
):
    members, nodes, width = own.shape
    rim = low.shape[1]
    part = width // 2
    noises = noise[...]
    gain = gains(noises, w_noise[...])
    d_normed = jnp.zeros((members * nodes, width), F32)
    d_normed_rim = jnp.zeros((members * 2 * rim, width), F32)
    for c in range(2):
        for k in range(3):
            column = k * width + c * part
            weight = w_qkv[:, column : column + part]
            d_normed = d_normed + mm(d_proj[c, :, k * part : (k + 1) * part], weight, NT)
            if k:
                d_normed_rim = d_normed_rim + mm(
                    d_rim[c, :, (k - 1) * part : k * part], weight, NT
                )
    d_noise = jnp.zeros(g_noise.shape, F32)
    noise_columns = jnp.concatenate([noises] * (8 // members), axis=0).T
    for m in range(members):
        here = slice(m * nodes, (m + 1) * nodes)
        rims = slice(2 * rim * m, 2 * rim * (m + 1))
        hat, inverse = normalise(own[m].astype(F32))
        d_gain = jnp.sum(d_normed[here] * hat, axis=0, keepdims=True)
        rows = norm_back(d_normed[here], gain[m : m + 1], hat, inverse)
        d_own[m] = (rows + d_updated[here].astype(F32)).T
        hat, inverse = normalise(jnp.concatenate([low[m], high[m]], axis=0).astype(F32))
        d_gain = d_gain + jnp.sum(d_normed_rim[rims] * hat, axis=0, keepdims=True)
        rows = norm_back(d_normed_rim[rims], gain[m : m + 1], hat, inverse)
        d_low[m] = rows[:rim].astype(BF16)
        d_high[m] = rows[rim:].astype(BF16)
        d_noise = d_noise + noise_columns[:, m : m + 1] * d_gain
    g_noise[...] = d_noise.astype(BF16)


def pack_body(
    normed, normed_theirs, d_proj, d_rim, d_theirs, keep, came, g_noise, loss, plane, *rest
):
    *stacks, g_half, stack = rest
    core, depth = lax.axis_index("core"), depth_here()
    rows = d_proj.shape[1]
    wide = 2 * d_proj.shape[2] // 3
    width = normed.shape[1]
    mine = d_proj[core]
    rim = d_rim[core]
    for r in range(0, width, 256):
        at = slice(r, r + 256)
        total = mm(normed[:rows, at], mine, TN) + mm(normed_theirs[:rows, at], d_theirs[:rows], TN)
        g_half[at, : wide // 2] = total[:, : wide // 2].astype(BF16)
        edge = mm(normed[rows:, at], rim, TN)
        edge = edge + mm(normed_theirs[rows:, at], d_theirs[rows:, :wide], TN)
        g_half[at, wide // 2 :] = (total[:, wide // 2 :] + edge).astype(BF16)
    for k in range(GROUPS):
        for sub in range(4):
            level, spot = k // 4, 4 * (k % 4) + sub
            first = keep[4 * k + sub].astype(F32) + came[4 * k + sub].astype(F32)
            plane[spot, level, :, : TILE * SLOTS_A] = first.astype(BF16)
            for j in range(SLOTS_B):
                slot = SLOTS_B * sub + j
                if slot < 27:
                    row, column = 48 * k + 16 * (slot // 9), TILE * (slot % 9)
                    piece = g_half[row : row + 16, column : column + TILE]
                elif k < 12:
                    row, column = 16 * (k // 6), TILE * (k % 6)
                    piece = g_noise[row : row + 16, column : column + TILE]
                elif k == 12:
                    piece = loss[...]
                else:
                    piece = jnp.zeros((16, TILE), BF16)
                lane = TILE * (SLOTS_A + j)
                if lane < HALF:
                    plane[spot, level, :, lane : lane + TILE] = piece
                else:
                    stack[level, spot, :, lane - HALF : lane - HALF + TILE] = piece
    for shift in range(4):
        stacks[shift][...] = stack[lax.rem(depth + shift, 4)]


def first_sum_body(came, *rest):
    depth = depth_here()
    stacks, targets, (stack, column) = rest[:4], rest[4:8], rest[8:]
    for j in range(came.shape[1]):
        total = came[0, j].astype(F32)
        for i in range(1, came.shape[0]):
            total = total + came[i, j].astype(F32)
        column[:, j] = total.astype(BF16)
    for shift, target in enumerate(targets):
        target[...] = column[lax.rem(depth + shift, 4)]
    total = stacks[0][...].astype(F32)
    for part in stacks[1:]:
        total = total + part[...].astype(F32)
    stack[...] = total.astype(BF16)


def second_sum_body(one, two, three, four, came, column, spread):
    total = one[...].astype(F32) + two[...].astype(F32)
    total = total + three[...].astype(F32) + four[...].astype(F32)
    column[...] = total.astype(BF16)
    total = came[0].astype(F32)
    for i in range(1, came.shape[0]):
        total = total + came[i].astype(F32)
    total = total.astype(BF16)
    for i in range(came.shape[0]):
        spread[i] = total


def spread_body(one, two, three, four, spread, column):
    depth = depth_here()
    for shift, piece in enumerate((one, two, three, four)):
        column[lax.rem(depth + (4 - shift), 4)] = piece[...]
    for j in range(spread.shape[1]):
        total = column[:, j]
        for i in range(spread.shape[0]):
            spread[i, j] = total


def unpack_tiles(core, plane, stacks, targets, pred, noise, halves, sems):
    wide = halves[1].shape[1]
    depth = depth_here()
    copies = []
    total = None
    for step in range(4):
        level = lax.rem(depth + 4 - step, 4)
        here = plane.at[:, level]

        def tile(group, sub, j):
            lane, spot = TILE * j, 4 * group + sub
            if lane < HALF:
                return here[spot, :, lane : lane + TILE].astype(F32)
            return stacks[step][spot, :, lane - HALF : lane - HALF + TILE].astype(F32)

        def first(group, slot):
            return tile(group, slot // SLOTS_A, slot % SLOTS_A)

        def second(group, slot):
            return tile(group, slot // SLOTS_B, SLOTS_A + slot % SLOTS_B)

        base = 192 * step
        for group in range(4):
            for slot in range(27):
                row, column = base + 48 * group + 16 * (slot // 9), TILE * (slot % 9)
                halves[0][row : row + 16, column : column + TILE] = second(group, slot)
            for slot in range(18):
                row, column = base + 48 * group + 16 * (slot % 9 // 3), TILE * (slot % 3)
                halves[1 + slot // 9][row : row + 16, column : column + TILE] = first(group, slot)
            k = 4 * level + group
            for slot in (18, 19):
                index = k + GROUPS * (slot - 18)

                @pl.when(index < 18)
                def _():
                    row = pl.multiple_of(16 * lax.div(index, 3), 16)
                    column = pl.multiple_of(TILE * lax.rem(index, 3), TILE)
                    pred[pl.ds(row, 16), pl.ds(column, TILE)] = first(group, slot)

            spare = second(group, 27)

            @pl.when(k < 12)
            def _():
                row = pl.multiple_of(16 * lax.div(k, 6), 16)
                column = pl.multiple_of(TILE * lax.rem(k, 6), TILE)
                noise[pl.ds(row, 16), pl.ds(column, TILE)] = spare

            here_loss = jnp.where(k == 12, spare, 0.0)
            total = here_loss if total is None else total + here_loss
        rows = pl.ds(pl.multiple_of(192 * level, 16), 192)
        for target, half, sections in ((0, 0, 3), (1, 1, 1), (2, 2, 1)):
            for section in range(sections):
                start = pl.multiple_of(2 * wide * section + wide * core, TILE)
                copies.append(
                    pltpu.make_async_copy(
                        halves[half].at[base : base + 192, wide * section : wide * (section + 1)],
                        targets[target].at[rows, pl.ds(start, wide)],
                        sems.at[len(copies)],
                    )
                )
                copies[-1].start()
    return copies, jnp.sum(total, keepdims=True)


def unpack_mine_body(
    plane, one, two, three, four, g_qkv, g_hid, g_out, pred, noise, loss, *scratch
):
    *halves, sems = scratch
    copies, total = unpack_tiles(
        lax.axis_index("core"), plane, (one, two, three, four), (g_qkv, g_hid, g_out), pred, noise,
        halves, sems,
    )
    loss[...] = total
    for copy in copies:
        copy.wait()


def unpack_theirs_body(
    plane, one, two, three, four, counts, _qkv, _hid, _out, pred_mine, noise_mine, loss_mine,
    g_qkv, g_hid, g_out, g_pred, noise, mean, *scratch
):
    *halves, pred, sems = scratch
    mine = lax.axis_index("core")
    copies, total = unpack_tiles(
        1 - mine, plane, (one, two, three, four), (g_qkv, g_hid, g_out), pred, noise, halves, sems
    )
    noise[...] = noise[...] + noise_mine[...]
    channels, width = g_pred.shape
    wide = width // 2
    for c in range(2):
        own = pred_mine[:channels]
        g_pred[:, c * wide : (c + 1) * wide] = jnp.where(mine == c, own, pred[:channels])
    live = jnp.sum(counts[...].astype(F32), keepdims=True)
    mean[...] = (total + loss_mine[...]) / (channels * live)
    for copy in copies:
        copy.wait()


def unpack(plane, stacks, width, channels, counts=None, before=()):
    wide = width // 2
    big = ((width, 3 * width), (width, width), (width, width))
    small = ((channels, width) if before else (96, wide), (32, width), (1, 1))
    scratch = [pltpu.VMEM((width, n), F32) for n in (3 * wide, wide, wide)]
    if before:
        scratch.append(pltpu.VMEM((96, wide), F32))
    scratch.append(pltpu.SemaphoreType.DMA((20,)))
    anywhere = pl.BlockSpec(memory_space=pl.ANY)
    args = (plane, *stacks)
    if before:
        args += (counts, *before)
    return pl.pallas_call(
        unpack_theirs_body if before else unpack_mine_body,
        out_shape=[jax.ShapeDtypeStruct(shape, F32) for shape in big + small],
        in_specs=[anywhere if 6 <= i < 9 else VMEM for i in range(len(args))],
        out_specs=[anywhere] * 3 + [VMEM] * 3,
        scratch_shapes=scratch,
        input_output_aliases={6 + i: i for i in range(3)} if before else {},
        compiler_params=pltpu.CompilerParams(vmem_limit_bytes=20 * MIB),
        cost_estimate=pl.CostEstimate(flops=0, bytes_accessed=9 * 10**6, transcendentals=0),
    )(*args)


def join_body(d_own, rows, from_next, from_prev, d_latent):
    nodes = d_own.shape[2]
    rim = rows.shape[1]
    index = lax.broadcasted_iota(jnp.int32, (nodes, 2 * rim), 0)
    both = jnp.concatenate([rows[0:1, :], rows[1:2, :]], axis=1)
    table = (index == both).astype(F32).T.astype(BF16)
    for m in range(d_own.shape[0]):
        back = jnp.concatenate([from_next[m], from_prev[m]], axis=0)
        d_latent[m] = d_own[m] + mm(back, table, TN)


def on_device(
    latent, send_rows, neighbours, degree, dec_nodes, counts, targets, member_noise,
    w_qkv, w_out, w_noise, w_hid, w_pred,
):
    members, width, nodes = latent.shape
    rim = send_rows.shape[1]
    points = dec_nodes.shape[1]
    channels = targets.shape[0]
    rows = members * nodes
    rims = members * 2 * rim
    degree = degree[None, :]
    size = lax.axis_size(SPACE)
    up = [(i, i + 1) for i in range(size - 1)]
    down = [(i + 1, i) for i in range(size - 1)]

    sent_up, sent_down = call(
        send_body, [((members, rim, width), BF16)] * 2, latent, send_rows
    )
    low = lax.ppermute(sent_up, SPACE, up)
    high = lax.ppermute(sent_down, SPACE, down)
    own, normed, proj = call(
        local_body,
        [((members, nodes, width), BF16), ((rows, width), BF16), ((rows, 3 * width), BF16)],
        latent, member_noise, w_noise, w_qkv,
        flops=2 * rows * width * 3 * width,
    )
    normed_all, proj_rim, attended, stored, hidden, slope, forecast, table = call(
        forward_body,
        [
            ((rows + rims, width), BF16), ((rims, 2 * width), BF16), ((rows, width), BF16),
            ((rows, width), BF16), ((members, width, points), BF16),
            ((members, width, points), BF16), ((members, channels, points), BF16),
            ((nodes, points), BF16),
        ],
        own, normed, proj, low, high, member_noise, w_noise, w_qkv, w_out, w_hid, w_pred,
        neighbours, degree, dec_nodes,
        flops=3 * 10**9,
    )
    gathered = gather_members(forecast)
    packed_shape = (CHUNKS, 16, TILE * (SLOTS_A + SLOTS_B))
    first_shape = (CHUNKS, 16, TILE * SLOTS_A)
    swap = [(0, 1), (1, 0)]
    normed_theirs = lax.ppermute(normed_all, "core", swap)
    d_updated, d_attended, keep, send, loss = call(
        crps_body,
        [
            ((rows, width), BF16), ((rows, width), BF16), (first_shape, BF16),
            (first_shape, BF16), ((16, TILE), BF16),
        ],
        counts, forecast, *gathered, targets, hidden, slope, table, stored, attended,
        w_out, w_hid, w_pred,
        smem=(0,),
        scratch=[
            pltpu.VMEM((members, width, points), BF16),
            pltpu.VMEM((members, channels, points), BF16),
            pltpu.VMEM((2,) + first_shape, BF16),
        ],
        flops=6 * 10**9,
    )
    came = lax.ppermute(send, "core", swap)
    d_proj, d_rim, d_send = call(
        attend_back_body,
        [
            ((2, rows, 3 * width // 2), BF16), ((2, rims, width), BF16),
            ((rows + rims, 3 * width // 2), BF16),
        ],
        proj, proj_rim, neighbours, degree, d_attended,
        scratch=[pltpu.VMEM((nodes + 2 * rim, nodes), F32)],
        flops=2 * 10**9,
    )
    d_theirs = lax.ppermute(d_send, "core", swap)
    d_own, d_low, d_high, g_noise = call(
        norm_back_body,
        [
            ((members, width, nodes), F32), ((members, rim, width), BF16),
            ((members, rim, width), BF16), ((32, width), BF16),
        ],
        own, low, high, member_noise, w_noise, w_qkv, d_proj, d_rim, d_updated,
        flops=2 * 10**9,
    )
    planes, levels = ("x", "y"), ("zlo", "zhi")
    spots = lax.axis_size(planes)
    tile = (16, HALF)
    chunk = (16 // spots,) + tile
    ring = [2 * (z % 2) + z // 2 for z in range(4)]

    def shifted(pieces):
        moved = []
        for shift, piece in enumerate(pieces, 1):
            pairs = [(ring[z], ring[(z + shift) % 4]) for z in range(4)]
            moved.append(lax.ppermute(piece, levels, pairs))
        return moved

    def swapped(a):
        return lax.all_to_all(a, planes, 0, 0, tiled=True)

    plane, *stacks = call(
        pack_body,
        [((16, 4) + tile, BF16)] + [((16,) + tile, BF16)] * 4,
        normed_all, normed_theirs, d_proj, d_rim, d_theirs, keep, came, g_noise, loss,
        scratch=[
            pltpu.VMEM((width, 3 * width // 2), BF16), pltpu.VMEM((4, 16) + tile, BF16),
        ],
        flops=2 * 10**9,
    )
    from_next = lax.ppermute(d_low, SPACE, down)
    from_prev = lax.ppermute(d_high, SPACE, up)
    plane, from_next, from_prev = lax.optimization_barrier((plane, from_next, from_prev))
    stacks = [stacks[0]] + shifted(stacks[1:])
    plane = swapped(plane)
    *columns, stack = call(
        first_sum_body,
        [(chunk, BF16)] * 4 + [((16,) + tile, BF16)],
        plane.reshape((spots, 16 // spots, 4) + tile), *stacks,
        scratch=[pltpu.VMEM((4,) + chunk, BF16)],
    )
    columns = [columns[0]] + shifted(columns[1:])
    stack = swapped(stack)
    column, stack = call(
        second_sum_body,
        [(chunk, BF16), ((spots,) + chunk, BF16)],
        *columns, stack.reshape((spots,) + chunk),
    )
    columns = [column] + shifted([column] * 3)
    stack = swapped(stack.reshape((16,) + tile))
    (plane,) = call(
        spread_body, [((spots, 16 // spots, 4) + tile, BF16)], *columns,
        scratch=[pltpu.VMEM((4,) + chunk, BF16)],
    )
    stacks = [stack] + shifted([stack] * 3)
    plane = swapped(plane.reshape((16, 4) + tile))
    other_stacks = [lax.ppermute(a, "core", swap) for a in stacks]
    other_plane = lax.ppermute(plane, "core", swap)
    (d_latent,) = call(
        join_body, [((members, width, nodes), F32)], d_own, send_rows, from_next, from_prev
    )
    mine = unpack(plane, stacks, width, channels)
    g_qkv, g_hid, g_out, g_pred, g_noise, mean = unpack(
        other_plane, other_stacks, width, channels, counts[None, :], mine
    )
    return mean.reshape(()), d_latent, g_qkv, g_out, g_noise, g_hid, g_pred


def gather_members(forecast):
    swap = [(0, 1), (1, 0)]
    far = lax.ppermute(forecast, "zhi", swap)
    near = lax.ppermute(forecast, "core", swap)
    return near, far, lax.ppermute(far, "core", swap)


def solution(mesh):
    axes = ("x", "zlo", "y", "zhi", "core")
    side = 4 if mesh.shape["space"] == 32 else 1
    mesh = jax.sharding.Mesh(mesh.devices.reshape(side, 2, side, 2, 2), axes)
    member, space = ("zhi", "core"), SPACE
    in_specs = (
        P(member, None, space), P(None, space), P(None, space), P(space),
        P(None, space), P(), P(None, space), P(member, None), P(), P(), P(), P(), P(),
    )
    out_specs = (P(), P(member, None, space), P(), P(), P(), P(), P())
    return jax.shard_map(
        on_device, mesh=mesh, in_specs=in_specs, out_specs=out_specs, check_vma=False
    )
```

```python
import functools

import jax
import jax.numpy as jnp
from jax import lax
from jax.experimental import pallas as pl
from jax.experimental.pallas import tpu as pltpu
from jax.sharding import PartitionSpec as P

HEADS = 6
HEAD = 128
TILE = 128
GROUPS = 16
SPACE = ("x", "zlo", "y")
SPLIT = 896
REST = 1536 - SPLIT
SLOTS_A = 5
SLOTS_B = 7
CHUNKS = 4 * GROUPS
EPS = 1e-5
F32 = jnp.float32
BF16 = jnp.bfloat16
NN = (((1,), (0,)), ((), ()))
NT = (((1,), (1,)), ((), ()))
TN = (((0,), (0,)), ((), ()))
VMEM = pl.BlockSpec(memory_space=pltpu.VMEM)
SMEM = pl.BlockSpec(memory_space=pltpu.SMEM)
APART = pl.BlockSpec(memory_space=pltpu.HBM)
MIB = 1024 * 1024


def mm(a, b, dims=NN):
    return lax.dot_general(a, b, dims, preferred_element_type=F32)


def call(body, out_shape, *args, smem=(), apart=(), far=(), flops=0, scratch=(), vmem=16):
    out_shape = [
        pltpu.HBM(s, d) if i in far else jax.ShapeDtypeStruct(s, d)
        for i, (s, d) in enumerate(out_shape)
    ]
    size = sum(a.size * a.dtype.itemsize for a in args)
    args = [
        pltpu.with_memory_space_constraint(a, pltpu.HBM) if i in apart else a
        for i, a in enumerate(args)
    ]
    return pl.pallas_call(
        body,
        out_shape=out_shape,
        in_specs=[
            SMEM if i in smem else APART if i in apart else VMEM for i in range(len(args))
        ],
        out_specs=[APART if i in far else VMEM for i in range(len(out_shape))],
        scratch_shapes=list(scratch),
        compiler_params=pltpu.CompilerParams(vmem_limit_bytes=vmem * MIB),
        cost_estimate=pl.CostEstimate(flops=flops, bytes_accessed=size, transcendentals=0),
    )(*args)


def gains(noise, w_noise):
    return 1.0 + lax.dot_general(
        noise, w_noise, NN, precision=lax.Precision.HIGHEST, preferred_element_type=F32
    )


def normalise(rows):
    centre = rows - jnp.mean(rows, axis=1, keepdims=True)
    inverse = lax.rsqrt(jnp.mean(centre * centre, axis=1, keepdims=True) + EPS)
    return centre * inverse, inverse


def norm_back(cotangent, gain, hat, inverse):
    d_hat = cotangent * gain
    mean = jnp.mean(d_hat, axis=1, keepdims=True)
    along = jnp.mean(d_hat * hat, axis=1, keepdims=True)
    return inverse * (d_hat - mean - hat * along)


def depth_here():
    return 2 * lax.axis_index("zhi") + lax.axis_index("zlo")


def send_body(latent_far, rows_far, sent_up, sent_down, latent, rows, sems):
    for copy in fetch((latent_far, rows_far), (latent, rows), sems):
        copy.wait()
    nodes = latent.shape[2]
    rim = rows.shape[1]
    both = jnp.concatenate([rows[0:1, :], rows[1:2, :]], axis=1)
    table = lax.broadcasted_iota(jnp.int32, (nodes, 2 * rim), 0) == both
    table = table.astype(F32).T.astype(BF16)
    for m in range(latent.shape[0]):
        picked = mm(table, latent[m], NT).astype(BF16)
        sent_up[m] = picked[:rim]
        sent_down[m] = picked[rim:]


def fetch(sources, targets, sems):
    copies = [
        pltpu.make_async_copy(a, b, sems.at[i]) for i, (a, b) in enumerate(zip(sources, targets))
    ]
    for copy in copies:
        copy.start()
    return copies


def local_body(
    latent_far, noise_far, w_noise_far, w_qkv, own, normed, proj,
    latent, noise, w_noise, held, total, sems,
):
    thirds = [slice(r, r + 256) for r in range(0, held.shape[0], 256)]
    copies = fetch(
        [latent_far, noise_far, w_noise_far] + [w_qkv.at[r] for r in thirds],
        [latent, noise, w_noise] + [held.at[r] for r in thirds],
        sems,
    )
    for copy in copies[:3]:
        copy.wait()
    copies = copies[3:]
    gain = gains(noise[...], w_noise[...])
    members, _, nodes = latent.shape
    for m in range(members):
        rows = latent[m].astype(F32).T
        own[m] = rows.astype(BF16)
        hat, _ = normalise(rows)
        normed[m * nodes : (m + 1) * nodes] = (hat * gain[m : m + 1]).astype(BF16)
    for i, r in enumerate(thirds):
        copies[i].wait()
        part = mm(normed[:, r], held[r])
        if i == 0:
            total[...] = part
        elif i < len(thirds) - 1:
            total[...] = total[...] + part
        else:
            proj[...] = (total[...] + part).astype(BF16)


def slot_mask(nbr, degree, rows):
    slots, nodes = nbr.shape
    index = lax.broadcasted_iota(jnp.int32, (rows, nodes), 0)
    total = jnp.zeros((rows, nodes), F32)
    for j in range(slots):
        live = (index == nbr[j : j + 1, :]) & (degree[...] > j)
        total = total + live.astype(F32)
    return total / degree[...].astype(F32)


def point_table(dec_nodes, nodes):
    points = dec_nodes.shape[1]
    index = lax.broadcasted_iota(jnp.int32, (nodes, points), 0)
    total = jnp.zeros((nodes, points), F32)
    for j in range(dec_nodes.shape[0]):
        total = total + (index == dec_nodes[j : j + 1, :]).astype(F32)
    return total.astype(BF16)


def extend(own, low, high):
    return jnp.concatenate([low, own, high], axis=0)


def forward_body(
    own, normed, proj, low, high, noise, w_noise, w_qkv, w_out, w_hid, w_pred, nbr, degree,
    dec_nodes,
    normed_all, proj_rim, attended, stored, hidden, slope, forecast, table,
    held_qkv, held_out, held_hid, sems,
):
    wide = own.shape[2]
    copies = fetch(
        (w_qkv.at[:, wide:], w_out, w_hid), (held_qkv, held_out, held_hid), sems
    )
    members, nodes, width = own.shape
    rim = low.shape[1]
    gain = gains(noise[...], w_noise[...])
    for m in range(members):
        rows = jnp.concatenate([low[m], high[m]], axis=0).astype(F32)
        hat, _ = normalise(rows)
        at = members * nodes + 2 * rim * m
        normed_all[at : at + 2 * rim] = (hat * gain[m : m + 1]).astype(BF16)
    normed_all[: members * nodes] = normed[...]
    copies[0].wait()
    proj_rim[...] = mm(normed_all[members * nodes :], held_qkv[...]).astype(BF16)
    mask = slot_mask(nbr, degree, nodes + 2 * rim)
    for m in range(members):
        here = slice(m * nodes, (m + 1) * nodes)
        lo = slice(2 * rim * m, 2 * rim * m + rim)
        hi = slice(2 * rim * m + rim, 2 * rim * (m + 1))
        for h in range(HEADS):
            at = [slice(k * width + h * HEAD, k * width + (h + 1) * HEAD) for k in range(3)]
            rim_at = [slice(a.start - width, a.stop - width) for a in at]
            key = extend(proj[here, at[1]], proj_rim[lo, rim_at[1]], proj_rim[hi, rim_at[1]])
            value = extend(proj[here, at[2]], proj_rim[lo, rim_at[2]], proj_rim[hi, rim_at[2]])
            score = mm(key, proj[here, at[0]], NT) * HEAD**-0.5
            weight = (jax.nn.sigmoid(score) * mask).astype(BF16)
            attended[here, at[0]] = mm(weight, value, TN).astype(BF16)
    copies[1].wait()
    branch = mm(attended[...], held_out[...])
    for m in range(members):
        here = slice(m * nodes, (m + 1) * nodes)
        stored[here] = (own[m].astype(F32) + branch[here]).astype(BF16)
    table[...] = point_table(dec_nodes, nodes)
    copies[2].wait()
    mixed = mm(stored[...], held_hid[...]).astype(BF16)
    block = 256
    for m in range(members):
        part = mixed[m * nodes : (m + 1) * nodes]
        for g in range(0, dec_nodes.shape[1], block):
            pre = mm(part, table[:, g : g + block], TN) * (1.0 / 3.0)
            sig = 0.5 * jnp.tanh(0.5 * pre) + 0.5
            hid = pre * sig
            hidden[m, :, g : g + block] = hid.astype(BF16)
            slope[m, :, g : g + block] = (sig + hid * (1.0 - sig)).astype(BF16)
            forecast[m, :, g : g + block] = mm(
                w_pred[...], hidden[m, :, g : g + block]
            ).astype(BF16)


def smooth(v):
    square = v * v + 0.25
    inverse = lax.rsqrt(square)
    return square * inverse - 0.5, v * inverse


def crps_body(
    counts, mine, *rest
):
    (*others, targets, hidden, slope, table, stored, attended, w_out, w_hid, w_pred,
     d_updated, d_attended, keep, send, loss, d_pre, d_cast, halves) = rest
    live_count = counts[lax.axis_index(SPACE)]
    core = lax.axis_index("core")
    members, channels, points = mine.shape
    total = members * (1 + len(others))
    block = 256
    nodes = table.shape[0]
    scale = 0.5 / (total * (total - 1))
    losses = []
    for g in range(0, points, block):
        at = slice(g, g + block)
        live = lax.broadcasted_iota(jnp.int32, (1, block), 1) + g < live_count
        live = live.astype(F32)
        own = [mine[m, :, at].astype(F32) for m in range(members)]
        aim = targets[:, at]
        near = jnp.zeros((channels, block), F32)
        far = jnp.zeros((channels, block), F32)
        slopes = []
        for m in range(members):
            value, grad = smooth(own[m] - aim)
            near = near + value
            slopes.append([grad, jnp.zeros((channels, block), F32)])
        for a in range(members):
            for b in range(a + 1, members):
                value, grad = smooth(own[a] - own[b])
                far = far + 2.0 * value
                slopes[a][1] = slopes[a][1] + grad
                slopes[b][1] = slopes[b][1] - grad
        for other in others:
            for k in range(members):
                theirs = other[k, :, at].astype(F32)
                for m in range(members):
                    value, grad = smooth(own[m] - theirs)
                    far = far + value
                    slopes[m][1] = slopes[m][1] + grad
        for m in range(members):
            grad = slopes[m][0] * (1.0 / total) - slopes[m][1] * (2.0 * scale)
            d_cast[m, :, at] = (grad * live).astype(BF16)
        column = jnp.sum(near * (1.0 / total) - far * scale, axis=0, keepdims=True) * live
        losses.append(column)
    for i in range(16):
        at = i % 2
        piece = losses[i // 2 % 4][:, TILE * at : TILE * (at + 1)]
        loss[i : i + 1] = piece.astype(BF16) if i < 8 else jnp.zeros((1, TILE), BF16)
    back = w_pred[...].astype(F32).T.astype(BF16)
    grad = jnp.zeros((channels, hidden.shape[1]), F32)
    for m in range(members):
        grad = grad + mm(d_cast[m], hidden[m], NT)
        for g in range(0, points, block):
            at = slice(g, g + block)
            d_hid = mm(back, d_cast[m, :, at])
            d_pre[m, :, at] = (d_hid * slope[m, :, at].astype(F32)).astype(BF16)
    g_pred = jnp.zeros((96 - channels, grad.shape[1]), F32)
    g_pred = jnp.concatenate([grad, g_pred], axis=0).astype(BF16)
    pooled = [
        (mm(table[...], d_pre[m], NT) * (1.0 / 3.0)).astype(BF16) for m in range(members)
    ]
    pooled = jnp.concatenate(pooled, axis=0)
    g_hid = mm(stored[...], pooled, TN).astype(BF16)
    d_updated[...] = mm(pooled, w_hid[...], NT).astype(BF16)
    g_out = mm(attended[...], d_updated[...], TN).astype(BF16)
    d_attended[...] = mm(d_updated[...], w_out[...], NT).astype(BF16)
    half = g_hid.shape[1] // 2
    for c in range(2):
        for k in range(GROUPS):
            for slot in range(SLOTS_A * 4):
                chunk, lane = 4 * k + slot // SLOTS_A, TILE * (slot % SLOTS_A)
                grad, row, column = tile_of_first(k, slot, (g_hid, g_out, g_pred))
                if grad is None:
                    piece = jnp.zeros((16, TILE), BF16)
                else:
                    column = c * half + TILE * column
                    piece = grad[16 * row : 16 * row + 16, column : column + TILE]
                halves[c, chunk, :, lane : lane + TILE] = piece
    keep[...] = halves[core]
    send[...] = halves[1 - core]


def tile_of_first(k, slot, grads):
    if slot < 18:
        part = slot % 9
        return grads[slot // 9], 3 * k + part // 3, part % 3
    tile = k + GROUPS * (slot - 18)
    if tile < 18:
        return grads[2], tile // 3, tile % 3
    return None, 0, 0


def attend_back_body(
    proj, proj_rim, nbr, degree, d_attended,
    d_proj, d_rim, send, mask,
):
    nodes = nbr.shape[1]
    members = proj.shape[0] // nodes
    width = HEADS * HEAD
    rim = proj_rim.shape[0] // (2 * members)
    per_half = HEADS // 2
    part = width // 2
    mask[...] = slot_mask(nbr, degree, nodes + 2 * rim)
    for m in range(members):
        here = slice(m * nodes, (m + 1) * nodes)
        lo = slice(2 * rim * m, 2 * rim * m + rim)
        hi = slice(2 * rim * m + rim, 2 * rim * (m + 1))
        for h in range(HEADS):
            at = [slice(k * width + h * HEAD, k * width + (h + 1) * HEAD) for k in range(3)]
            rim_at = [slice(a.start - width, a.stop - width) for a in at]
            query = proj[here, at[0]]
            key = extend(proj[here, at[1]], proj_rim[lo, rim_at[1]], proj_rim[hi, rim_at[1]])
            value = extend(proj[here, at[2]], proj_rim[lo, rim_at[2]], proj_rim[hi, rim_at[2]])
            out = d_attended[here, at[0]]
            sig = jax.nn.sigmoid(mm(key, query, NT) * HEAD**-0.5)
            weight = sig * mask[...]
            d_value = mm(weight.astype(BF16), out).astype(BF16)
            d_weight = mm(value, out, NT)
            d_score = (d_weight * weight * (1.0 - sig) * HEAD**-0.5).astype(BF16)
            d_key = mm(d_score, query).astype(BF16)
            c, j = h // per_half, h % per_half
            spot = [slice(k * part + j * HEAD, k * part + (j + 1) * HEAD) for k in range(3)]
            d_proj[c, here, spot[0]] = mm(d_score, key, TN).astype(BF16)
            for k, d in ((1, d_key), (2, d_value)):
                d_rim[c, lo, spot[k - 1]] = d[:rim]
                d_proj[c, here, spot[k]] = d[rim : rim + nodes]
                d_rim[c, hi, spot[k - 1]] = d[rim + nodes :]
    rows = members * nodes
    theirs = 1 - lax.axis_index("core")
    send[:rows] = d_proj[theirs]
    send[rows:, : 2 * part] = d_rim[theirs]
    send[rows:, 2 * part :] = jnp.zeros((2 * rim * members, part), BF16)


def norm_back_body(
    own, low, high, noise, w_noise, w_qkv, d_proj, d_rim, d_updated,
    d_own, d_low, d_high, g_noise,
):
    members, nodes, width = own.shape
    rim = low.shape[1]
    part = width // 2
    noises = noise[...]
    gain = gains(noises, w_noise[...])
    d_normed = jnp.zeros((members * nodes, width), F32)
    d_normed_rim = jnp.zeros((members * 2 * rim, width), F32)
    for c in range(2):
        for k in range(3):
            column = k * width + c * part
            weight = w_qkv[:, column : column + part]
            d_normed = d_normed + mm(d_proj[c, :, k * part : (k + 1) * part], weight, NT)
            if k:
                d_normed_rim = d_normed_rim + mm(
                    d_rim[c, :, (k - 1) * part : k * part], weight, NT
                )
    d_noise = jnp.zeros(g_noise.shape, F32)
    noise_columns = jnp.concatenate([noises] * (8 // members), axis=0).T
    for m in range(members):
        here = slice(m * nodes, (m + 1) * nodes)
        rims = slice(2 * rim * m, 2 * rim * (m + 1))
        hat, inverse = normalise(own[m].astype(F32))
        d_gain = jnp.sum(d_normed[here] * hat, axis=0, keepdims=True)
        rows = norm_back(d_normed[here], gain[m : m + 1], hat, inverse)
        d_own[m] = (rows + d_updated[here].astype(F32)).T
        hat, inverse = normalise(jnp.concatenate([low[m], high[m]], axis=0).astype(F32))
        d_gain = d_gain + jnp.sum(d_normed_rim[rims] * hat, axis=0, keepdims=True)
        rows = norm_back(d_normed_rim[rims], gain[m : m + 1], hat, inverse)
        d_low[m] = rows[:rim].astype(BF16)
        d_high[m] = rows[rim:].astype(BF16)
        d_noise = d_noise + noise_columns[:, m : m + 1] * d_gain
    g_noise[...] = d_noise.astype(BF16)


def pack_first_body(keep, came, *stacks):
    depth = depth_here()
    for shift, target in enumerate(stacks):
        level = lax.rem(depth + shift, 4)
        target[...] = (keep[level].astype(F32) + came[level].astype(F32)).astype(BF16)


def pack_body(
    normed, normed_theirs, d_proj, d_rim, d_theirs, g_noise, loss, plane_far, g_half, plane, sems
):
    copies = []
    core = lax.axis_index("core")
    rows = d_proj.shape[1]
    wide = 2 * d_proj.shape[2] // 3
    width = normed.shape[1]
    mine = d_proj[core]
    rim = d_rim[core]
    for r in range(0, width, 192):
        at = slice(r, r + 192)
        total = mm(normed[:rows, at], mine, TN) + mm(normed_theirs[:rows, at], d_theirs[:rows], TN)
        g_half[at, : wide // 2] = total[:, : wide // 2].astype(BF16)
        edge = mm(normed[rows:, at], rim, TN)
        edge = edge + mm(normed_theirs[rows:, at], d_theirs[rows:, :wide], TN)
        g_half[at, wide // 2 :] = (total[:, wide // 2 :] + edge).astype(BF16)
        level = r // 192
        for k in range(4 * level, 4 * level + 4):
            for slot in range(4 * SLOTS_B):
                spot, lane = 4 * (k % 4) + slot // SLOTS_B, TILE * (slot % SLOTS_B)
                if slot < 27:
                    row, column = 48 * k + 16 * (slot // 9), TILE * (slot % 9)
                    piece = g_half[row : row + 16, column : column + TILE]
                elif k < 12:
                    row, column = 16 * (k // 6), TILE * (k % 6)
                    piece = g_noise[row : row + 16, column : column + TILE]
                elif k == 12:
                    piece = loss[...]
                else:
                    piece = jnp.zeros((16, TILE), BF16)
                plane[spot, level, :, lane : lane + TILE] = piece
        copies += fetch([plane.at[:, level]], [plane_far.at[:, level]], sems.at[level : level + 1])
    for copy in copies:
        copy.wait()


def sum_plane_body(came, *rest):
    depth = depth_here()
    targets, column = rest[:4], rest[4]
    for j in range(came.shape[1]):
        total = came[0, j].astype(F32)
        for i in range(1, came.shape[0]):
            total = total + came[i, j].astype(F32)
        column[:, j] = total.astype(BF16)
    for shift, target in enumerate(targets):
        target[...] = column[lax.rem(depth + shift, 4)]


def sum_stack_body(one, two, three, four, total):
    part = one[...].astype(F32) + two[...].astype(F32)
    total[...] = (part + three[...].astype(F32) + four[...].astype(F32)).astype(BF16)


def second_sum_body(one, two, three, four, came, column, spread):
    total = one[...].astype(F32) + two[...].astype(F32)
    total = total + three[...].astype(F32) + four[...].astype(F32)
    column[...] = total.astype(BF16)
    total = came[0].astype(F32)
    for i in range(1, came.shape[0]):
        total = total + came[i].astype(F32)
    total = total.astype(BF16)
    for i in range(came.shape[0]):
        spread[i] = total


def spread_body(one, two, three, four, spread, column, sems):
    depth = depth_here()
    for shift, piece in enumerate((one, two, three, four)):
        column[lax.rem(depth + (4 - shift), 4)] = piece[...]
    parts, spots = spread.shape[1], spread.shape[0]
    sources = [column.at[:, j] for j in range(parts) for i in range(spots)]
    targets = [spread.at[i, j] for j in range(parts) for i in range(spots)]
    for copy in fetch(sources, targets, sems):
        copy.wait()


def unpack_first_body(*refs):
    mine, theirs, (g_hid, g_out, g_pred, hid, out, pred, sems) = refs[:4], refs[4:8], refs[8:]
    depth, core = depth_here(), lax.axis_index("core")
    width = hid.shape[1]
    copies = []
    for step in range(4):
        level = lax.rem(depth + 4 - step, 4)
        for side, which in ((mine, core), (theirs, 1 - core)):
            start = which * (width // 2)

            def column(j):
                return pl.ds(pl.multiple_of(start + TILE * j, TILE), TILE)

            for group in range(4):
                k = 4 * level + group
                for slot in range(4 * SLOTS_A):
                    spot, lane = 4 * group + slot // SLOTS_A, TILE * (slot % SLOTS_A)
                    piece = side[step][spot, :, lane : lane + TILE].astype(F32)
                    if slot < 18:
                        row = 192 * step + 48 * group + 16 * (slot % 9 // 3)
                        (hid, out)[slot // 9][row : row + 16, column(slot % 3)] = piece
                    else:
                        index = k + GROUPS * (slot - 18)

                        @pl.when(index < 18)
                        def _():
                            row = pl.multiple_of(16 * lax.div(index, 3), 16)
                            pred[pl.ds(row, 16), column(lax.rem(index, 3))] = piece

        base = slice(192 * step, 192 * step + 192)
        rows = pl.ds(pl.multiple_of(192 * level, 16), 192)
        copies += fetch(
            (hid.at[base], out.at[base]), (g_hid.at[rows], g_out.at[rows]),
            sems.at[2 * step : 2 * step + 2],
        )
    g_pred[...] = pred[: g_pred.shape[0]]
    for copy in copies:
        copy.wait()


def unpack_plane(core, plane, g_qkv, noise, held, sems):
    wide = held.shape[1] // 3
    copies = []
    total = jnp.zeros((16, TILE), F32)
    for level in range(4):
        for group in range(4):
            k = 4 * level + group
            for slot in range(4 * SLOTS_B):
                spot, lane = 4 * group + slot // SLOTS_B, TILE * (slot % SLOTS_B)
                if slot == 27 and k > 12:
                    continue
                piece = plane[spot, level, :, lane : lane + TILE].astype(F32)
                if slot < 27:
                    row, column = 48 * k + 16 * (slot // 9), TILE * (slot % 9)
                    held[row : row + 16, column : column + TILE] = piece
                elif k < 12:
                    row, column = 16 * (k // 6), TILE * (k % 6)
                    noise[row : row + 16, column : column + TILE] = piece
                else:
                    total = piece
        base = slice(192 * level, 192 * level + 192)
        for section in range(3):
            start = pl.multiple_of(2 * wide * section + wide * core, TILE)
            copies += fetch(
                [held.at[base, wide * section : wide * (section + 1)]],
                [g_qkv.at[base, pl.ds(start, wide)]],
                sems.at[len(copies) : len(copies) + 1],
            )
    return copies, jnp.sum(total, keepdims=True)


def unpack_mine_body(plane, g_qkv, noise, loss, held, sems):
    copies, total = unpack_plane(lax.axis_index("core"), plane, g_qkv, noise, held, sems)
    loss[...] = total
    for copy in copies:
        copy.wait()


def unpack_theirs_body(
    plane, counts, _qkv, noise_mine, loss_mine, g_qkv, noise, mean, held, sems, channels
):
    copies, total = unpack_plane(1 - lax.axis_index("core"), plane, g_qkv, noise, held, sems)
    noise[...] = noise[...] + noise_mine[...]
    live = jnp.sum(counts[...].astype(F32), keepdims=True)
    mean[...] = (total + loss_mine[...]) / (channels * live)
    for copy in copies:
        copy.wait()


def unpack(plane, width, channels=0, counts=None, before=()):
    anywhere = pl.BlockSpec(memory_space=pl.ANY)
    body = unpack_mine_body
    args = (plane,)
    if before:
        body = functools.partial(unpack_theirs_body, channels=channels)
        args += (counts, *before)
    shapes = ((width, 3 * width), (32, width), (1, 1))
    return pl.pallas_call(
        body,
        out_shape=[jax.ShapeDtypeStruct(shape, F32) for shape in shapes],
        in_specs=[anywhere if i == 2 else VMEM for i in range(len(args))],
        out_specs=[anywhere, VMEM, VMEM],
        scratch_shapes=[
            pltpu.VMEM((width, 3 * width // 2), F32), pltpu.SemaphoreType.DMA((12,)),
        ],
        input_output_aliases={2: 0} if before else {},
        compiler_params=pltpu.CompilerParams(vmem_limit_bytes=16 * MIB),
        cost_estimate=pl.CostEstimate(flops=0, bytes_accessed=6 * 10**6, transcendentals=0),
    )(*args)


def unpack_first(mine, theirs, width, channels):
    shapes = ((width, width), (width, width), (channels, width))
    anywhere = pl.BlockSpec(memory_space=pl.ANY)
    return pl.pallas_call(
        unpack_first_body,
        out_shape=[jax.ShapeDtypeStruct(shape, F32) for shape in shapes],
        in_specs=[VMEM] * 8,
        out_specs=[anywhere, anywhere, VMEM],
        scratch_shapes=[
            pltpu.VMEM((width, width), F32), pltpu.VMEM((width, width), F32),
            pltpu.VMEM((96, width), F32), pltpu.SemaphoreType.DMA((8,)),
        ],
        compiler_params=pltpu.CompilerParams(vmem_limit_bytes=16 * MIB),
        cost_estimate=pl.CostEstimate(flops=0, bytes_accessed=8 * 10**6, transcendentals=0),
    )(*mine, *theirs)


def join_body(d_own, rows, from_next, from_prev, d_latent):
    nodes = d_own.shape[2]
    rim = rows.shape[1]
    index = lax.broadcasted_iota(jnp.int32, (nodes, 2 * rim), 0)
    both = jnp.concatenate([rows[0:1, :], rows[1:2, :]], axis=1)
    table = (index == both).astype(F32).T.astype(BF16)
    for m in range(d_own.shape[0]):
        back = jnp.concatenate([from_next[m], from_prev[m]], axis=0)
        d_latent[m] = d_own[m] + mm(back, table, TN)


def on_device(
    latent, send_rows, neighbours, degree, dec_nodes, counts, targets, member_noise,
    w_qkv, w_out, w_noise, w_hid, w_pred,
):
    members, width, nodes = latent.shape
    rim = send_rows.shape[1]
    points = dec_nodes.shape[1]
    channels = targets.shape[0]
    rows = members * nodes
    rims = members * 2 * rim
    degree = degree[None, :]
    size = lax.axis_size(SPACE)
    up = [(i, i + 1) for i in range(size - 1)]
    down = [(i + 1, i) for i in range(size - 1)]

    sent_up, sent_down = call(
        send_body, [((members, rim, width), BF16)] * 2, latent, send_rows,
        apart=(0, 1),
        scratch=[
            pltpu.VMEM(latent.shape, BF16), pltpu.VMEM(send_rows.shape, jnp.int32),
            pltpu.SemaphoreType.DMA((2,)),
        ],
    )
    low = lax.ppermute(sent_up, SPACE, up)
    high = lax.ppermute(sent_down, SPACE, down)
    own, normed, proj = call(
        local_body,
        [((members, nodes, width), BF16), ((rows, width), BF16), ((rows, 3 * width), BF16)],
        latent, member_noise, w_noise, w_qkv,
        apart=(0, 1, 2, 3),
        scratch=[
            pltpu.VMEM(latent.shape, BF16), pltpu.VMEM(member_noise.shape, F32),
            pltpu.VMEM(w_noise.shape, F32),
            pltpu.VMEM((width, 3 * width), BF16), pltpu.VMEM((rows, 3 * width), F32),
            pltpu.SemaphoreType.DMA((6,)),
        ],
        flops=2 * rows * width * 3 * width,
    )
    normed_all, proj_rim, attended, stored, hidden, slope, forecast, table = call(
        forward_body,
        [
            ((rows + rims, width), BF16), ((rims, 2 * width), BF16), ((rows, width), BF16),
            ((rows, width), BF16), ((members, width, points), BF16),
            ((members, width, points), BF16), ((members, channels, points), BF16),
            ((nodes, points), BF16),
        ],
        own, normed, proj, low, high, member_noise, w_noise, w_qkv, w_out, w_hid, w_pred,
        neighbours, degree, dec_nodes,
        apart=(7, 8, 9),
        scratch=[
            pltpu.VMEM((width, 2 * width), BF16), pltpu.VMEM((width, width), BF16),
            pltpu.VMEM((width, width), BF16), pltpu.SemaphoreType.DMA((3,)),
        ],
        flops=3 * 10**9,
    )
    gathered = gather_members(forecast)
    planes, levels = ("x", "y"), ("zlo", "zhi")
    spots = lax.axis_size(planes)
    tile, rest_tile = (16, SPLIT), (16, REST)
    chunk, rest_chunk = (16 // spots,) + tile, (16 // spots,) + rest_tile
    ring = [2 * (z % 2) + z // 2 for z in range(4)]

    def shifted(pieces):
        moved = []
        for shift, piece in enumerate(pieces, 1):
            pairs = [(ring[z], ring[(z + shift) % 4]) for z in range(4)]
            moved.append(lax.ppermute(piece, levels, pairs))
        return moved

    def swapped(a):
        return lax.all_to_all(a, planes, 0, 0, tiled=True)

    first_shape = (CHUNKS, 16, TILE * SLOTS_A)
    swap = [(0, 1), (1, 0)]
    normed_theirs = lax.ppermute(normed_all, "core", swap)
    d_updated, d_attended, keep, send, loss = call(
        crps_body,
        [
            ((rows, width), BF16), ((rows, width), BF16), (first_shape, BF16),
            (first_shape, BF16), ((16, TILE), BF16),
        ],
        counts, forecast, *gathered, targets, hidden, slope, table, stored, attended,
        w_out, w_hid, w_pred,
        smem=(0,),
        scratch=[
            pltpu.VMEM((members, width, points), BF16),
            pltpu.VMEM((members, channels, points), BF16),
            pltpu.VMEM((2,) + first_shape, BF16),
        ],
        flops=6 * 10**9,
    )
    came = lax.ppermute(send, "core", swap)
    tall = (4, 16) + rest_tile
    stacks = call(
        pack_first_body, [((16,) + rest_tile, BF16)] * 4, keep.reshape(tall), came.reshape(tall)
    )
    stacks = [stacks[0]] + shifted(stacks[1:])
    d_proj, d_rim, d_send = call(
        attend_back_body,
        [
            ((2, rows, 3 * width // 2), BF16), ((2, rims, width), BF16),
            ((rows + rims, 3 * width // 2), BF16),
        ],
        proj, proj_rim, neighbours, degree, d_attended,
        scratch=[pltpu.VMEM((nodes + 2 * rim, nodes), F32)],
        flops=2 * 10**9,
    )
    d_theirs = lax.ppermute(d_send, "core", swap)
    d_own, d_low, d_high, g_noise = call(
        norm_back_body,
        [
            ((members, width, nodes), F32), ((members, rim, width), BF16),
            ((members, rim, width), BF16), ((32, width), BF16),
        ],
        own, low, high, member_noise, w_noise, w_qkv, d_proj, d_rim, d_updated,
        flops=2 * 10**9,
    )
    (plane,) = call(
        pack_body,
        [((16, 4) + tile, BF16)],
        normed_all, normed_theirs, d_proj, d_rim, d_theirs, g_noise, loss,
        scratch=[
            pltpu.VMEM((width, 3 * width // 2), BF16), pltpu.VMEM((16, 4) + tile, BF16),
            pltpu.SemaphoreType.DMA((4,)),
        ],
        far=(0,),
        flops=2 * 10**9,
    )
    plane, d_low, d_high = lax.optimization_barrier((plane, d_low, d_high))
    from_next = lax.ppermute(d_low, SPACE, down)
    from_prev = lax.ppermute(d_high, SPACE, up)
    plane = swapped(plane)
    stacks, from_next, from_prev = lax.optimization_barrier((stacks, from_next, from_prev))
    (stack,) = call(sum_stack_body, [((16,) + rest_tile, BF16)], *stacks)
    columns = call(
        sum_plane_body,
        [(chunk, BF16)] * 4,
        plane.reshape((spots, 16 // spots, 4) + tile),
        scratch=[pltpu.VMEM((4,) + chunk, BF16)],
    )
    columns = [columns[0]] + shifted(columns[1:])
    stack = swapped(stack)
    column, stack = call(
        second_sum_body,
        [(chunk, BF16), ((spots,) + rest_chunk, BF16)],
        *columns, stack.reshape((spots,) + rest_chunk),
    )
    columns = [column] + shifted([column] * 3)
    stack = swapped(stack.reshape((16,) + rest_tile))
    (d_latent,) = call(
        join_body, [((members, width, nodes), F32)], d_own, send_rows, from_next, from_prev
    )
    columns, stack, d_latent = lax.optimization_barrier((columns, stack, d_latent))
    (plane,) = call(
        spread_body, [((spots, 16 // spots, 4) + tile, BF16)], *columns,
        far=(0,),
        scratch=[pltpu.VMEM((4,) + chunk, BF16), pltpu.SemaphoreType.DMA((16,))],
    )
    stacks = [stack] + shifted([stack] * 3)
    other_stacks = [lax.ppermute(a, "core", swap) for a in stacks]
    g_hid, g_out, g_pred = unpack_first(stacks, other_stacks, width, channels)
    plane = swapped(plane.reshape((16, 4) + tile))
    plane, g_hid, g_out, g_pred = lax.optimization_barrier((plane, g_hid, g_out, g_pred))
    other_plane = lax.ppermute(plane, "core", swap)
    mine = unpack(plane, width)
    g_qkv, g_noise, mean = unpack(other_plane, width, channels, counts[None, :], mine)
    return mean.reshape(()), d_latent, g_qkv, g_out, g_noise, g_hid, g_pred


def gather_members(forecast):
    swap = [(0, 1), (1, 0)]
    far = lax.ppermute(forecast, "zhi", swap)
    near = lax.ppermute(forecast, "core", swap)
    return near, far, lax.ppermute(far, "core", swap)


def solution(mesh):
    axes = ("x", "zlo", "y", "zhi", "core")
    side = 4 if mesh.shape["space"] == 32 else 1
    mesh = jax.sharding.Mesh(mesh.devices.reshape(side, 2, side, 2, 2), axes)
    member, space = ("zhi", "core"), SPACE
    in_specs = (
        P(member, None, space), P(None, space), P(None, space), P(space),
        P(None, space), P(), P(None, space), P(member, None), P(), P(), P(), P(), P(),
    )
    out_specs = (P(), P(member, None, space), P(), P(), P(), P(), P())
    return jax.shard_map(
        on_device, mesh=mesh, in_specs=in_specs, out_specs=out_specs, check_vma=False
    )
```

```python
import functools

import jax
import jax.numpy as jnp
from jax import lax
from jax.experimental import pallas as pl
from jax.experimental.pallas import tpu as pltpu
from jax.sharding import PartitionSpec as P

HEADS = 6
HEAD = 128
TILE = 128
GROUPS = 16
SPACE = ("x", "zlo", "y")
SPLIT = 896
REST = 1536 - SPLIT
SLOTS_A = 5
SLOTS_B = 7
CHUNKS = 4 * GROUPS
EPS = 1e-5
F32 = jnp.float32
BF16 = jnp.bfloat16
NN = (((1,), (0,)), ((), ()))
NT = (((1,), (1,)), ((), ()))
TN = (((0,), (0,)), ((), ()))
VMEM = pl.BlockSpec(memory_space=pltpu.VMEM)
SMEM = pl.BlockSpec(memory_space=pltpu.SMEM)
APART = pl.BlockSpec(memory_space=pltpu.HBM)
MIB = 1024 * 1024


def mm(a, b, dims=NN):
    return lax.dot_general(a, b, dims, preferred_element_type=F32)


def call(body, out_shape, *args, smem=(), apart=(), far=(), flops=0, scratch=(), vmem=16):
    out_shape = [
        pltpu.HBM(s, d) if i in far else jax.ShapeDtypeStruct(s, d)
        for i, (s, d) in enumerate(out_shape)
    ]
    size = sum(a.size * a.dtype.itemsize for a in args)
    args = [
        pltpu.with_memory_space_constraint(a, pltpu.HBM) if i in apart else a
        for i, a in enumerate(args)
    ]
    return pl.pallas_call(
        body,
        out_shape=out_shape,
        in_specs=[
            SMEM if i in smem else APART if i in apart else VMEM for i in range(len(args))
        ],
        out_specs=[APART if i in far else VMEM for i in range(len(out_shape))],
        scratch_shapes=list(scratch),
        compiler_params=pltpu.CompilerParams(vmem_limit_bytes=vmem * MIB),
        cost_estimate=pl.CostEstimate(flops=flops, bytes_accessed=size, transcendentals=0),
    )(*args)


def gains(noise, w_noise):
    return 1.0 + lax.dot_general(
        noise, w_noise, NN, precision=lax.Precision.HIGHEST, preferred_element_type=F32
    )


def normalise(rows):
    centre = rows - jnp.mean(rows, axis=1, keepdims=True)
    inverse = lax.rsqrt(jnp.mean(centre * centre, axis=1, keepdims=True) + EPS)
    return centre * inverse, inverse


def norm_back(cotangent, gain, hat, inverse):
    d_hat = cotangent * gain
    mean = jnp.mean(d_hat, axis=1, keepdims=True)
    along = jnp.mean(d_hat * hat, axis=1, keepdims=True)
    return inverse * (d_hat - mean - hat * along)


def depth_here():
    return 2 * lax.axis_index("zhi") + lax.axis_index("zlo")


def send_body(latent_far, rows_far, sent_up, sent_down, latent, rows, sems):
    for copy in fetch((latent_far, rows_far), (latent, rows), sems):
        copy.wait()
    nodes = latent.shape[2]
    rim = rows.shape[1]
    both = jnp.concatenate([rows[0:1, :], rows[1:2, :]], axis=1)
    table = lax.broadcasted_iota(jnp.int32, (nodes, 2 * rim), 0) == both
    table = table.astype(F32).T.astype(BF16)
    for m in range(latent.shape[0]):
        picked = mm(table, latent[m], NT).astype(BF16)
        sent_up[m] = picked[:rim]
        sent_down[m] = picked[rim:]


def fetch(sources, targets, sems):
    copies = [
        pltpu.make_async_copy(a, b, sems.at[i]) for i, (a, b) in enumerate(zip(sources, targets))
    ]
    for copy in copies:
        copy.start()
    return copies


def local_body(
    latent_far, noise_far, w_noise_far, w_qkv, own, normed, proj, held,
    latent, noise, w_noise, total, sems,
):
    thirds = [slice(r, r + 256) for r in range(0, held.shape[0], 256)]
    copies = fetch(
        [latent_far, noise_far, w_noise_far] + [w_qkv.at[r] for r in thirds],
        [latent, noise, w_noise] + [held.at[r] for r in thirds],
        sems,
    )
    for copy in copies[:3]:
        copy.wait()
    copies = copies[3:]
    gain = gains(noise[...], w_noise[...])
    members, _, nodes = latent.shape
    for m in range(members):
        rows = latent[m].astype(F32).T
        own[m] = rows.astype(BF16)
        hat, _ = normalise(rows)
        normed[m * nodes : (m + 1) * nodes] = (hat * gain[m : m + 1]).astype(BF16)
    for i, r in enumerate(thirds):
        copies[i].wait()
        part = mm(normed[:, r], held[r])
        if i == 0:
            total[...] = part
        elif i < len(thirds) - 1:
            total[...] = total[...] + part
        else:
            proj[...] = (total[...] + part).astype(BF16)


def slot_mask(nbr, degree, rows):
    slots, nodes = nbr.shape
    index = lax.broadcasted_iota(jnp.int32, (rows, nodes), 0)
    total = jnp.zeros((rows, nodes), F32)
    for j in range(slots):
        live = (index == nbr[j : j + 1, :]) & (degree[...] > j)
        total = total + live.astype(F32)
    return total / degree[...].astype(F32)


def point_table(dec_nodes, nodes):
    points = dec_nodes.shape[1]
    index = lax.broadcasted_iota(jnp.int32, (nodes, points), 0)
    total = jnp.zeros((nodes, points), F32)
    for j in range(dec_nodes.shape[0]):
        total = total + (index == dec_nodes[j : j + 1, :]).astype(F32)
    return total.astype(BF16)


def extend(own, low, high):
    return jnp.concatenate([low, own, high], axis=0)


def forward_body(
    own, normed, proj, low, high, noise, w_noise, w_qkv, w_out, w_hid, w_pred, nbr, degree,
    dec_nodes,
    normed_all, proj_rim, attended, stored, hidden, slope, forecast, table,
    held_out, held_hid, sems,
):
    copies = fetch((w_out, w_hid), (held_out, held_hid), sems)
    members, nodes, width = own.shape
    rim = low.shape[1]
    gain = gains(noise[...], w_noise[...])
    for m in range(members):
        rows = jnp.concatenate([low[m], high[m]], axis=0).astype(F32)
        hat, _ = normalise(rows)
        at = members * nodes + 2 * rim * m
        normed_all[at : at + 2 * rim] = (hat * gain[m : m + 1]).astype(BF16)
    normed_all[: members * nodes] = normed[...]
    proj_rim[...] = mm(normed_all[members * nodes :], w_qkv[:, width:]).astype(BF16)
    mask = slot_mask(nbr, degree, nodes + 2 * rim)
    for m in range(members):
        here = slice(m * nodes, (m + 1) * nodes)
        lo = slice(2 * rim * m, 2 * rim * m + rim)
        hi = slice(2 * rim * m + rim, 2 * rim * (m + 1))
        for h in range(HEADS):
            at = [slice(k * width + h * HEAD, k * width + (h + 1) * HEAD) for k in range(3)]
            rim_at = [slice(a.start - width, a.stop - width) for a in at]
            key = extend(proj[here, at[1]], proj_rim[lo, rim_at[1]], proj_rim[hi, rim_at[1]])
            value = extend(proj[here, at[2]], proj_rim[lo, rim_at[2]], proj_rim[hi, rim_at[2]])
            score = mm(key, proj[here, at[0]], NT) * HEAD**-0.5
            weight = (jax.nn.sigmoid(score) * mask).astype(BF16)
            attended[here, at[0]] = mm(weight, value, TN).astype(BF16)
    copies[0].wait()
    branch = mm(attended[...], held_out[...])
    for m in range(members):
        here = slice(m * nodes, (m + 1) * nodes)
        stored[here] = (own[m].astype(F32) + branch[here]).astype(BF16)
    table[...] = point_table(dec_nodes, nodes)
    copies[1].wait()
    mixed = mm(stored[...], held_hid[...]).astype(BF16)
    block = 256
    for m in range(members):
        part = mixed[m * nodes : (m + 1) * nodes]
        for g in range(0, dec_nodes.shape[1], block):
            pre = mm(part, table[:, g : g + block], TN) * (1.0 / 3.0)
            sig = 0.5 * jnp.tanh(0.5 * pre) + 0.5
            hid = pre * sig
            hidden[m, :, g : g + block] = hid.astype(BF16)
            slope[m, :, g : g + block] = (sig + hid * (1.0 - sig)).astype(BF16)
            forecast[m, :, g : g + block] = mm(
                w_pred[...], hidden[m, :, g : g + block]
            ).astype(BF16)


def smooth(v):
    square = v * v + 0.25
    inverse = lax.rsqrt(square)
    return square * inverse - 0.5, v * inverse


def crps_body(
    counts, mine, *rest
):
    (*others, targets, hidden, slope, table, stored, attended, w_out, w_hid, w_pred,
     d_updated, d_attended, keep, send, loss, d_pre, d_cast, halves) = rest
    live_count = counts[lax.axis_index(SPACE)]
    core = lax.axis_index("core")
    members, channels, points = mine.shape
    total = members * (1 + len(others))
    block = 256
    nodes = table.shape[0]
    scale = 0.5 / (total * (total - 1))
    losses = []
    for g in range(0, points, block):
        at = slice(g, g + block)
        live = lax.broadcasted_iota(jnp.int32, (1, block), 1) + g < live_count
        live = live.astype(F32)
        own = [mine[m, :, at].astype(F32) for m in range(members)]
        aim = targets[:, at]
        near = jnp.zeros((channels, block), F32)
        far = jnp.zeros((channels, block), F32)
        slopes = []
        for m in range(members):
            value, grad = smooth(own[m] - aim)
            near = near + value
            slopes.append([grad, jnp.zeros((channels, block), F32)])
        for a in range(members):
            for b in range(a + 1, members):
                value, grad = smooth(own[a] - own[b])
                far = far + 2.0 * value
                slopes[a][1] = slopes[a][1] + grad
                slopes[b][1] = slopes[b][1] - grad
        for other in others:
            for k in range(members):
                theirs = other[k, :, at].astype(F32)
                for m in range(members):
                    value, grad = smooth(own[m] - theirs)
                    far = far + value
                    slopes[m][1] = slopes[m][1] + grad
        for m in range(members):
            grad = slopes[m][0] * (1.0 / total) - slopes[m][1] * (2.0 * scale)
            d_cast[m, :, at] = (grad * live).astype(BF16)
        column = jnp.sum(near * (1.0 / total) - far * scale, axis=0, keepdims=True) * live
        losses.append(column)
    for i in range(16):
        at = i % 2
        piece = losses[i // 2 % 4][:, TILE * at : TILE * (at + 1)]
        loss[i : i + 1] = piece.astype(BF16) if i < 8 else jnp.zeros((1, TILE), BF16)
    back = w_pred[...].astype(F32).T.astype(BF16)
    grad = jnp.zeros((channels, hidden.shape[1]), F32)
    for m in range(members):
        grad = grad + mm(d_cast[m], hidden[m], NT)
        for g in range(0, points, block):
            at = slice(g, g + block)
            d_hid = mm(back, d_cast[m, :, at])
            d_pre[m, :, at] = (d_hid * slope[m, :, at].astype(F32)).astype(BF16)
    g_pred = jnp.zeros((96 - channels, grad.shape[1]), F32)
    g_pred = jnp.concatenate([grad, g_pred], axis=0).astype(BF16)
    pooled = [
        (mm(table[...], d_pre[m], NT) * (1.0 / 3.0)).astype(BF16) for m in range(members)
    ]
    pooled = jnp.concatenate(pooled, axis=0)
    g_hid = mm(stored[...], pooled, TN).astype(BF16)
    d_updated[...] = mm(pooled, w_hid[...], NT).astype(BF16)
    g_out = mm(attended[...], d_updated[...], TN).astype(BF16)
    d_attended[...] = mm(d_updated[...], w_out[...], NT).astype(BF16)
    half = g_hid.shape[1] // 2
    for c in range(2):
        for k in range(GROUPS):
            for slot in range(SLOTS_A * 4):
                chunk, lane = 4 * k + slot // SLOTS_A, TILE * (slot % SLOTS_A)
                grad, row, column = tile_of_first(k, slot, (g_hid, g_out, g_pred))
                if grad is None:
                    piece = jnp.zeros((16, TILE), BF16)
                else:
                    column = c * half + TILE * column
                    piece = grad[16 * row : 16 * row + 16, column : column + TILE]
                halves[c, chunk, :, lane : lane + TILE] = piece
    keep[...] = halves[core]
    send[...] = halves[1 - core]


def tile_of_first(k, slot, grads):
    if slot < 18:
        part = slot % 9
        return grads[slot // 9], 3 * k + part // 3, part % 3
    tile = k + GROUPS * (slot - 18)
    if tile < 18:
        return grads[2], tile // 3, tile % 3
    return None, 0, 0


def attend_back_body(
    proj, proj_rim, nbr, degree, d_attended,
    d_proj, d_rim, send, mask,
):
    nodes = nbr.shape[1]
    members = proj.shape[0] // nodes
    width = HEADS * HEAD
    rim = proj_rim.shape[0] // (2 * members)
    per_half = HEADS // 2
    part = width // 2
    mask[...] = slot_mask(nbr, degree, nodes + 2 * rim)
    for m in range(members):
        here = slice(m * nodes, (m + 1) * nodes)
        lo = slice(2 * rim * m, 2 * rim * m + rim)
        hi = slice(2 * rim * m + rim, 2 * rim * (m + 1))
        for h in range(HEADS):
            at = [slice(k * width + h * HEAD, k * width + (h + 1) * HEAD) for k in range(3)]
            rim_at = [slice(a.start - width, a.stop - width) for a in at]
            query = proj[here, at[0]]
            key = extend(proj[here, at[1]], proj_rim[lo, rim_at[1]], proj_rim[hi, rim_at[1]])
            value = extend(proj[here, at[2]], proj_rim[lo, rim_at[2]], proj_rim[hi, rim_at[2]])
            out = d_attended[here, at[0]]
            sig = jax.nn.sigmoid(mm(key, query, NT) * HEAD**-0.5)
            weight = sig * mask[...]
            d_value = mm(weight.astype(BF16), out).astype(BF16)
            d_weight = mm(value, out, NT)
            d_score = (d_weight * weight * (1.0 - sig) * HEAD**-0.5).astype(BF16)
            d_key = mm(d_score, query).astype(BF16)
            c, j = h // per_half, h % per_half
            spot = [slice(k * part + j * HEAD, k * part + (j + 1) * HEAD) for k in range(3)]
            d_proj[c, here, spot[0]] = mm(d_score, key, TN).astype(BF16)
            for k, d in ((1, d_key), (2, d_value)):
                d_rim[c, lo, spot[k - 1]] = d[:rim]
                d_proj[c, here, spot[k]] = d[rim : rim + nodes]
                d_rim[c, hi, spot[k - 1]] = d[rim + nodes :]
    rows = members * nodes
    theirs = 1 - lax.axis_index("core")
    send[:rows] = d_proj[theirs]
    send[rows:, : 2 * part] = d_rim[theirs]
    send[rows:, 2 * part :] = jnp.zeros((2 * rim * members, part), BF16)


def norm_back_body(
    own, low, high, noise, w_noise, w_qkv, d_proj, d_rim, d_updated,
    d_own, d_low, d_high, g_noise,
):
    members, nodes, width = own.shape
    rim = low.shape[1]
    part = width // 2
    noises = noise[...]
    gain = gains(noises, w_noise[...])
    d_normed = jnp.zeros((members * nodes, width), F32)
    d_normed_rim = jnp.zeros((members * 2 * rim, width), F32)
    for c in range(2):
        for k in range(3):
            column = k * width + c * part
            weight = w_qkv[:, column : column + part]
            d_normed = d_normed + mm(d_proj[c, :, k * part : (k + 1) * part], weight, NT)
            if k:
                d_normed_rim = d_normed_rim + mm(
                    d_rim[c, :, (k - 1) * part : k * part], weight, NT
                )
    d_noise = jnp.zeros(g_noise.shape, F32)
    noise_columns = jnp.concatenate([noises] * (8 // members), axis=0).T
    for m in range(members):
        here = slice(m * nodes, (m + 1) * nodes)
        rims = slice(2 * rim * m, 2 * rim * (m + 1))
        hat, inverse = normalise(own[m].astype(F32))
        d_gain = jnp.sum(d_normed[here] * hat, axis=0, keepdims=True)
        rows = norm_back(d_normed[here], gain[m : m + 1], hat, inverse)
        d_own[m] = (rows + d_updated[here].astype(F32)).T
        hat, inverse = normalise(jnp.concatenate([low[m], high[m]], axis=0).astype(F32))
        d_gain = d_gain + jnp.sum(d_normed_rim[rims] * hat, axis=0, keepdims=True)
        rows = norm_back(d_normed_rim[rims], gain[m : m + 1], hat, inverse)
        d_low[m] = rows[:rim].astype(BF16)
        d_high[m] = rows[rim:].astype(BF16)
        d_noise = d_noise + noise_columns[:, m : m + 1] * d_gain
    g_noise[...] = d_noise.astype(BF16)


def pack_first_body(keep, came, *stacks):
    depth = depth_here()
    for shift, target in enumerate(stacks):
        level = lax.rem(depth + shift, 4)
        target[...] = (keep[level].astype(F32) + came[level].astype(F32)).astype(BF16)


def pack_body(
    normed, normed_theirs, d_proj, d_rim, d_theirs, g_noise, loss, plane_far, g_half, plane, sems
):
    copies = []
    core = lax.axis_index("core")
    rows = d_proj.shape[1]
    wide = 2 * d_proj.shape[2] // 3
    width = normed.shape[1]
    mine = d_proj[core]
    rim = d_rim[core]
    for r in range(0, width, 192):
        at = slice(r, r + 192)
        total = mm(normed[:rows, at], mine, TN) + mm(normed_theirs[:rows, at], d_theirs[:rows], TN)
        g_half[at, : wide // 2] = total[:, : wide // 2].astype(BF16)
        edge = mm(normed[rows:, at], rim, TN)
        edge = edge + mm(normed_theirs[rows:, at], d_theirs[rows:, :wide], TN)
        g_half[at, wide // 2 :] = (total[:, wide // 2 :] + edge).astype(BF16)
        level = r // 192
        for k in range(4 * level, 4 * level + 4):
            for slot in range(4 * SLOTS_B):
                spot, lane = 4 * (k % 4) + slot // SLOTS_B, TILE * (slot % SLOTS_B)
                if slot < 27:
                    row, column = 48 * k + 16 * (slot // 9), TILE * (slot % 9)
                    piece = g_half[row : row + 16, column : column + TILE]
                elif k < 12:
                    row, column = 16 * (k // 6), TILE * (k % 6)
                    piece = g_noise[row : row + 16, column : column + TILE]
                elif k == 12:
                    piece = loss[...]
                else:
                    piece = jnp.zeros((16, TILE), BF16)
                plane[spot, level, :, lane : lane + TILE] = piece
        copies += fetch([plane.at[:, level]], [plane_far.at[:, level]], sems.at[level : level + 1])
    for copy in copies:
        copy.wait()


def sum_plane_body(came, *rest):
    depth = depth_here()
    targets, column = rest[:4], rest[4]
    for j in range(came.shape[1]):
        total = came[0, j].astype(F32)
        for i in range(1, came.shape[0]):
            total = total + came[i, j].astype(F32)
        column[:, j] = total.astype(BF16)
    for shift, target in enumerate(targets):
        target[...] = column[lax.rem(depth + shift, 4)]


def sum_stack_body(one, two, three, four, total):
    part = one[...].astype(F32) + two[...].astype(F32)
    total[...] = (part + three[...].astype(F32) + four[...].astype(F32)).astype(BF16)


def second_sum_body(one, two, three, four, came, column, spread):
    total = one[...].astype(F32) + two[...].astype(F32)
    total = total + three[...].astype(F32) + four[...].astype(F32)
    column[...] = total.astype(BF16)
    total = came[0].astype(F32)
    for i in range(1, came.shape[0]):
        total = total + came[i].astype(F32)
    total = total.astype(BF16)
    for i in range(came.shape[0]):
        spread[i] = total


def spread_body(one, two, three, four, spread, column, sems):
    depth = depth_here()
    for shift, piece in enumerate((one, two, three, four)):
        column[lax.rem(depth + (4 - shift), 4)] = piece[...]
    parts, spots = spread.shape[1], spread.shape[0]
    sources = [column.at[:, j] for j in range(parts) for i in range(spots)]
    targets = [spread.at[i, j] for j in range(parts) for i in range(spots)]
    for copy in fetch(sources, targets, sems):
        copy.wait()


def unpack_first_body(*refs):
    mine, theirs, (g_hid, g_out, g_pred, hid, out, pred, sems) = refs[:4], refs[4:8], refs[8:]
    depth, core = depth_here(), lax.axis_index("core")
    width = hid.shape[1]
    copies = []
    for step in range(4):
        level = lax.rem(depth + 4 - step, 4)
        for side, which in ((mine, core), (theirs, 1 - core)):
            start = which * (width // 2)

            def column(j):
                return pl.ds(pl.multiple_of(start + TILE * j, TILE), TILE)

            for group in range(4):
                k = 4 * level + group
                for slot in range(4 * SLOTS_A):
                    spot, lane = 4 * group + slot // SLOTS_A, TILE * (slot % SLOTS_A)
                    piece = side[step][spot, :, lane : lane + TILE].astype(F32)
                    if slot < 18:
                        row = 192 * step + 48 * group + 16 * (slot % 9 // 3)
                        (hid, out)[slot // 9][row : row + 16, column(slot % 3)] = piece
                    else:
                        index = k + GROUPS * (slot - 18)

                        @pl.when(index < 18)
                        def _():
                            row = pl.multiple_of(16 * lax.div(index, 3), 16)
                            pred[pl.ds(row, 16), column(lax.rem(index, 3))] = piece

        base = slice(192 * step, 192 * step + 192)
        rows = pl.ds(pl.multiple_of(192 * level, 16), 192)
        copies += fetch(
            (hid.at[base], out.at[base]), (g_hid.at[rows], g_out.at[rows]),
            sems.at[2 * step : 2 * step + 2],
        )
    g_pred[...] = pred[: g_pred.shape[0]]
    for copy in copies:
        copy.wait()


def unpack_plane(core, plane, g_qkv, noise, held, sems):
    wide = held.shape[1] // 3
    copies = []
    total = jnp.zeros((16, TILE), F32)
    for level in range(4):
        for group in range(4):
            k = 4 * level + group
            for slot in range(4 * SLOTS_B):
                spot, lane = 4 * group + slot // SLOTS_B, TILE * (slot % SLOTS_B)
                if slot == 27 and k > 12:
                    continue
                piece = plane[spot, level, :, lane : lane + TILE].astype(F32)
                if slot < 27:
                    row, column = 48 * k + 16 * (slot // 9), TILE * (slot % 9)
                    held[row : row + 16, column : column + TILE] = piece
                elif k < 12:
                    row, column = 16 * (k // 6), TILE * (k % 6)
                    noise[row : row + 16, column : column + TILE] = piece
                else:
                    total = piece
        base = slice(192 * level, 192 * level + 192)
        for section in range(3):
            start = pl.multiple_of(2 * wide * section + wide * core, TILE)
            copies += fetch(
                [held.at[base, wide * section : wide * (section + 1)]],
                [g_qkv.at[base, pl.ds(start, wide)]],
                sems.at[len(copies) : len(copies) + 1],
            )
    return copies, jnp.sum(total, keepdims=True)


def unpack_mine_body(plane, g_qkv, noise, loss, held, sems):
    copies, total = unpack_plane(lax.axis_index("core"), plane, g_qkv, noise, held, sems)
    loss[...] = total
    for copy in copies:
        copy.wait()


def unpack_theirs_body(
    plane, counts, _qkv, noise_mine, loss_mine, g_qkv, noise, mean, held, sems, channels
):
    copies, total = unpack_plane(1 - lax.axis_index("core"), plane, g_qkv, noise, held, sems)
    noise[...] = noise[...] + noise_mine[...]
    live = jnp.sum(counts[...].astype(F32), keepdims=True)
    mean[...] = (total + loss_mine[...]) / (channels * live)
    for copy in copies:
        copy.wait()


def unpack(plane, width, channels=0, counts=None, before=()):
    anywhere = pl.BlockSpec(memory_space=pl.ANY)
    body = unpack_mine_body
    args = (plane,)
    if before:
        body = functools.partial(unpack_theirs_body, channels=channels)
        args += (counts, *before)
    shapes = ((width, 3 * width), (32, width), (1, 1))
    return pl.pallas_call(
        body,
        out_shape=[jax.ShapeDtypeStruct(shape, F32) for shape in shapes],
        in_specs=[anywhere if i == 2 else VMEM for i in range(len(args))],
        out_specs=[anywhere, VMEM, VMEM],
        scratch_shapes=[
            pltpu.VMEM((width, 3 * width // 2), F32), pltpu.SemaphoreType.DMA((12,)),
        ],
        input_output_aliases={2: 0} if before else {},
        compiler_params=pltpu.CompilerParams(vmem_limit_bytes=16 * MIB),
        cost_estimate=pl.CostEstimate(flops=0, bytes_accessed=6 * 10**6, transcendentals=0),
    )(*args)


def unpack_first(mine, theirs, width, channels):
    shapes = ((width, width), (width, width), (channels, width))
    anywhere = pl.BlockSpec(memory_space=pl.ANY)
    return pl.pallas_call(
        unpack_first_body,
        out_shape=[jax.ShapeDtypeStruct(shape, F32) for shape in shapes],
        in_specs=[VMEM] * 8,
        out_specs=[anywhere, anywhere, VMEM],
        scratch_shapes=[
            pltpu.VMEM((width, width), F32), pltpu.VMEM((width, width), F32),
            pltpu.VMEM((96, width), F32), pltpu.SemaphoreType.DMA((8,)),
        ],
        compiler_params=pltpu.CompilerParams(vmem_limit_bytes=16 * MIB),
        cost_estimate=pl.CostEstimate(flops=0, bytes_accessed=8 * 10**6, transcendentals=0),
    )(*mine, *theirs)


def join_body(d_own, rows, from_next, from_prev, d_latent):
    nodes = d_own.shape[2]
    rim = rows.shape[1]
    index = lax.broadcasted_iota(jnp.int32, (nodes, 2 * rim), 0)
    both = jnp.concatenate([rows[0:1, :], rows[1:2, :]], axis=1)
    table = (index == both).astype(F32).T.astype(BF16)
    for m in range(d_own.shape[0]):
        back = jnp.concatenate([from_next[m], from_prev[m]], axis=0)
        d_latent[m] = d_own[m] + mm(back, table, TN)


def on_device(
    latent, send_rows, neighbours, degree, dec_nodes, counts, targets, member_noise,
    w_qkv, w_out, w_noise, w_hid, w_pred,
):
    members, width, nodes = latent.shape
    rim = send_rows.shape[1]
    points = dec_nodes.shape[1]
    channels = targets.shape[0]
    rows = members * nodes
    rims = members * 2 * rim
    degree = degree[None, :]
    size = lax.axis_size(SPACE)
    up = [(i, i + 1) for i in range(size - 1)]
    down = [(i + 1, i) for i in range(size - 1)]

    sent_up, sent_down = call(
        send_body, [((members, rim, width), BF16)] * 2, latent, send_rows,
        apart=(0, 1),
        scratch=[
            pltpu.VMEM(latent.shape, BF16), pltpu.VMEM(send_rows.shape, jnp.int32),
            pltpu.SemaphoreType.DMA((2,)),
        ],
    )
    low = lax.ppermute(sent_up, SPACE, up)
    high = lax.ppermute(sent_down, SPACE, down)
    own, normed, proj, held_qkv = call(
        local_body,
        [
            ((members, nodes, width), BF16), ((rows, width), BF16), ((rows, 3 * width), BF16),
            (w_qkv.shape, BF16),
        ],
        latent, member_noise, w_noise, w_qkv,
        apart=(0, 1, 2, 3),
        scratch=[
            pltpu.VMEM(latent.shape, BF16), pltpu.VMEM(member_noise.shape, F32),
            pltpu.VMEM(w_noise.shape, F32),
            pltpu.VMEM((rows, 3 * width), F32), pltpu.SemaphoreType.DMA((6,)),
        ],
        flops=2 * rows * width * 3 * width,
    )
    normed_all, proj_rim, attended, stored, hidden, slope, forecast, table = call(
        forward_body,
        [
            ((rows + rims, width), BF16), ((rims, 2 * width), BF16), ((rows, width), BF16),
            ((rows, width), BF16), ((members, width, points), BF16),
            ((members, width, points), BF16), ((members, channels, points), BF16),
            ((nodes, points), BF16),
        ],
        own, normed, proj, low, high, member_noise, w_noise, held_qkv, w_out, w_hid, w_pred,
        neighbours, degree, dec_nodes,
        apart=(8, 9),
        scratch=[
            pltpu.VMEM((width, width), BF16), pltpu.VMEM((width, width), BF16),
            pltpu.SemaphoreType.DMA((2,)),
        ],
        flops=3 * 10**9,
    )
    gathered = gather_members(forecast)
    planes, levels = ("x", "y"), ("zlo", "zhi")
    spots = lax.axis_size(planes)
    tile, rest_tile = (16, SPLIT), (16, REST)
    chunk, rest_chunk = (16 // spots,) + tile, (16 // spots,) + rest_tile
    ring = [2 * (z % 2) + z // 2 for z in range(4)]

    def shifted(pieces):
        moved = []
        for shift, piece in enumerate(pieces, 1):
            pairs = [(ring[z], ring[(z + shift) % 4]) for z in range(4)]
            moved.append(lax.ppermute(piece, levels, pairs))
        return moved

    def swapped(a):
        return lax.all_to_all(a, planes, 0, 0, tiled=True)

    first_shape = (CHUNKS, 16, TILE * SLOTS_A)
    swap = [(0, 1), (1, 0)]
    normed_theirs = lax.ppermute(normed_all, "core", swap)
    d_updated, d_attended, keep, send, loss = call(
        crps_body,
        [
            ((rows, width), BF16), ((rows, width), BF16), (first_shape, BF16),
            (first_shape, BF16), ((16, TILE), BF16),
        ],
        counts, forecast, *gathered, targets, hidden, slope, table, stored, attended,
        w_out, w_hid, w_pred,
        smem=(0,),
        scratch=[
            pltpu.VMEM((members, width, points), BF16),
            pltpu.VMEM((members, channels, points), BF16),
            pltpu.VMEM((2,) + first_shape, BF16),
        ],
        flops=6 * 10**9,
    )
    came = lax.ppermute(send, "core", swap)
    tall = (4, 16) + rest_tile
    stacks = call(
        pack_first_body, [((16,) + rest_tile, BF16)] * 4, keep.reshape(tall), came.reshape(tall)
    )
    stacks = [stacks[0]] + shifted(stacks[1:])
    d_proj, d_rim, d_send = call(
        attend_back_body,
        [
            ((2, rows, 3 * width // 2), BF16), ((2, rims, width), BF16),
            ((rows + rims, 3 * width // 2), BF16),
        ],
        proj, proj_rim, neighbours, degree, d_attended,
        scratch=[pltpu.VMEM((nodes + 2 * rim, nodes), F32)],
        flops=2 * 10**9,
    )
    d_theirs = lax.ppermute(d_send, "core", swap)
    d_own, d_low, d_high, g_noise = call(
        norm_back_body,
        [
            ((members, width, nodes), F32), ((members, rim, width), BF16),
            ((members, rim, width), BF16), ((32, width), BF16),
        ],
        own, low, high, member_noise, w_noise, held_qkv, d_proj, d_rim, d_updated,
        flops=2 * 10**9,
    )
    (plane,) = call(
        pack_body,
        [((16, 4) + tile, BF16)],
        normed_all, normed_theirs, d_proj, d_rim, d_theirs, g_noise, loss,
        scratch=[
            pltpu.VMEM((width, 3 * width // 2), BF16), pltpu.VMEM((16, 4) + tile, BF16),
            pltpu.SemaphoreType.DMA((4,)),
        ],
        far=(0,),
        flops=2 * 10**9,
    )
    plane, d_low, d_high = lax.optimization_barrier((plane, d_low, d_high))
    from_next = lax.ppermute(d_low, SPACE, down)
    from_prev = lax.ppermute(d_high, SPACE, up)
    plane = swapped(plane)
    stacks, from_next, from_prev = lax.optimization_barrier((stacks, from_next, from_prev))
    (stack,) = call(sum_stack_body, [((16,) + rest_tile, BF16)], *stacks)
    columns = call(
        sum_plane_body,
        [(chunk, BF16)] * 4,
        plane.reshape((spots, 16 // spots, 4) + tile),
        scratch=[pltpu.VMEM((4,) + chunk, BF16)],
    )
    columns = [columns[0]] + shifted(columns[1:])
    stack = swapped(stack)
    column, stack = call(
        second_sum_body,
        [(chunk, BF16), ((spots,) + rest_chunk, BF16)],
        *columns, stack.reshape((spots,) + rest_chunk),
    )
    columns = [column] + shifted([column] * 3)
    stack = swapped(stack.reshape((16,) + rest_tile))
    (d_latent,) = call(
        join_body, [((members, width, nodes), F32)], d_own, send_rows, from_next, from_prev
    )
    columns, stack, d_latent = lax.optimization_barrier((columns, stack, d_latent))
    (plane,) = call(
        spread_body, [((spots, 16 // spots, 4) + tile, BF16)], *columns,
        far=(0,),
        scratch=[pltpu.VMEM((4,) + chunk, BF16), pltpu.SemaphoreType.DMA((16,))],
    )
    stacks = [stack] + shifted([stack] * 3)
    other_stacks = [lax.ppermute(a, "core", swap) for a in stacks]
    g_hid, g_out, g_pred = unpack_first(stacks, other_stacks, width, channels)
    plane = swapped(plane.reshape((16, 4) + tile))
    plane, g_hid, g_out, g_pred = lax.optimization_barrier((plane, g_hid, g_out, g_pred))
    other_plane = lax.ppermute(plane, "core", swap)
    mine = unpack(plane, width)
    g_qkv, g_noise, mean = unpack(other_plane, width, channels, counts[None, :], mine)
    return mean.reshape(()), d_latent, g_qkv, g_out, g_noise, g_hid, g_pred


def gather_members(forecast):
    swap = [(0, 1), (1, 0)]
    far = lax.ppermute(forecast, "zhi", swap)
    near = lax.ppermute(forecast, "core", swap)
    return near, far, lax.ppermute(far, "core", swap)


def solution(mesh):
    axes = ("x", "zlo", "y", "zhi", "core")
    side = 4 if mesh.shape["space"] == 32 else 1
    mesh = jax.sharding.Mesh(mesh.devices.reshape(side, 2, side, 2, 2), axes)
    member, space = ("zhi", "core"), SPACE
    in_specs = (
        P(member, None, space), P(None, space), P(None, space), P(space),
        P(None, space), P(), P(None, space), P(member, None), P(), P(), P(), P(), P(),
    )
    out_specs = (P(), P(member, None, space), P(), P(), P(), P(), P())
    return jax.shard_map(
        on_device, mesh=mesh, in_specs=in_specs, out_specs=out_specs, check_vma=False
    )
```

```python
import functools

import jax
import jax.numpy as jnp
from jax import lax
from jax.experimental import pallas as pl
from jax.experimental.pallas import tpu as pltpu
from jax.sharding import PartitionSpec as P

HEADS = 6
HEAD = 128
TILE = 128
GROUPS = 16
SPACE = ("x", "zlo", "y")
SPLIT = 896
REST = 1536 - SPLIT
SLOTS_A = 5
SLOTS_B = 7
CHUNKS = 4 * GROUPS
EPS = 1e-5
F32 = jnp.float32
BF16 = jnp.bfloat16
NN = (((1,), (0,)), ((), ()))
NT = (((1,), (1,)), ((), ()))
TN = (((0,), (0,)), ((), ()))
VMEM = pl.BlockSpec(memory_space=pltpu.VMEM)
SMEM = pl.BlockSpec(memory_space=pltpu.SMEM)
APART = pl.BlockSpec(memory_space=pltpu.HBM)
MIB = 1024 * 1024


def mm(a, b, dims=NN):
    return lax.dot_general(a, b, dims, preferred_element_type=F32)


def call(body, out_shape, *args, smem=(), apart=(), far=(), flops=0, scratch=(), vmem=16):
    out_shape = [
        pltpu.HBM(s, d) if i in far else jax.ShapeDtypeStruct(s, d)
        for i, (s, d) in enumerate(out_shape)
    ]
    size = sum(a.size * a.dtype.itemsize for a in args)
    args = [
        pltpu.with_memory_space_constraint(a, pltpu.HBM) if i in apart else a
        for i, a in enumerate(args)
    ]
    return pl.pallas_call(
        body,
        out_shape=out_shape,
        in_specs=[
            SMEM if i in smem else APART if i in apart else VMEM for i in range(len(args))
        ],
        out_specs=[APART if i in far else VMEM for i in range(len(out_shape))],
        scratch_shapes=list(scratch),
        compiler_params=pltpu.CompilerParams(vmem_limit_bytes=vmem * MIB),
        cost_estimate=pl.CostEstimate(flops=flops, bytes_accessed=size, transcendentals=0),
    )(*args)


def gains(noise, w_noise):
    return 1.0 + lax.dot_general(
        noise, w_noise, NN, precision=lax.Precision.HIGHEST, preferred_element_type=F32
    )


def normalise(rows):
    centre = rows - jnp.mean(rows, axis=1, keepdims=True)
    inverse = lax.rsqrt(jnp.mean(centre * centre, axis=1, keepdims=True) + EPS)
    return centre * inverse, inverse


def norm_back(cotangent, gain, hat, inverse):
    d_hat = cotangent * gain
    mean = jnp.mean(d_hat, axis=1, keepdims=True)
    along = jnp.mean(d_hat * hat, axis=1, keepdims=True)
    return inverse * (d_hat - mean - hat * along)


def depth_here():
    return 2 * lax.axis_index("zhi") + lax.axis_index("zlo")


def send_body(latent_far, rows_far, sent_up, sent_down, latent, rows, sems):
    for copy in fetch((latent_far, rows_far), (latent, rows), sems):
        copy.wait()
    nodes = latent.shape[2]
    rim = rows.shape[1]
    both = jnp.concatenate([rows[0:1, :], rows[1:2, :]], axis=1)
    table = lax.broadcasted_iota(jnp.int32, (nodes, 2 * rim), 0) == both
    table = table.astype(F32).T.astype(BF16)
    for m in range(latent.shape[0]):
        picked = mm(table, latent[m], NT).astype(BF16)
        sent_up[m] = picked[:rim]
        sent_down[m] = picked[rim:]


def fetch(sources, targets, sems):
    copies = [
        pltpu.make_async_copy(a, b, sems.at[i]) for i, (a, b) in enumerate(zip(sources, targets))
    ]
    for copy in copies:
        copy.start()
    return copies


def local_body(
    latent_far, noise_far, w_noise_far, w_qkv, own, normed, proj, held,
    latent, noise, w_noise, total, sems,
):
    thirds = [slice(r, r + 256) for r in range(0, held.shape[0], 256)]
    copies = fetch(
        [latent_far, noise_far, w_noise_far] + [w_qkv.at[r] for r in thirds],
        [latent, noise, w_noise] + [held.at[r] for r in thirds],
        sems,
    )
    for copy in copies[:3]:
        copy.wait()
    copies = copies[3:]
    gain = gains(noise[...], w_noise[...])
    members, _, nodes = latent.shape
    for m in range(members):
        rows = latent[m].astype(F32).T
        own[m] = rows.astype(BF16)
        hat, _ = normalise(rows)
        normed[m * nodes : (m + 1) * nodes] = (hat * gain[m : m + 1]).astype(BF16)
    for i, r in enumerate(thirds):
        copies[i].wait()
        part = mm(normed[:, r], held[r])
        if i == 0:
            total[...] = part
        elif i < len(thirds) - 1:
            total[...] = total[...] + part
        else:
            proj[...] = (total[...] + part).astype(BF16)


def slot_mask(nbr, degree, rows):
    slots, nodes = nbr.shape
    index = lax.broadcasted_iota(jnp.int32, (rows, nodes), 0)
    total = jnp.zeros((rows, nodes), F32)
    for j in range(slots):
        live = (index == nbr[j : j + 1, :]) & (degree[...] > j)
        total = total + live.astype(F32)
    return total / degree[...].astype(F32)


def point_table(dec_nodes, nodes):
    points = dec_nodes.shape[1]
    index = lax.broadcasted_iota(jnp.int32, (nodes, points), 0)
    total = jnp.zeros((nodes, points), F32)
    for j in range(dec_nodes.shape[0]):
        total = total + (index == dec_nodes[j : j + 1, :]).astype(F32)
    return total.astype(BF16)


def extend(own, low, high):
    return jnp.concatenate([low, own, high], axis=0)


def forward_body(
    own, normed, proj, low, high, noise, w_noise, w_qkv, w_out, w_hid, w_pred, nbr, degree,
    dec_nodes,
    normed_all, proj_rim, attended, stored, hidden, slope, forecast, table,
    held_out, held_hid, sems,
):
    copies = fetch((w_out, w_hid), (held_out, held_hid), sems)
    members, nodes, width = own.shape
    rim = low.shape[1]
    gain = gains(noise[...], w_noise[...])
    for m in range(members):
        rows = jnp.concatenate([low[m], high[m]], axis=0).astype(F32)
        hat, _ = normalise(rows)
        at = members * nodes + 2 * rim * m
        normed_all[at : at + 2 * rim] = (hat * gain[m : m + 1]).astype(BF16)
    normed_all[: members * nodes] = normed[...]
    proj_rim[...] = mm(normed_all[members * nodes :], w_qkv[:, width:]).astype(BF16)
    mask = slot_mask(nbr, degree, nodes + 2 * rim)
    for m in range(members):
        here = slice(m * nodes, (m + 1) * nodes)
        lo = slice(2 * rim * m, 2 * rim * m + rim)
        hi = slice(2 * rim * m + rim, 2 * rim * (m + 1))
        for h in range(HEADS):
            at = [slice(k * width + h * HEAD, k * width + (h + 1) * HEAD) for k in range(3)]
            rim_at = [slice(a.start - width, a.stop - width) for a in at]
            key = extend(proj[here, at[1]], proj_rim[lo, rim_at[1]], proj_rim[hi, rim_at[1]])
            value = extend(proj[here, at[2]], proj_rim[lo, rim_at[2]], proj_rim[hi, rim_at[2]])
            score = mm(key, proj[here, at[0]], NT) * HEAD**-0.5
            weight = (jax.nn.sigmoid(score) * mask).astype(BF16)
            attended[here, at[0]] = mm(weight, value, TN).astype(BF16)
    copies[0].wait()
    branch = mm(attended[...], held_out[...])
    for m in range(members):
        here = slice(m * nodes, (m + 1) * nodes)
        stored[here] = (own[m].astype(F32) + branch[here]).astype(BF16)
    table[...] = point_table(dec_nodes, nodes)
    copies[1].wait()
    mixed = mm(stored[...], held_hid[...]).astype(BF16)
    block = 256
    for m in range(members):
        part = mixed[m * nodes : (m + 1) * nodes]
        for g in range(0, dec_nodes.shape[1], block):
            pre = mm(part, table[:, g : g + block], TN) * (1.0 / 3.0)
            sig = 0.5 * jnp.tanh(0.5 * pre) + 0.5
            hid = pre * sig
            hidden[m, :, g : g + block] = hid.astype(BF16)
            slope[m, :, g : g + block] = (sig + hid * (1.0 - sig)).astype(BF16)
            forecast[m, :, g : g + block] = mm(
                w_pred[...], hidden[m, :, g : g + block]
            ).astype(BF16)


def smooth(v):
    square = v * v + 0.25
    inverse = lax.rsqrt(square)
    return square * inverse - 0.5, v * inverse


def crps_near_body(mine, near, targets, slopes, columns):
    members, channels, points = mine.shape
    total = 8
    block = 256
    scale = 0.5 / (total * (total - 1))
    for g in range(0, points, block):
        at = slice(g, g + block)
        own = [mine[m, :, at].astype(F32) for m in range(members)]
        aim = targets[:, at]
        close = jnp.zeros((channels, block), F32)
        apart = jnp.zeros((channels, block), F32)
        first = []
        grads = [jnp.zeros((channels, block), F32)] * members
        for m in range(members):
            value, grad = smooth(own[m] - aim)
            close = close + value
            first.append(grad)
        for a in range(members):
            for b in range(a + 1, members):
                value, grad = smooth(own[a] - own[b])
                apart = apart + 2.0 * value
                grads[a] = grads[a] + grad
                grads[b] = grads[b] - grad
        for k in range(members):
            theirs = near[k, :, at].astype(F32)
            for m in range(members):
                value, grad = smooth(own[m] - theirs)
                apart = apart + value
                grads[m] = grads[m] + grad
        for m in range(members):
            slopes[m, :, at] = first[m] * (1.0 / total) - grads[m] * (2.0 * scale)
        columns[:, at] = jnp.sum(
            close * (1.0 / total) - apart * scale, axis=0, keepdims=True
        )


def crps_body(
    counts, mine, *rest
):
    (*others, slopes, columns, hidden, slope, table, stored, attended, w_out, w_hid, w_pred,
     d_updated, d_attended, keep, send, loss, d_pre, d_cast, halves) = rest
    live_count = counts[lax.axis_index(SPACE)]
    core = lax.axis_index("core")
    members, channels, points = mine.shape
    total = 8
    block = 256
    scale = 0.5 / (total * (total - 1))
    losses = []
    for g in range(0, points, block):
        at = slice(g, g + block)
        live = lax.broadcasted_iota(jnp.int32, (1, block), 1) + g < live_count
        live = live.astype(F32)
        own = [mine[m, :, at].astype(F32) for m in range(members)]
        apart = jnp.zeros((channels, block), F32)
        grads = [jnp.zeros((channels, block), F32)] * members
        for other in others:
            for k in range(members):
                theirs = other[k, :, at].astype(F32)
                for m in range(members):
                    value, grad = smooth(own[m] - theirs)
                    apart = apart + value
                    grads[m] = grads[m] + grad
        for m in range(members):
            grad = slopes[m, :, at] - grads[m] * (2.0 * scale)
            d_cast[m, :, at] = (grad * live).astype(BF16)
        column = columns[:, at] - jnp.sum(apart, axis=0, keepdims=True) * scale
        losses.append(column * live)
    for i in range(16):
        at = i % 2
        piece = losses[i // 2 % 4][:, TILE * at : TILE * (at + 1)]
        loss[i : i + 1] = piece.astype(BF16) if i < 8 else jnp.zeros((1, TILE), BF16)
    back = w_pred[...].astype(F32).T.astype(BF16)
    grad = jnp.zeros((channels, hidden.shape[1]), F32)
    for m in range(members):
        grad = grad + mm(d_cast[m], hidden[m], NT)
        for g in range(0, points, block):
            at = slice(g, g + block)
            d_hid = mm(back, d_cast[m, :, at])
            d_pre[m, :, at] = (d_hid * slope[m, :, at].astype(F32)).astype(BF16)
    g_pred = jnp.zeros((96 - channels, grad.shape[1]), F32)
    g_pred = jnp.concatenate([grad, g_pred], axis=0).astype(BF16)
    pooled = [
        (mm(table[...], d_pre[m], NT) * (1.0 / 3.0)).astype(BF16) for m in range(members)
    ]
    pooled = jnp.concatenate(pooled, axis=0)
    g_hid = mm(stored[...], pooled, TN).astype(BF16)
    d_updated[...] = mm(pooled, w_hid[...], NT).astype(BF16)
    g_out = mm(attended[...], d_updated[...], TN).astype(BF16)
    d_attended[...] = mm(d_updated[...], w_out[...], NT).astype(BF16)
    half = g_hid.shape[1] // 2
    for c in range(2):
        for k in range(GROUPS):
            for slot in range(SLOTS_A * 4):
                chunk, lane = 4 * k + slot // SLOTS_A, TILE * (slot % SLOTS_A)
                grad, row, column = tile_of_first(k, slot, (g_hid, g_out, g_pred))
                if grad is None:
                    piece = jnp.zeros((16, TILE), BF16)
                else:
                    column = c * half + TILE * column
                    piece = grad[16 * row : 16 * row + 16, column : column + TILE]
                halves[c, chunk, :, lane : lane + TILE] = piece
    keep[...] = halves[core]
    send[...] = halves[1 - core]


def tile_of_first(k, slot, grads):
    if slot < 18:
        part = slot % 9
        return grads[slot // 9], 3 * k + part // 3, part % 3
    tile = k + GROUPS * (slot - 18)
    if tile < 18:
        return grads[2], tile // 3, tile % 3
    return None, 0, 0


def attend_back_body(
    proj, proj_rim, nbr, degree, d_attended,
    d_proj, d_rim, send, mask,
):
    nodes = nbr.shape[1]
    members = proj.shape[0] // nodes
    width = HEADS * HEAD
    rim = proj_rim.shape[0] // (2 * members)
    per_half = HEADS // 2
    part = width // 2
    mask[...] = slot_mask(nbr, degree, nodes + 2 * rim)
    for m in range(members):
        here = slice(m * nodes, (m + 1) * nodes)
        lo = slice(2 * rim * m, 2 * rim * m + rim)
        hi = slice(2 * rim * m + rim, 2 * rim * (m + 1))
        for h in range(HEADS):
            at = [slice(k * width + h * HEAD, k * width + (h + 1) * HEAD) for k in range(3)]
            rim_at = [slice(a.start - width, a.stop - width) for a in at]
            query = proj[here, at[0]]
            key = extend(proj[here, at[1]], proj_rim[lo, rim_at[1]], proj_rim[hi, rim_at[1]])
            value = extend(proj[here, at[2]], proj_rim[lo, rim_at[2]], proj_rim[hi, rim_at[2]])
            out = d_attended[here, at[0]]
            sig = jax.nn.sigmoid(mm(key, query, NT) * HEAD**-0.5)
            weight = sig * mask[...]
            d_value = mm(weight.astype(BF16), out).astype(BF16)
            d_weight = mm(value, out, NT)
            d_score = (d_weight * weight * (1.0 - sig) * HEAD**-0.5).astype(BF16)
            d_key = mm(d_score, query).astype(BF16)
            c, j = h // per_half, h % per_half
            spot = [slice(k * part + j * HEAD, k * part + (j + 1) * HEAD) for k in range(3)]
            d_proj[c, here, spot[0]] = mm(d_score, key, TN).astype(BF16)
            for k, d in ((1, d_key), (2, d_value)):
                d_rim[c, lo, spot[k - 1]] = d[:rim]
                d_proj[c, here, spot[k]] = d[rim : rim + nodes]
                d_rim[c, hi, spot[k - 1]] = d[rim + nodes :]
    rows = members * nodes
    theirs = 1 - lax.axis_index("core")
    send[:rows] = d_proj[theirs]
    send[rows:, : 2 * part] = d_rim[theirs]
    send[rows:, 2 * part :] = jnp.zeros((2 * rim * members, part), BF16)


def norm_back_body(
    own, low, high, noise, w_noise, w_qkv, d_proj, d_rim, d_updated,
    d_own, d_low, d_high, g_noise,
):
    members, nodes, width = own.shape
    rim = low.shape[1]
    part = width // 2
    noises = noise[...]
    gain = gains(noises, w_noise[...])
    d_normed = jnp.zeros((members * nodes, width), F32)
    d_normed_rim = jnp.zeros((members * 2 * rim, width), F32)
    for c in range(2):
        for k in range(3):
            column = k * width + c * part
            weight = w_qkv[:, column : column + part]
            d_normed = d_normed + mm(d_proj[c, :, k * part : (k + 1) * part], weight, NT)
            if k:
                d_normed_rim = d_normed_rim + mm(
                    d_rim[c, :, (k - 1) * part : k * part], weight, NT
                )
    d_noise = jnp.zeros(g_noise.shape, F32)
    noise_columns = jnp.concatenate([noises] * (8 // members), axis=0).T
    for m in range(members):
        here = slice(m * nodes, (m + 1) * nodes)
        rims = slice(2 * rim * m, 2 * rim * (m + 1))
        hat, inverse = normalise(own[m].astype(F32))
        d_gain = jnp.sum(d_normed[here] * hat, axis=0, keepdims=True)
        rows = norm_back(d_normed[here], gain[m : m + 1], hat, inverse)
        d_own[m] = (rows + d_updated[here].astype(F32)).T
        hat, inverse = normalise(jnp.concatenate([low[m], high[m]], axis=0).astype(F32))
        d_gain = d_gain + jnp.sum(d_normed_rim[rims] * hat, axis=0, keepdims=True)
        rows = norm_back(d_normed_rim[rims], gain[m : m + 1], hat, inverse)
        d_low[m] = rows[:rim].astype(BF16)
        d_high[m] = rows[rim:].astype(BF16)
        d_noise = d_noise + noise_columns[:, m : m + 1] * d_gain
    g_noise[...] = d_noise.astype(BF16)


def pack_first_body(keep, came, *stacks):
    depth = depth_here()
    for shift, target in enumerate(stacks):
        level = lax.rem(depth + shift, 4)
        target[...] = (keep[level].astype(F32) + came[level].astype(F32)).astype(BF16)


def pack_body(
    normed, normed_theirs, d_proj, d_rim, d_theirs, g_noise, loss, plane_far, g_half, plane, sems
):
    copies = []
    core = lax.axis_index("core")
    rows = d_proj.shape[1]
    wide = 2 * d_proj.shape[2] // 3
    width = normed.shape[1]
    mine = d_proj[core]
    rim = d_rim[core]
    for r in range(0, width, 192):
        at = slice(r, r + 192)
        total = mm(normed[:rows, at], mine, TN) + mm(normed_theirs[:rows, at], d_theirs[:rows], TN)
        g_half[at, : wide // 2] = total[:, : wide // 2].astype(BF16)
        edge = mm(normed[rows:, at], rim, TN)
        edge = edge + mm(normed_theirs[rows:, at], d_theirs[rows:, :wide], TN)
        g_half[at, wide // 2 :] = (total[:, wide // 2 :] + edge).astype(BF16)
        level = r // 192
        for k in range(4 * level, 4 * level + 4):
            for slot in range(4 * SLOTS_B):
                spot, lane = 4 * (k % 4) + slot // SLOTS_B, TILE * (slot % SLOTS_B)
                if slot < 27:
                    row, column = 48 * k + 16 * (slot // 9), TILE * (slot % 9)
                    piece = g_half[row : row + 16, column : column + TILE]
                elif k < 12:
                    row, column = 16 * (k // 6), TILE * (k % 6)
                    piece = g_noise[row : row + 16, column : column + TILE]
                elif k == 12:
                    piece = loss[...]
                else:
                    piece = jnp.zeros((16, TILE), BF16)
                plane[spot, level, :, lane : lane + TILE] = piece
        copies += fetch([plane.at[:, level]], [plane_far.at[:, level]], sems.at[level : level + 1])
    for copy in copies:
        copy.wait()


def sum_plane_body(came, *rest):
    depth = depth_here()
    targets, column = rest[:4], rest[4]
    for j in range(came.shape[1]):
        total = came[0, j].astype(F32)
        for i in range(1, came.shape[0]):
            total = total + came[i, j].astype(F32)
        column[:, j] = total.astype(BF16)
    for shift, target in enumerate(targets):
        target[...] = column[lax.rem(depth + shift, 4)]


def sum_stack_body(one, two, three, four, total):
    part = one[...].astype(F32) + two[...].astype(F32)
    total[...] = (part + three[...].astype(F32) + four[...].astype(F32)).astype(BF16)


def second_sum_body(one, two, three, four, came, column, spread):
    total = one[...].astype(F32) + two[...].astype(F32)
    total = total + three[...].astype(F32) + four[...].astype(F32)
    column[...] = total.astype(BF16)
    total = came[0].astype(F32)
    for i in range(1, came.shape[0]):
        total = total + came[i].astype(F32)
    total = total.astype(BF16)
    for i in range(came.shape[0]):
        spread[i] = total


def spread_body(one, two, three, four, spread, column, sems):
    depth = depth_here()
    for shift, piece in enumerate((one, two, three, four)):
        column[lax.rem(depth + (4 - shift), 4)] = piece[...]
    parts, spots = spread.shape[1], spread.shape[0]
    sources = [column.at[:, j] for j in range(parts) for i in range(spots)]
    targets = [spread.at[i, j] for j in range(parts) for i in range(spots)]
    for copy in fetch(sources, targets, sems):
        copy.wait()


def unpack_first_body(*refs):
    mine, theirs, (g_hid, g_out, g_pred, hid, out, pred, sems) = refs[:4], refs[4:8], refs[8:]
    depth, core = depth_here(), lax.axis_index("core")
    width = hid.shape[1]
    copies = []
    for step in range(4):
        level = lax.rem(depth + 4 - step, 4)
        for side, which in ((mine, core), (theirs, 1 - core)):
            start = which * (width // 2)

            def column(j):
                return pl.ds(pl.multiple_of(start + TILE * j, TILE), TILE)

            for group in range(4):
                k = 4 * level + group
                for slot in range(4 * SLOTS_A):
                    spot, lane = 4 * group + slot // SLOTS_A, TILE * (slot % SLOTS_A)
                    piece = side[step][spot, :, lane : lane + TILE].astype(F32)
                    if slot < 18:
                        row = 192 * step + 48 * group + 16 * (slot % 9 // 3)
                        (hid, out)[slot // 9][row : row + 16, column(slot % 3)] = piece
                    else:
                        index = k + GROUPS * (slot - 18)

                        @pl.when(index < 18)
                        def _():
                            row = pl.multiple_of(16 * lax.div(index, 3), 16)
                            pred[pl.ds(row, 16), column(lax.rem(index, 3))] = piece

        base = slice(192 * step, 192 * step + 192)
        rows = pl.ds(pl.multiple_of(192 * level, 16), 192)
        copies += fetch(
            (hid.at[base], out.at[base]), (g_hid.at[rows], g_out.at[rows]),
            sems.at[2 * step : 2 * step + 2],
        )
    g_pred[...] = pred[: g_pred.shape[0]]
    for copy in copies:
        copy.wait()


def unpack_plane(core, plane, g_qkv, noise, held, sems):
    wide = held.shape[1] // 3
    copies = []
    total = jnp.zeros((16, TILE), F32)
    for level in range(4):
        for group in range(4):
            k = 4 * level + group
            for slot in range(4 * SLOTS_B):
                spot, lane = 4 * group + slot // SLOTS_B, TILE * (slot % SLOTS_B)
                if slot == 27 and k > 12:
                    continue
                piece = plane[spot, level, :, lane : lane + TILE].astype(F32)
                if slot < 27:
                    row, column = 48 * k + 16 * (slot // 9), TILE * (slot % 9)
                    held[row : row + 16, column : column + TILE] = piece
                elif k < 12:
                    row, column = 16 * (k // 6), TILE * (k % 6)
                    noise[row : row + 16, column : column + TILE] = piece
                else:
                    total = piece
        base = slice(192 * level, 192 * level + 192)
        for section in range(3):
            start = pl.multiple_of(2 * wide * section + wide * core, TILE)
            copies += fetch(
                [held.at[base, wide * section : wide * (section + 1)]],
                [g_qkv.at[base, pl.ds(start, wide)]],
                sems.at[len(copies) : len(copies) + 1],
            )
    return copies, jnp.sum(total, keepdims=True)


def unpack_mine_body(plane, g_qkv, noise, loss, held, sems):
    copies, total = unpack_plane(lax.axis_index("core"), plane, g_qkv, noise, held, sems)
    loss[...] = total
    for copy in copies:
        copy.wait()


def unpack_theirs_body(
    plane, counts, _qkv, noise_mine, loss_mine, g_qkv, noise, mean, held, sems, channels
):
    copies, total = unpack_plane(1 - lax.axis_index("core"), plane, g_qkv, noise, held, sems)
    noise[...] = noise[...] + noise_mine[...]
    live = jnp.sum(counts[...].astype(F32), keepdims=True)
    mean[...] = (total + loss_mine[...]) / (channels * live)
    for copy in copies:
        copy.wait()


def unpack(plane, width, channels=0, counts=None, before=()):
    anywhere = pl.BlockSpec(memory_space=pl.ANY)
    body = unpack_mine_body
    args = (plane,)
    if before:
        body = functools.partial(unpack_theirs_body, channels=channels)
        args += (counts, *before)
    shapes = ((width, 3 * width), (32, width), (1, 1))
    return pl.pallas_call(
        body,
        out_shape=[jax.ShapeDtypeStruct(shape, F32) for shape in shapes],
        in_specs=[anywhere if i == 2 else VMEM for i in range(len(args))],
        out_specs=[anywhere, VMEM, VMEM],
        scratch_shapes=[
            pltpu.VMEM((width, 3 * width // 2), F32), pltpu.SemaphoreType.DMA((12,)),
        ],
        input_output_aliases={2: 0} if before else {},
        compiler_params=pltpu.CompilerParams(vmem_limit_bytes=16 * MIB),
        cost_estimate=pl.CostEstimate(flops=0, bytes_accessed=6 * 10**6, transcendentals=0),
    )(*args)


def unpack_first(mine, theirs, width, channels):
    shapes = ((width, width), (width, width), (channels, width))
    anywhere = pl.BlockSpec(memory_space=pl.ANY)
    return pl.pallas_call(
        unpack_first_body,
        out_shape=[jax.ShapeDtypeStruct(shape, F32) for shape in shapes],
        in_specs=[VMEM] * 8,
        out_specs=[anywhere, anywhere, VMEM],
        scratch_shapes=[
            pltpu.VMEM((width, width), F32), pltpu.VMEM((width, width), F32),
            pltpu.VMEM((96, width), F32), pltpu.SemaphoreType.DMA((8,)),
        ],
        compiler_params=pltpu.CompilerParams(vmem_limit_bytes=16 * MIB),
        cost_estimate=pl.CostEstimate(flops=0, bytes_accessed=8 * 10**6, transcendentals=0),
    )(*mine, *theirs)


def join_body(d_own, rows, from_next, from_prev, d_latent):
    nodes = d_own.shape[2]
    rim = rows.shape[1]
    index = lax.broadcasted_iota(jnp.int32, (nodes, 2 * rim), 0)
    both = jnp.concatenate([rows[0:1, :], rows[1:2, :]], axis=1)
    table = (index == both).astype(F32).T.astype(BF16)
    for m in range(d_own.shape[0]):
        back = jnp.concatenate([from_next[m], from_prev[m]], axis=0)
        d_latent[m] = d_own[m] + mm(back, table, TN)


def on_device(
    latent, send_rows, neighbours, degree, dec_nodes, counts, targets, member_noise,
    w_qkv, w_out, w_noise, w_hid, w_pred,
):
    members, width, nodes = latent.shape
    rim = send_rows.shape[1]
    points = dec_nodes.shape[1]
    channels = targets.shape[0]
    rows = members * nodes
    rims = members * 2 * rim
    degree = degree[None, :]
    size = lax.axis_size(SPACE)
    up = [(i, i + 1) for i in range(size - 1)]
    down = [(i + 1, i) for i in range(size - 1)]

    sent_up, sent_down = call(
        send_body, [((members, rim, width), BF16)] * 2, latent, send_rows,
        apart=(0, 1),
        scratch=[
            pltpu.VMEM(latent.shape, BF16), pltpu.VMEM(send_rows.shape, jnp.int32),
            pltpu.SemaphoreType.DMA((2,)),
        ],
    )
    low = lax.ppermute(sent_up, SPACE, up)
    high = lax.ppermute(sent_down, SPACE, down)
    own, normed, proj, held_qkv = call(
        local_body,
        [
            ((members, nodes, width), BF16), ((rows, width), BF16), ((rows, 3 * width), BF16),
            (w_qkv.shape, BF16),
        ],
        latent, member_noise, w_noise, w_qkv,
        apart=(0, 1, 2, 3),
        scratch=[
            pltpu.VMEM(latent.shape, BF16), pltpu.VMEM(member_noise.shape, F32),
            pltpu.VMEM(w_noise.shape, F32),
            pltpu.VMEM((rows, 3 * width), F32), pltpu.SemaphoreType.DMA((6,)),
        ],
        flops=2 * rows * width * 3 * width,
    )
    normed_all, proj_rim, attended, stored, hidden, slope, forecast, table = call(
        forward_body,
        [
            ((rows + rims, width), BF16), ((rims, 2 * width), BF16), ((rows, width), BF16),
            ((rows, width), BF16), ((members, width, points), BF16),
            ((members, width, points), BF16), ((members, channels, points), BF16),
            ((nodes, points), BF16),
        ],
        own, normed, proj, low, high, member_noise, w_noise, held_qkv, w_out, w_hid, w_pred,
        neighbours, degree, dec_nodes,
        apart=(8, 9),
        scratch=[
            pltpu.VMEM((width, width), BF16), pltpu.VMEM((width, width), BF16),
            pltpu.SemaphoreType.DMA((2,)),
        ],
        flops=3 * 10**9,
    )
    near, *gathered = gather_members(forecast)
    slopes, columns = call(
        crps_near_body, [((members, channels, points), F32), ((1, points), F32)],
        forecast, near, targets,
        flops=10**8,
    )
    planes, levels = ("x", "y"), ("zlo", "zhi")
    spots = lax.axis_size(planes)
    tile, rest_tile = (16, SPLIT), (16, REST)
    chunk, rest_chunk = (16 // spots,) + tile, (16 // spots,) + rest_tile
    ring = [2 * (z % 2) + z // 2 for z in range(4)]

    def shifted(pieces):
        moved = []
        for shift, piece in enumerate(pieces, 1):
            pairs = [(ring[z], ring[(z + shift) % 4]) for z in range(4)]
            moved.append(lax.ppermute(piece, levels, pairs))
        return moved

    def swapped(a):
        return lax.all_to_all(a, planes, 0, 0, tiled=True)

    first_shape = (CHUNKS, 16, TILE * SLOTS_A)
    swap = [(0, 1), (1, 0)]
    normed_theirs = lax.ppermute(normed_all, "core", swap)
    d_updated, d_attended, keep, send, loss = call(
        crps_body,
        [
            ((rows, width), BF16), ((rows, width), BF16), (first_shape, BF16),
            (first_shape, BF16), ((16, TILE), BF16),
        ],
        counts, forecast, *gathered, slopes, columns, hidden, slope, table, stored, attended,
        w_out, w_hid, w_pred,
        smem=(0,),
        scratch=[
            pltpu.VMEM((members, width, points), BF16),
            pltpu.VMEM((members, channels, points), BF16),
            pltpu.VMEM((2,) + first_shape, BF16),
        ],
        flops=6 * 10**9,
    )
    came = lax.ppermute(send, "core", swap)
    tall = (4, 16) + rest_tile
    stacks = call(
        pack_first_body, [((16,) + rest_tile, BF16)] * 4, keep.reshape(tall), came.reshape(tall)
    )
    stacks = [stacks[0]] + shifted(stacks[1:])
    d_proj, d_rim, d_send = call(
        attend_back_body,
        [
            ((2, rows, 3 * width // 2), BF16), ((2, rims, width), BF16),
            ((rows + rims, 3 * width // 2), BF16),
        ],
        proj, proj_rim, neighbours, degree, d_attended,
        scratch=[pltpu.VMEM((nodes + 2 * rim, nodes), F32)],
        flops=2 * 10**9,
    )
    d_theirs = lax.ppermute(d_send, "core", swap)
    d_own, d_low, d_high, g_noise = call(
        norm_back_body,
        [
            ((members, width, nodes), F32), ((members, rim, width), BF16),
            ((members, rim, width), BF16), ((32, width), BF16),
        ],
        own, low, high, member_noise, w_noise, held_qkv, d_proj, d_rim, d_updated,
        flops=2 * 10**9,
    )
    (plane,) = call(
        pack_body,
        [((16, 4) + tile, BF16)],
        normed_all, normed_theirs, d_proj, d_rim, d_theirs, g_noise, loss,
        scratch=[
            pltpu.VMEM((width, 3 * width // 2), BF16), pltpu.VMEM((16, 4) + tile, BF16),
            pltpu.SemaphoreType.DMA((4,)),
        ],
        far=(0,),
        flops=2 * 10**9,
    )
    plane, d_low, d_high = lax.optimization_barrier((plane, d_low, d_high))
    from_next = lax.ppermute(d_low, SPACE, down)
    from_prev = lax.ppermute(d_high, SPACE, up)
    plane = swapped(plane)
    stacks, from_next, from_prev = lax.optimization_barrier((stacks, from_next, from_prev))
    (stack,) = call(sum_stack_body, [((16,) + rest_tile, BF16)], *stacks)
    columns = call(
        sum_plane_body,
        [(chunk, BF16)] * 4,
        plane.reshape((spots, 16 // spots, 4) + tile),
        scratch=[pltpu.VMEM((4,) + chunk, BF16)],
    )
    columns = [columns[0]] + shifted(columns[1:])
    stack = swapped(stack)
    column, stack = call(
        second_sum_body,
        [(chunk, BF16), ((spots,) + rest_chunk, BF16)],
        *columns, stack.reshape((spots,) + rest_chunk),
    )
    columns = [column] + shifted([column] * 3)
    stack = swapped(stack.reshape((16,) + rest_tile))
    (d_latent,) = call(
        join_body, [((members, width, nodes), F32)], d_own, send_rows, from_next, from_prev
    )
    columns, stack, d_latent = lax.optimization_barrier((columns, stack, d_latent))
    (plane,) = call(
        spread_body, [((spots, 16 // spots, 4) + tile, BF16)], *columns,
        far=(0,),
        scratch=[pltpu.VMEM((4,) + chunk, BF16), pltpu.SemaphoreType.DMA((16,))],
    )
    stacks = [stack] + shifted([stack] * 3)
    other_stacks = [lax.ppermute(a, "core", swap) for a in stacks]
    g_hid, g_out, g_pred = unpack_first(stacks, other_stacks, width, channels)
    plane = swapped(plane.reshape((16, 4) + tile))
    plane, g_hid, g_out, g_pred = lax.optimization_barrier((plane, g_hid, g_out, g_pred))
    other_plane = lax.ppermute(plane, "core", swap)
    mine = unpack(plane, width)
    g_qkv, g_noise, mean = unpack(other_plane, width, channels, counts[None, :], mine)
    return mean.reshape(()), d_latent, g_qkv, g_out, g_noise, g_hid, g_pred


def gather_members(forecast):
    swap = [(0, 1), (1, 0)]
    far = lax.ppermute(forecast, "zhi", swap)
    near = lax.ppermute(forecast, "core", swap)
    return near, far, lax.ppermute(far, "core", swap)


def solution(mesh):
    axes = ("x", "zlo", "y", "zhi", "core")
    side = 4 if mesh.shape["space"] == 32 else 1
    mesh = jax.sharding.Mesh(mesh.devices.reshape(side, 2, side, 2, 2), axes)
    member, space = ("zhi", "core"), SPACE
    in_specs = (
        P(member, None, space), P(None, space), P(None, space), P(space),
        P(None, space), P(), P(None, space), P(member, None), P(), P(), P(), P(), P(),
    )
    out_specs = (P(), P(member, None, space), P(), P(), P(), P(), P())
    return jax.shard_map(
        on_device, mesh=mesh, in_specs=in_specs, out_specs=out_specs, check_vma=False
    )
```

```python
import functools

import jax
import jax.numpy as jnp
from jax import lax
from jax.experimental import pallas as pl
from jax.experimental.pallas import tpu as pltpu
from jax.sharding import PartitionSpec as P

HEADS = 6
HEAD = 128
TILE = 128
GROUPS = 16
SPACE = ("x", "zlo", "y")
SPLIT = 896
REST = 1536 - SPLIT
SLOTS_A = 5
SLOTS_B = 7
CHUNKS = 4 * GROUPS
EPS = 1e-5
F32 = jnp.float32
BF16 = jnp.bfloat16
NN = (((1,), (0,)), ((), ()))
NT = (((1,), (1,)), ((), ()))
TN = (((0,), (0,)), ((), ()))
VMEM = pl.BlockSpec(memory_space=pltpu.VMEM)
SMEM = pl.BlockSpec(memory_space=pltpu.SMEM)
APART = pl.BlockSpec(memory_space=pltpu.HBM)
MIB = 1024 * 1024


def mm(a, b, dims=NN):
    return lax.dot_general(a, b, dims, preferred_element_type=F32)


def call(body, out_shape, *args, smem=(), apart=(), far=(), flops=0, scratch=(), vmem=16):
    out_shape = [
        pltpu.HBM(s, d) if i in far else jax.ShapeDtypeStruct(s, d)
        for i, (s, d) in enumerate(out_shape)
    ]
    size = sum(a.size * a.dtype.itemsize for a in args)
    args = [
        pltpu.with_memory_space_constraint(a, pltpu.HBM) if i in apart else a
        for i, a in enumerate(args)
    ]
    return pl.pallas_call(
        body,
        out_shape=out_shape,
        in_specs=[
            SMEM if i in smem else APART if i in apart else VMEM for i in range(len(args))
        ],
        out_specs=[APART if i in far else VMEM for i in range(len(out_shape))],
        scratch_shapes=list(scratch),
        compiler_params=pltpu.CompilerParams(vmem_limit_bytes=vmem * MIB),
        cost_estimate=pl.CostEstimate(flops=flops, bytes_accessed=size, transcendentals=0),
    )(*args)


def gains(noise, w_noise):
    return 1.0 + lax.dot_general(
        noise, w_noise, NN, precision=lax.Precision.HIGHEST, preferred_element_type=F32
    )


def normalise(rows):
    centre = rows - jnp.mean(rows, axis=1, keepdims=True)
    inverse = lax.rsqrt(jnp.mean(centre * centre, axis=1, keepdims=True) + EPS)
    return centre * inverse, inverse


def norm_back(cotangent, gain, hat, inverse):
    d_hat = cotangent * gain
    mean = jnp.mean(d_hat, axis=1, keepdims=True)
    along = jnp.mean(d_hat * hat, axis=1, keepdims=True)
    return inverse * (d_hat - mean - hat * along)


def depth_here():
    return 2 * lax.axis_index("zhi") + lax.axis_index("zlo")


def send_body(latent_far, rows_far, sent_up, sent_down, latent, rows, sems):
    for copy in fetch((latent_far, rows_far), (latent, rows), sems):
        copy.wait()
    nodes = latent.shape[2]
    rim = rows.shape[1]
    both = jnp.concatenate([rows[0:1, :], rows[1:2, :]], axis=1)
    table = lax.broadcasted_iota(jnp.int32, (nodes, 2 * rim), 0) == both
    table = table.astype(F32).T.astype(BF16)
    for m in range(latent.shape[0]):
        picked = mm(table, latent[m], NT).astype(BF16)
        sent_up[m] = picked[:rim]
        sent_down[m] = picked[rim:]


def fetch(sources, targets, sems):
    copies = [
        pltpu.make_async_copy(a, b, sems.at[i]) for i, (a, b) in enumerate(zip(sources, targets))
    ]
    for copy in copies:
        copy.start()
    return copies


def local_body(
    latent_far, noise_far, w_noise_far, w_qkv, own, normed, proj, held,
    latent, noise, w_noise, total, sems,
):
    thirds = [slice(r, r + 256) for r in range(0, held.shape[0], 256)]
    copies = fetch(
        [latent_far, noise_far, w_noise_far] + [w_qkv.at[r] for r in thirds],
        [latent, noise, w_noise] + [held.at[r] for r in thirds],
        sems,
    )
    for copy in copies[:3]:
        copy.wait()
    copies = copies[3:]
    gain = gains(noise[...], w_noise[...])
    members, _, nodes = latent.shape
    for m in range(members):
        rows = latent[m].astype(F32).T
        own[m] = rows.astype(BF16)
        hat, _ = normalise(rows)
        normed[m * nodes : (m + 1) * nodes] = (hat * gain[m : m + 1]).astype(BF16)
    for i, r in enumerate(thirds):
        copies[i].wait()
        part = mm(normed[:, r], held[r])
        if i == 0:
            total[...] = part
        elif i < len(thirds) - 1:
            total[...] = total[...] + part
        else:
            proj[...] = (total[...] + part).astype(BF16)


def slot_mask(nbr, degree, rows):
    slots, nodes = nbr.shape
    index = lax.broadcasted_iota(jnp.int32, (rows, nodes), 0)
    total = jnp.zeros((rows, nodes), F32)
    for j in range(slots):
        live = (index == nbr[j : j + 1, :]) & (degree[...] > j)
        total = total + live.astype(F32)
    return total / degree[...].astype(F32)


def point_table(dec_nodes, nodes):
    points = dec_nodes.shape[1]
    index = lax.broadcasted_iota(jnp.int32, (nodes, points), 0)
    total = jnp.zeros((nodes, points), F32)
    for j in range(dec_nodes.shape[0]):
        total = total + (index == dec_nodes[j : j + 1, :]).astype(F32)
    return total.astype(BF16)


def extend(own, low, high):
    return jnp.concatenate([low, own, high], axis=0)


def forward_body(
    own, normed, proj, low, high, noise, w_noise, w_qkv, w_out, w_hid, w_pred, nbr, degree,
    dec_nodes,
    normed_all, proj_rim, attended, stored, hidden, slope, forecast, table,
    held_out, held_hid, sems,
):
    copies = fetch((w_out, w_hid), (held_out, held_hid), sems)
    members, nodes, width = own.shape
    rim = low.shape[1]
    gain = gains(noise[...], w_noise[...])
    for m in range(members):
        rows = jnp.concatenate([low[m], high[m]], axis=0).astype(F32)
        hat, _ = normalise(rows)
        at = members * nodes + 2 * rim * m
        normed_all[at : at + 2 * rim] = (hat * gain[m : m + 1]).astype(BF16)
    normed_all[: members * nodes] = normed[...]
    proj_rim[...] = mm(normed_all[members * nodes :], w_qkv[:, width:]).astype(BF16)
    mask = slot_mask(nbr, degree, nodes + 2 * rim)
    for m in range(members):
        here = slice(m * nodes, (m + 1) * nodes)
        lo = slice(2 * rim * m, 2 * rim * m + rim)
        hi = slice(2 * rim * m + rim, 2 * rim * (m + 1))
        for h in range(HEADS):
            at = [slice(k * width + h * HEAD, k * width + (h + 1) * HEAD) for k in range(3)]
            rim_at = [slice(a.start - width, a.stop - width) for a in at]
            key = extend(proj[here, at[1]], proj_rim[lo, rim_at[1]], proj_rim[hi, rim_at[1]])
            value = extend(proj[here, at[2]], proj_rim[lo, rim_at[2]], proj_rim[hi, rim_at[2]])
            score = mm(key, proj[here, at[0]], NT) * HEAD**-0.5
            weight = (jax.nn.sigmoid(score) * mask).astype(BF16)
            attended[here, at[0]] = mm(weight, value, TN).astype(BF16)
    copies[0].wait()
    branch = mm(attended[...], held_out[...])
    for m in range(members):
        here = slice(m * nodes, (m + 1) * nodes)
        stored[here] = (own[m].astype(F32) + branch[here]).astype(BF16)
    table[...] = point_table(dec_nodes, nodes)
    copies[1].wait()
    mixed = mm(stored[...], held_hid[...]).astype(BF16)
    block = 256
    for m in range(members):
        part = mixed[m * nodes : (m + 1) * nodes]
        for g in range(0, dec_nodes.shape[1], block):
            pre = mm(part, table[:, g : g + block], TN) * (1.0 / 3.0)
            sig = 0.5 * jnp.tanh(0.5 * pre) + 0.5
            hid = pre * sig
            hidden[m, :, g : g + block] = hid.astype(BF16)
            slope[m, :, g : g + block] = (sig + hid * (1.0 - sig)).astype(BF16)
            forecast[m, :, g : g + block] = mm(
                w_pred[...], hidden[m, :, g : g + block]
            ).astype(BF16)


def smooth(v):
    square = v * v + 0.25
    inverse = lax.rsqrt(square)
    return square * inverse - 0.5, v * inverse


def crps_near_body(mine, near, targets, slopes, columns):
    members, channels, points = mine.shape
    total = 8
    block = 256
    scale = 0.5 / (total * (total - 1))
    for g in range(0, points, block):
        at = slice(g, g + block)
        own = [mine[m, :, at].astype(F32) for m in range(members)]
        aim = targets[:, at]
        close = jnp.zeros((channels, block), F32)
        apart = jnp.zeros((channels, block), F32)
        first = []
        grads = [jnp.zeros((channels, block), F32)] * members
        for m in range(members):
            value, grad = smooth(own[m] - aim)
            close = close + value
            first.append(grad)
        for a in range(members):
            for b in range(a + 1, members):
                value, grad = smooth(own[a] - own[b])
                apart = apart + 2.0 * value
                grads[a] = grads[a] + grad
                grads[b] = grads[b] - grad
        for k in range(members):
            theirs = near[k, :, at].astype(F32)
            for m in range(members):
                value, grad = smooth(own[m] - theirs)
                apart = apart + value
                grads[m] = grads[m] + grad
        for m in range(members):
            slopes[m, :, at] = first[m] * (1.0 / total) - grads[m] * (2.0 * scale)
        columns[:, at] = jnp.sum(
            close * (1.0 / total) - apart * scale, axis=0, keepdims=True
        )


def crps_body(
    counts, mine, *rest
):
    (*others, slopes, columns, hidden, slope, table, stored, attended, w_out, w_hid, w_pred,
     d_updated, d_attended, keep, send, loss, d_pre, d_cast, halves) = rest
    live_count = counts[lax.axis_index(SPACE)]
    core = lax.axis_index("core")
    members, channels, points = mine.shape
    total = 8
    block = 256
    scale = 0.5 / (total * (total - 1))
    losses = []
    for g in range(0, points, block):
        at = slice(g, g + block)
        live = lax.broadcasted_iota(jnp.int32, (1, block), 1) + g < live_count
        live = live.astype(F32)
        own = [mine[m, :, at].astype(F32) for m in range(members)]
        apart = jnp.zeros((channels, block), F32)
        grads = [jnp.zeros((channels, block), F32)] * members
        for other in others:
            for k in range(members):
                theirs = other[k, :, at].astype(F32)
                for m in range(members):
                    value, grad = smooth(own[m] - theirs)
                    apart = apart + value
                    grads[m] = grads[m] + grad
        for m in range(members):
            grad = slopes[m, :, at] - grads[m] * (2.0 * scale)
            d_cast[m, :, at] = (grad * live).astype(BF16)
        column = columns[:, at] - jnp.sum(apart, axis=0, keepdims=True) * scale
        losses.append(column * live)
    for i in range(16):
        at = i % 2
        piece = losses[i // 2 % 4][:, TILE * at : TILE * (at + 1)]
        loss[i : i + 1] = piece.astype(BF16) if i < 8 else jnp.zeros((1, TILE), BF16)
    back = w_pred[...].astype(F32).T.astype(BF16)
    grad = jnp.zeros((channels, hidden.shape[1]), F32)
    for m in range(members):
        grad = grad + mm(d_cast[m], hidden[m], NT)
        for g in range(0, points, block):
            at = slice(g, g + block)
            d_hid = mm(back, d_cast[m, :, at])
            d_pre[m, :, at] = (d_hid * slope[m, :, at].astype(F32)).astype(BF16)
    g_pred = jnp.zeros((96 - channels, grad.shape[1]), F32)
    g_pred = jnp.concatenate([grad, g_pred], axis=0).astype(BF16)
    pooled = [
        (mm(table[...], d_pre[m], NT) * (1.0 / 3.0)).astype(BF16) for m in range(members)
    ]
    pooled = jnp.concatenate(pooled, axis=0)
    g_hid = mm(stored[...], pooled, TN).astype(BF16)
    d_updated[...] = mm(pooled, w_hid[...], NT).astype(BF16)
    g_out = mm(attended[...], d_updated[...], TN).astype(BF16)
    d_attended[...] = mm(d_updated[...], w_out[...], NT).astype(BF16)
    half = g_hid.shape[1] // 2
    for c in range(2):
        for k in range(GROUPS):
            for slot in range(SLOTS_A * 4):
                chunk, lane = 4 * k + slot // SLOTS_A, TILE * (slot % SLOTS_A)
                grad, row, column = tile_of_first(k, slot, (g_hid, g_out, g_pred))
                if grad is None:
                    piece = jnp.zeros((16, TILE), BF16)
                else:
                    column = c * half + TILE * column
                    piece = grad[16 * row : 16 * row + 16, column : column + TILE]
                halves[c, chunk, :, lane : lane + TILE] = piece
    keep[...] = halves[core]
    send[...] = halves[1 - core]


def tile_of_first(k, slot, grads):
    if slot < 18:
        part = slot % 9
        return grads[slot // 9], 3 * k + part // 3, part % 3
    tile = k + GROUPS * (slot - 18)
    if tile < 18:
        return grads[2], tile // 3, tile % 3
    return None, 0, 0


def attend_back_body(
    proj, proj_rim, nbr, degree, d_attended,
    d_proj, d_rim, send, mask,
):
    nodes = nbr.shape[1]
    members = proj.shape[0] // nodes
    width = HEADS * HEAD
    rim = proj_rim.shape[0] // (2 * members)
    per_half = HEADS // 2
    part = width // 2
    mask[...] = slot_mask(nbr, degree, nodes + 2 * rim)
    for m in range(members):
        here = slice(m * nodes, (m + 1) * nodes)
        lo = slice(2 * rim * m, 2 * rim * m + rim)
        hi = slice(2 * rim * m + rim, 2 * rim * (m + 1))
        for h in range(HEADS):
            at = [slice(k * width + h * HEAD, k * width + (h + 1) * HEAD) for k in range(3)]
            rim_at = [slice(a.start - width, a.stop - width) for a in at]
            query = proj[here, at[0]]
            key = extend(proj[here, at[1]], proj_rim[lo, rim_at[1]], proj_rim[hi, rim_at[1]])
            value = extend(proj[here, at[2]], proj_rim[lo, rim_at[2]], proj_rim[hi, rim_at[2]])
            out = d_attended[here, at[0]]
            sig = jax.nn.sigmoid(mm(key, query, NT) * HEAD**-0.5)
            weight = sig * mask[...]
            d_value = mm(weight.astype(BF16), out).astype(BF16)
            d_weight = mm(value, out, NT)
            d_score = (d_weight * weight * (1.0 - sig) * HEAD**-0.5).astype(BF16)
            d_key = mm(d_score, query).astype(BF16)
            c, j = h // per_half, h % per_half
            spot = [slice(k * part + j * HEAD, k * part + (j + 1) * HEAD) for k in range(3)]
            d_proj[c, here, spot[0]] = mm(d_score, key, TN).astype(BF16)
            for k, d in ((1, d_key), (2, d_value)):
                d_rim[c, lo, spot[k - 1]] = d[:rim]
                d_proj[c, here, spot[k]] = d[rim : rim + nodes]
                d_rim[c, hi, spot[k - 1]] = d[rim + nodes :]
    rows = members * nodes
    theirs = 1 - lax.axis_index("core")
    send[:rows] = d_proj[theirs]
    send[rows:, : 2 * part] = d_rim[theirs]
    send[rows:, 2 * part :] = jnp.zeros((2 * rim * members, part), BF16)


def norm_back_body(
    own, low, high, noise, w_noise, w_qkv, d_proj, d_rim, d_updated,
    d_own, d_low, d_high, g_noise,
):
    members, nodes, width = own.shape
    rim = low.shape[1]
    part = width // 2
    noises = noise[...]
    gain = gains(noises, w_noise[...])
    d_normed = jnp.zeros((members * nodes, width), F32)
    d_normed_rim = jnp.zeros((members * 2 * rim, width), F32)
    for c in range(2):
        for k in range(3):
            column = k * width + c * part
            weight = w_qkv[:, column : column + part]
            d_normed = d_normed + mm(d_proj[c, :, k * part : (k + 1) * part], weight, NT)
            if k:
                d_normed_rim = d_normed_rim + mm(
                    d_rim[c, :, (k - 1) * part : k * part], weight, NT
                )
    d_noise = jnp.zeros(g_noise.shape, F32)
    noise_columns = jnp.concatenate([noises] * (8 // members), axis=0).T
    for m in range(members):
        here = slice(m * nodes, (m + 1) * nodes)
        rims = slice(2 * rim * m, 2 * rim * (m + 1))
        hat, inverse = normalise(own[m].astype(F32))
        d_gain = jnp.sum(d_normed[here] * hat, axis=0, keepdims=True)
        rows = norm_back(d_normed[here], gain[m : m + 1], hat, inverse)
        d_own[m] = (rows + d_updated[here].astype(F32)).T
        hat, inverse = normalise(jnp.concatenate([low[m], high[m]], axis=0).astype(F32))
        d_gain = d_gain + jnp.sum(d_normed_rim[rims] * hat, axis=0, keepdims=True)
        rows = norm_back(d_normed_rim[rims], gain[m : m + 1], hat, inverse)
        d_low[m] = rows[:rim].astype(BF16)
        d_high[m] = rows[rim:].astype(BF16)
        d_noise = d_noise + noise_columns[:, m : m + 1] * d_gain
    g_noise[...] = d_noise.astype(BF16)


def pack_first_body(keep, came, *stacks):
    depth = depth_here()
    for shift, target in enumerate(stacks):
        level = lax.rem(depth + shift, 4)
        target[...] = (keep[level].astype(F32) + came[level].astype(F32)).astype(BF16)


def pack_body(
    normed, normed_theirs, d_proj, d_rim, d_theirs, g_noise, loss, plane_far, g_half, plane, sems
):
    copies = []
    core = lax.axis_index("core")
    rows = d_proj.shape[1]
    wide = 2 * d_proj.shape[2] // 3
    width = normed.shape[1]
    mine = d_proj[core]
    rim = d_rim[core]
    for r in range(0, width, 192):
        at = slice(r, r + 192)
        total = mm(normed[:rows, at], mine, TN) + mm(normed_theirs[:rows, at], d_theirs[:rows], TN)
        g_half[at, : wide // 2] = total[:, : wide // 2].astype(BF16)
        edge = mm(normed[rows:, at], rim, TN)
        edge = edge + mm(normed_theirs[rows:, at], d_theirs[rows:, :wide], TN)
        g_half[at, wide // 2 :] = (total[:, wide // 2 :] + edge).astype(BF16)
        level = r // 192
        for k in range(4 * level, 4 * level + 4):
            for slot in range(4 * SLOTS_B):
                spot, lane = 4 * (k % 4) + slot // SLOTS_B, TILE * (slot % SLOTS_B)
                if slot < 27:
                    row, column = 48 * k + 16 * (slot // 9), TILE * (slot % 9)
                    piece = g_half[row : row + 16, column : column + TILE]
                elif k < 12:
                    row, column = 16 * (k // 6), TILE * (k % 6)
                    piece = g_noise[row : row + 16, column : column + TILE]
                elif k == 12:
                    piece = loss[...]
                else:
                    piece = jnp.zeros((16, TILE), BF16)
                plane[spot, level, :, lane : lane + TILE] = piece
        copies += fetch([plane.at[:, level]], [plane_far.at[:, level]], sems.at[level : level + 1])
    for copy in copies:
        copy.wait()


def sum_plane_body(came, *rest):
    depth = depth_here()
    targets, column = rest[:4], rest[4]
    for j in range(came.shape[1]):
        total = came[0, j].astype(F32)
        for i in range(1, came.shape[0]):
            total = total + came[i, j].astype(F32)
        column[:, j] = total.astype(BF16)
    for shift, target in enumerate(targets):
        target[...] = column[lax.rem(depth + shift, 4)]


def sum_stack_body(one, two, three, four, total):
    part = one[...].astype(F32) + two[...].astype(F32)
    total[...] = (part + three[...].astype(F32) + four[...].astype(F32)).astype(BF16)


def second_sum_body(one, two, three, four, came, column, spread):
    total = one[...].astype(F32) + two[...].astype(F32)
    total = total + three[...].astype(F32) + four[...].astype(F32)
    column[...] = total.astype(BF16)
    total = came[0].astype(F32)
    for i in range(1, came.shape[0]):
        total = total + came[i].astype(F32)
    total = total.astype(BF16)
    for i in range(came.shape[0]):
        spread[i] = total


def spread_body(one, two, three, four, spread, column, sems):
    depth = depth_here()
    for shift, piece in enumerate((one, two, three, four)):
        column[lax.rem(depth + (4 - shift), 4)] = piece[...]
    parts, spots = spread.shape[1], spread.shape[0]
    sources = [column.at[:, j] for j in range(parts) for i in range(spots)]
    targets = [spread.at[i, j] for j in range(parts) for i in range(spots)]
    for copy in fetch(sources, targets, sems):
        copy.wait()


def unpack_first_body(*refs):
    mine, theirs, (g_hid, g_out, g_pred, hid, out, pred, sems) = refs[:4], refs[4:8], refs[8:]
    depth, core = depth_here(), lax.axis_index("core")
    width = hid.shape[1]
    copies = []
    for step in range(4):
        level = lax.rem(depth + 4 - step, 4)
        for side, which in ((mine, core), (theirs, 1 - core)):
            start = which * (width // 2)

            def column(j):
                return pl.ds(pl.multiple_of(start + TILE * j, TILE), TILE)

            for group in range(4):
                k = 4 * level + group
                for slot in range(4 * SLOTS_A):
                    spot, lane = 4 * group + slot // SLOTS_A, TILE * (slot % SLOTS_A)
                    piece = side[step][spot, :, lane : lane + TILE].astype(F32)
                    if slot < 18:
                        row = 192 * step + 48 * group + 16 * (slot % 9 // 3)
                        (hid, out)[slot // 9][row : row + 16, column(slot % 3)] = piece
                    else:
                        index = k + GROUPS * (slot - 18)

                        @pl.when(index < 18)
                        def _():
                            row = pl.multiple_of(16 * lax.div(index, 3), 16)
                            pred[pl.ds(row, 16), column(lax.rem(index, 3))] = piece

        base = slice(192 * step, 192 * step + 192)
        rows = pl.ds(pl.multiple_of(192 * level, 16), 192)
        copies += fetch(
            (hid.at[base], out.at[base]), (g_hid.at[rows], g_out.at[rows]),
            sems.at[2 * step : 2 * step + 2],
        )
    g_pred[...] = pred[: g_pred.shape[0]]
    for copy in copies:
        copy.wait()


def unpack_plane(core, plane, g_qkv, noise, held, sems):
    wide = held.shape[1] // 3
    copies = []
    total = jnp.zeros((16, TILE), F32)
    for level in range(4):
        for group in range(4):
            k = 4 * level + group
            for slot in range(4 * SLOTS_B):
                spot, lane = 4 * group + slot // SLOTS_B, TILE * (slot % SLOTS_B)
                if slot == 27 and k > 12:
                    continue
                piece = plane[spot, level, :, lane : lane + TILE].astype(F32)
                if slot < 27:
                    row, column = 48 * k + 16 * (slot // 9), TILE * (slot % 9)
                    held[row : row + 16, column : column + TILE] = piece
                elif k < 12:
                    row, column = 16 * (k // 6), TILE * (k % 6)
                    noise[row : row + 16, column : column + TILE] = piece
                else:
                    total = piece
            if group % 2 == 0:
                continue
            base = slice(48 * k - 48, 48 * k + 48)
            for section in range(3):
                start = pl.multiple_of(2 * wide * section + wide * core, TILE)
                copies += fetch(
                    [held.at[base, wide * section : wide * (section + 1)]],
                    [g_qkv.at[base, pl.ds(start, wide)]],
                    sems.at[len(copies) : len(copies) + 1],
                )
    return copies, jnp.sum(total, keepdims=True)


def unpack_mine_body(plane, g_qkv, noise, loss, held, sems):
    copies, total = unpack_plane(lax.axis_index("core"), plane, g_qkv, noise, held, sems)
    loss[...] = total
    for copy in copies:
        copy.wait()


def unpack_theirs_body(
    plane, counts, _qkv, noise_mine, loss_mine, g_qkv, noise, mean, held, sems, channels
):
    copies, total = unpack_plane(1 - lax.axis_index("core"), plane, g_qkv, noise, held, sems)
    noise[...] = noise[...] + noise_mine[...]
    live = jnp.sum(counts[...].astype(F32), keepdims=True)
    mean[...] = (total + loss_mine[...]) / (channels * live)
    for copy in copies:
        copy.wait()


def unpack(plane, width, channels=0, counts=None, before=()):
    anywhere = pl.BlockSpec(memory_space=pl.ANY)
    body = unpack_mine_body
    args = (plane,)
    if before:
        body = functools.partial(unpack_theirs_body, channels=channels)
        args += (counts, *before)
    shapes = ((width, 3 * width), (32, width), (1, 1))
    return pl.pallas_call(
        body,
        out_shape=[jax.ShapeDtypeStruct(shape, F32) for shape in shapes],
        in_specs=[anywhere if i == 2 else VMEM for i in range(len(args))],
        out_specs=[anywhere, VMEM, VMEM],
        scratch_shapes=[
            pltpu.VMEM((width, 3 * width // 2), F32), pltpu.SemaphoreType.DMA((24,)),
        ],
        input_output_aliases={2: 0} if before else {},
        compiler_params=pltpu.CompilerParams(vmem_limit_bytes=16 * MIB),
        cost_estimate=pl.CostEstimate(flops=0, bytes_accessed=6 * 10**6, transcendentals=0),
    )(*args)


def unpack_first(mine, theirs, width, channels):
    shapes = ((width, width), (width, width), (channels, width))
    anywhere = pl.BlockSpec(memory_space=pl.ANY)
    return pl.pallas_call(
        unpack_first_body,
        out_shape=[jax.ShapeDtypeStruct(shape, F32) for shape in shapes],
        in_specs=[VMEM] * 8,
        out_specs=[anywhere, anywhere, VMEM],
        scratch_shapes=[
            pltpu.VMEM((width, width), F32), pltpu.VMEM((width, width), F32),
            pltpu.VMEM((96, width), F32), pltpu.SemaphoreType.DMA((8,)),
        ],
        compiler_params=pltpu.CompilerParams(vmem_limit_bytes=16 * MIB),
        cost_estimate=pl.CostEstimate(flops=0, bytes_accessed=8 * 10**6, transcendentals=0),
    )(*mine, *theirs)


def join_body(d_own, rows, from_next, from_prev, d_latent):
    nodes = d_own.shape[2]
    rim = rows.shape[1]
    index = lax.broadcasted_iota(jnp.int32, (nodes, 2 * rim), 0)
    both = jnp.concatenate([rows[0:1, :], rows[1:2, :]], axis=1)
    table = (index == both).astype(F32).T.astype(BF16)
    for m in range(d_own.shape[0]):
        back = jnp.concatenate([from_next[m], from_prev[m]], axis=0)
        d_latent[m] = d_own[m] + mm(back, table, TN)


def on_device(
    latent, send_rows, neighbours, degree, dec_nodes, counts, targets, member_noise,
    w_qkv, w_out, w_noise, w_hid, w_pred,
):
    members, width, nodes = latent.shape
    rim = send_rows.shape[1]
    points = dec_nodes.shape[1]
    channels = targets.shape[0]
    rows = members * nodes
    rims = members * 2 * rim
    degree = degree[None, :]
    size = lax.axis_size(SPACE)
    up = [(i, i + 1) for i in range(size - 1)]
    down = [(i + 1, i) for i in range(size - 1)]

    sent_up, sent_down = call(
        send_body, [((members, rim, width), BF16)] * 2, latent, send_rows,
        apart=(0, 1),
        scratch=[
            pltpu.VMEM(latent.shape, BF16), pltpu.VMEM(send_rows.shape, jnp.int32),
            pltpu.SemaphoreType.DMA((2,)),
        ],
    )
    low = lax.ppermute(sent_up, SPACE, up)
    high = lax.ppermute(sent_down, SPACE, down)
    own, normed, proj, held_qkv = call(
        local_body,
        [
            ((members, nodes, width), BF16), ((rows, width), BF16), ((rows, 3 * width), BF16),
            (w_qkv.shape, BF16),
        ],
        latent, member_noise, w_noise, w_qkv,
        apart=(0, 1, 2, 3),
        scratch=[
            pltpu.VMEM(latent.shape, BF16), pltpu.VMEM(member_noise.shape, F32),
            pltpu.VMEM(w_noise.shape, F32),
            pltpu.VMEM((rows, 3 * width), F32), pltpu.SemaphoreType.DMA((6,)),
        ],
        flops=2 * rows * width * 3 * width,
    )
    normed_all, proj_rim, attended, stored, hidden, slope, forecast, table = call(
        forward_body,
        [
            ((rows + rims, width), BF16), ((rims, 2 * width), BF16), ((rows, width), BF16),
            ((rows, width), BF16), ((members, width, points), BF16),
            ((members, width, points), BF16), ((members, channels, points), BF16),
            ((nodes, points), BF16),
        ],
        own, normed, proj, low, high, member_noise, w_noise, held_qkv, w_out, w_hid, w_pred,
        neighbours, degree, dec_nodes,
        apart=(8, 9),
        scratch=[
            pltpu.VMEM((width, width), BF16), pltpu.VMEM((width, width), BF16),
            pltpu.SemaphoreType.DMA((2,)),
        ],
        flops=3 * 10**9,
    )
    near, *gathered = gather_members(forecast)
    slopes, columns = call(
        crps_near_body, [((members, channels, points), F32), ((1, points), F32)],
        forecast, near, targets,
        flops=10**8,
    )
    planes, levels = ("x", "y"), ("zlo", "zhi")
    spots = lax.axis_size(planes)
    tile, rest_tile = (16, SPLIT), (16, REST)
    chunk, rest_chunk = (16 // spots,) + tile, (16 // spots,) + rest_tile
    ring = [2 * (z % 2) + z // 2 for z in range(4)]

    def shifted(pieces):
        moved = []
        for shift, piece in enumerate(pieces, 1):
            pairs = [(ring[z], ring[(z + shift) % 4]) for z in range(4)]
            moved.append(lax.ppermute(piece, levels, pairs))
        return moved

    def swapped(a):
        return lax.all_to_all(a, planes, 0, 0, tiled=True)

    first_shape = (CHUNKS, 16, TILE * SLOTS_A)
    swap = [(0, 1), (1, 0)]
    normed_theirs = lax.ppermute(normed_all, "core", swap)
    d_updated, d_attended, keep, send, loss = call(
        crps_body,
        [
            ((rows, width), BF16), ((rows, width), BF16), (first_shape, BF16),
            (first_shape, BF16), ((16, TILE), BF16),
        ],
        counts, forecast, *gathered, slopes, columns, hidden, slope, table, stored, attended,
        w_out, w_hid, w_pred,
        smem=(0,),
        scratch=[
            pltpu.VMEM((members, width, points), BF16),
            pltpu.VMEM((members, channels, points), BF16),
            pltpu.VMEM((2,) + first_shape, BF16),
        ],
        flops=6 * 10**9,
    )
    came = lax.ppermute(send, "core", swap)
    tall = (4, 16) + rest_tile
    stacks = call(
        pack_first_body, [((16,) + rest_tile, BF16)] * 4, keep.reshape(tall), came.reshape(tall)
    )
    stacks = [stacks[0]] + shifted(stacks[1:])
    d_proj, d_rim, d_send = call(
        attend_back_body,
        [
            ((2, rows, 3 * width // 2), BF16), ((2, rims, width), BF16),
            ((rows + rims, 3 * width // 2), BF16),
        ],
        proj, proj_rim, neighbours, degree, d_attended,
        scratch=[pltpu.VMEM((nodes + 2 * rim, nodes), F32)],
        flops=2 * 10**9,
    )
    d_theirs = lax.ppermute(d_send, "core", swap)
    d_own, d_low, d_high, g_noise = call(
        norm_back_body,
        [
            ((members, width, nodes), F32), ((members, rim, width), BF16),
            ((members, rim, width), BF16), ((32, width), BF16),
        ],
        own, low, high, member_noise, w_noise, held_qkv, d_proj, d_rim, d_updated,
        flops=2 * 10**9,
    )
    (plane,) = call(
        pack_body,
        [((16, 4) + tile, BF16)],
        normed_all, normed_theirs, d_proj, d_rim, d_theirs, g_noise, loss,
        scratch=[
            pltpu.VMEM((width, 3 * width // 2), BF16), pltpu.VMEM((16, 4) + tile, BF16),
            pltpu.SemaphoreType.DMA((4,)),
        ],
        far=(0,),
        flops=2 * 10**9,
    )
    plane, d_low, d_high = lax.optimization_barrier((plane, d_low, d_high))
    from_next = lax.ppermute(d_low, SPACE, down)
    from_prev = lax.ppermute(d_high, SPACE, up)
    plane = swapped(plane)
    stacks, from_next, from_prev = lax.optimization_barrier((stacks, from_next, from_prev))
    (stack,) = call(sum_stack_body, [((16,) + rest_tile, BF16)], *stacks)
    columns = call(
        sum_plane_body,
        [(chunk, BF16)] * 4,
        plane.reshape((spots, 16 // spots, 4) + tile),
        scratch=[pltpu.VMEM((4,) + chunk, BF16)],
    )
    columns = [columns[0]] + shifted(columns[1:])
    stack = swapped(stack)
    column, stack = call(
        second_sum_body,
        [(chunk, BF16), ((spots,) + rest_chunk, BF16)],
        *columns, stack.reshape((spots,) + rest_chunk),
    )
    columns = [column] + shifted([column] * 3)
    stack = swapped(stack.reshape((16,) + rest_tile))
    (d_latent,) = call(
        join_body, [((members, width, nodes), F32)], d_own, send_rows, from_next, from_prev
    )
    columns, stack, d_latent = lax.optimization_barrier((columns, stack, d_latent))
    (plane,) = call(
        spread_body, [((spots, 16 // spots, 4) + tile, BF16)], *columns,
        far=(0,),
        scratch=[pltpu.VMEM((4,) + chunk, BF16), pltpu.SemaphoreType.DMA((16,))],
    )
    stacks = [stack] + shifted([stack] * 3)
    other_stacks = [lax.ppermute(a, "core", swap) for a in stacks]
    g_hid, g_out, g_pred = unpack_first(stacks, other_stacks, width, channels)
    plane = swapped(plane.reshape((16, 4) + tile))
    plane, g_hid, g_out, g_pred = lax.optimization_barrier((plane, g_hid, g_out, g_pred))
    other_plane = lax.ppermute(plane, "core", swap)
    mine = unpack(plane, width)
    g_qkv, g_noise, mean = unpack(other_plane, width, channels, counts[None, :], mine)
    return mean.reshape(()), d_latent, g_qkv, g_out, g_noise, g_hid, g_pred


def gather_members(forecast):
    swap = [(0, 1), (1, 0)]
    far = lax.ppermute(forecast, "zhi", swap)
    near = lax.ppermute(forecast, "core", swap)
    return near, far, lax.ppermute(far, "core", swap)


def solution(mesh):
    axes = ("x", "zlo", "y", "zhi", "core")
    side = 4 if mesh.shape["space"] == 32 else 1
    mesh = jax.sharding.Mesh(mesh.devices.reshape(side, 2, side, 2, 2), axes)
    member, space = ("zhi", "core"), SPACE
    in_specs = (
        P(member, None, space), P(None, space), P(None, space), P(space),
        P(None, space), P(), P(None, space), P(member, None), P(), P(), P(), P(), P(),
    )
    out_specs = (P(), P(member, None, space), P(), P(), P(), P(), P())
    return jax.shard_map(
        on_device, mesh=mesh, in_specs=in_specs, out_specs=out_specs, check_vma=False
    )
```
